128 devices in a mesh: dp: 8 (over z_lo, y), ctx: 16 (over x, z_hi, core).
Axes of the slice: x: 4, y: 4, z: 4 (z_hi: 2, z_lo: 2; z = z_hi * 2 + z_lo), core: 2. Of those that a mesh axis runs over, the one named last changes fastest.
Arguments:
- tokens: bfloat16 [32, 4096, 768], P('dp', 'ctx'), may hold values from -6 to 6
- w_qkv: bfloat16 [768, 2304], replicated, may hold values from -0.21650635 to 0.21650635
- w_out: bfloat16 [768, 768], replicated, may hold values from -0.21875 to 0.21875
- ln_gain: float32 [768], replicated, may hold values from 0.25 to 1.75
- cache: bfloat16 [16384, 768], P(('dp', 'ctx')), may hold values from -0.5051815 to 0.5051815
- positive: int32 [32], replicated, may hold values from 0 to 16383
- lengths: int32 [32], P('dp'), may hold values from 2048 to 4096, as said below
Outputs:
- hidden: bfloat16 [32, 4096, 768], P('dp', 'ctx')
- loss: float32 [], replicated
- grad_out: float32 [768, 768], P(('dp', 'ctx'))
The draws below stay inside these ranges and needn't reach their ends.
Inputs may be any that keep to these rules, and one draw needn't show every extreme that they name: `lengths`: some document has exactly 4096 valid tokens in every draw.
All inputs are finite; a program needn't handle non-finite values.
Results may differ from the reference program's by a relative error of at most 0.003.
The reference program's roundings to bfloat16 on the way (of `qkv`, `weights`, `mixed` and `d_summed`) count: a program that leaves them out, or rounds other values in their place, can miss the bound.
Values may be sent and summed in bfloat16 or wider, within the bound.
No kernel may reach another device: no remote copies, remote signals or barrier semaphores. Data moves between devices by JAX's collectives and lax.ppermute only.
A program may use at most 128 MiB of HBM per device.

```python
import math
import jax
import jax.numpy as jnp
from jax import lax

D = 768
H = 12
HD = 64
TB = 256
WIN = 256
LEN = 4096
DOCS = 32
CACHE = 16384
N_CTX = 16


def draw_tokens(key, part):
    key = jax.random.fold_in(key, 31)
    values = jax.random.normal(jax.random.fold_in(key, 5), (DOCS, LEN, D), jnp.float32)
    return jnp.clip(values, -6.0, 6.0).astype(jnp.bfloat16)


def draw_w_qkv(key, part):
    key = jax.random.fold_in(key, 37)
    scale = D ** (-0.5)
    values = jax.random.normal(jax.random.fold_in(key, 1), (D, 3 * D), jnp.float32) * scale
    return jnp.clip(values, -6.0 * scale, 6.0 * scale).astype(jnp.bfloat16)


def draw_cache(key, part):
    key = jax.random.fold_in(key, 41)
    scale = D ** (-0.5)
    values = jnp.clip(jax.random.normal(jax.random.fold_in(key, 1), (CACHE, D), jnp.float32), -6.0, 6.0) * scale
    return jnp.clip(values, -14.0 * scale, 14.0 * scale).astype(jnp.bfloat16)


def draw_lengths(key, part):
    key = jax.random.fold_in(key, 11)
    drawn = jax.random.randint(key, (DOCS,), LEN // 2, LEN + 1)
    chosen = jax.random.randint(jax.random.fold_in(key, 2), (), 0, DOCS)
    return drawn.at[chosen].set(LEN).astype(jnp.int32)


def with_ends(entries, own_key, least, top_value):
    longest = entries.shape.index(max(entries.shape))
    spots = []
    for shift in (0, 1):
        where = [jax.random.randint(jax.random.fold_in(own_key, axis), (), 0, length) for axis, length in enumerate(entries.shape)]
        where[longest] = (where[longest] + shift) % entries.shape[longest]
        spots.append(tuple(where))
    return entries.at[spots[0]].set(least).at[spots[1]].set(top_value)


def gaussian(own_key, dims, width, bound, kind=jnp.bfloat16):
    return jnp.clip(width * jax.random.normal(own_key, dims, jnp.float32), -bound, bound).astype(kind)


def setup_inputs(seed: int = 0) -> dict:
    key_list = jax.random.split(jax.random.key(seed), 8)
    tokens = draw_tokens(jax.random.fold_in(key_list[7], 71), 0)
    w_qkv = draw_w_qkv(jax.random.fold_in(key_list[7], 71), 0)
    w_out = gaussian(key_list[2], (D, D), D ** -0.5, 0.21875)
    ln_gain = jnp.clip(1.0 + 0.15 * jax.random.normal(key_list[3], (D,), jnp.float32), 0.25, 1.75)
    cache = draw_cache(jax.random.fold_in(key_list[7], 71), 0)
    positive = with_ends(jax.random.randint(key_list[5], (DOCS,), 0, CACHE), jax.random.fold_in(key_list[5], 1), 0, CACHE - 1).astype(jnp.int32)
    lengths = draw_lengths(jax.random.fold_in(key_list[7], 71), 0)
    return dict(tokens=tokens, w_qkv=w_qkv, w_out=w_out, ln_gain=ln_gain, cache=cache, positive=positive, lengths=lengths)


TAU = 0.02

def alibi_slopes(heads):
    largest = 2 ** int(math.floor(math.log2(heads)))
    listed = [2.0 ** (-8.0 * (h + 1) / largest) for h in range(largest)]
    listed = listed + [2.0 ** (-4.0 * (2 * m + 1) / largest) for m in range(heads - largest)]
    return jnp.array(listed, dtype=jnp.float32)

def attend_block(q_rows, k_rows, v_rows, start, length):
    tb = q_rows.shape[0]
    ext = k_rows.shape[0]
    q = q_rows.reshape(tb, H, HD).astype(jnp.float32)
    k = k_rows.reshape(ext, H, HD).astype(jnp.float32)
    v = v_rows.reshape(ext, H, HD).astype(jnp.float32)
    scores = jnp.einsum('qhd,khd->hqk', q, k)
    qpos = start + jnp.arange(tb, dtype=jnp.int32)
    kpos = start - WIN + jnp.arange(ext, dtype=jnp.int32)
    dist = jnp.abs(qpos[:, None] - kpos[None, :])
    slopes = alibi_slopes(H)
    inside = (kpos >= 0) & (kpos < length)
    seen = (dist <= WIN)[None] & (inside[None, None, :] | (dist == 0)[None])
    scores = scores * 0.125 - slopes[:, None, None] * dist[None].astype(jnp.float32)
    scores = jnp.where(seen, scores, -1e+30)
    top = lax.optimization_barrier(jnp.max(scores, axis=2, keepdims=True))
    expo = jnp.exp(scores - top)
    weights = (expo / lax.optimization_barrier(jnp.sum(expo, axis=2, keepdims=True))).astype(jnp.bfloat16)
    out = jnp.einsum('hqk,khd->qhd', weights.astype(jnp.float32), v)
    return out.astype(jnp.bfloat16).reshape(tb, H * HD)

def forward_doc(tokens_doc, length, w_qkv):
    qkv = jnp.dot(tokens_doc, w_qkv, preferred_element_type=jnp.float32).astype(jnp.bfloat16)
    query = qkv[:, :D]
    keys = jnp.pad(qkv[:, D:2 * D], ((WIN, WIN), (0, 0)))
    values = jnp.pad(qkv[:, 2 * D:], ((WIN, WIN), (0, 0)))

    def one_block(index):
        start = (index * TB).astype(jnp.int32)
        q_rows = lax.dynamic_slice_in_dim(query, start, TB, 0)
        k_rows = lax.dynamic_slice_in_dim(keys, start, TB + 2 * WIN, 0)
        v_rows = lax.dynamic_slice_in_dim(values, start, TB + 2 * WIN, 0)
        return attend_block(q_rows, k_rows, v_rows, start, length)
    mixed = lax.map(one_block, jnp.arange(N_CTX, dtype=jnp.int32)).reshape(LEN, D)
    return mixed

def layer_norm_parts(tokens_doc, mixed, w_out):
    summed = tokens_doc.astype(jnp.float32) + jnp.dot(mixed, w_out, preferred_element_type=jnp.float32)
    mean = lax.optimization_barrier(jnp.mean(summed, axis=1, keepdims=True))
    centred = summed - mean
    rstd = lax.rsqrt(lax.optimization_barrier(jnp.mean(centred * centred, axis=1, keepdims=True)) + 1e-05)
    return (centred * rstd, rstd)

def reference(tokens, w_qkv, w_out, ln_gain, cache, positive, lengths):

    def fwd(item):
        tokens_doc, length = item
        mixed = forward_doc(tokens_doc, length, w_qkv)
        normed, rstd = layer_norm_parts(tokens_doc, mixed, w_out)
        hidden_f = normed * ln_gain
        keep = jnp.arange(LEN, dtype=jnp.int32) < length
        pooled = lax.optimization_barrier(jnp.sum(jnp.where(keep[:, None], hidden_f, 0.0), axis=0)) / length.astype(jnp.float32)
        return (mixed, hidden_f.astype(jnp.bfloat16), pooled)
    mixed_all, hidden, pooled = lax.map(fwd, (tokens, lengths))
    hi = lax.Precision.HIGHEST
    rinv = lax.rsqrt(lax.optimization_barrier(jnp.sum(pooled * pooled, axis=1, keepdims=True)) + 1e-06)
    emb = pooled * rinv
    cache_f = cache.astype(jnp.float32)
    cache_score = jnp.dot(emb, cache_f.T, precision=hi) / TAU
    eye = jnp.eye(DOCS, dtype=bool)
    batch_score = jnp.where(eye, -1e+30, jnp.dot(emb, emb.T, precision=hi) / TAU)
    lse = jax.nn.logsumexp(jnp.concatenate([cache_score, batch_score], axis=1), axis=1)
    hit = positive[:, None] == jnp.arange(CACHE, dtype=jnp.int32)[None, :]
    pos_score = lax.optimization_barrier(jnp.sum(jnp.where(hit, cache_score, 0.0), axis=1))
    loss = jnp.mean(lse - pos_score)
    g_cache = (jnp.exp(cache_score - lse[:, None]) - hit.astype(jnp.float32)) / DOCS
    g_batch = jnp.exp(batch_score - lse[:, None]) / DOCS
    d_emb = (jnp.dot(g_cache, cache_f, precision=hi) + jnp.dot(g_batch + g_batch.T, emb, precision=hi)) / TAU
    d_pooled = (d_emb - emb * lax.optimization_barrier(jnp.sum(emb * d_emb, axis=1, keepdims=True))) * rinv

    def bwd(total, item):
        tokens_doc, mixed, length, d_doc = item
        normed, rstd = layer_norm_parts(tokens_doc, mixed, w_out)
        keep = jnp.arange(LEN, dtype=jnp.int32) < length
        d_hidden = jnp.where(keep[:, None], d_doc[None, :] / length.astype(jnp.float32), 0.0)
        dy = d_hidden * ln_gain
        d_summed = rstd * (dy - lax.optimization_barrier(jnp.mean(dy, axis=1, keepdims=True)) - normed * lax.optimization_barrier(jnp.mean(dy * normed, axis=1, keepdims=True)))
        d_summed = d_summed.astype(jnp.bfloat16)
        return (total + jnp.dot(mixed.T, d_summed, preferred_element_type=jnp.float32), None)
    grad_out, _ = lax.scan(bwd, jnp.zeros((D, D), jnp.float32), (tokens, mixed_all, lengths, d_pooled))
    return (hidden, loss, grad_out)
```

```python
import functools
import math

import jax
import jax.numpy as jnp
from jax import lax
from jax.experimental import pallas as pl
from jax.experimental.pallas import tpu as pltpu
from jax.sharding import PartitionSpec as P

H = 12
WIN = 256
TAU = 0.02
FAR = 1e32
NT = (((1,), (1,)), ((), ()))
HIGHEST = lax.Precision.HIGHEST
VMEM = pl.BlockSpec(memory_space=pltpu.VMEM)
SMEM = pl.BlockSpec(memory_space=pltpu.SMEM)

CTX_STEPS = (1, 4, 12, 2)
DP_STEPS = (4, 1, 3)


def swap(value, axis, bits):
    return lax.ppermute(value, axis, [(i, i ^ bits) for i in range(lax.axis_size(axis))])


def call(kernel, out_shape, in_specs, out_specs, limit=100, flops=0, moved=0, **keywords):
    return pl.pallas_call(
        kernel,
        out_shape=out_shape,
        in_specs=in_specs,
        out_specs=out_specs,
        compiler_params=pltpu.CompilerParams(vmem_limit_bytes=limit * 2**20 // 2),
        cost_estimate=pl.CostEstimate(flops=flops, bytes_accessed=moved, transcendentals=0),
        **keywords,
    )


def f32(*shape):
    return jax.ShapeDtypeStruct(shape, jnp.float32)


def bf16(*shape):
    return jax.ShapeDtypeStruct(shape, jnp.bfloat16)


def slopes_of(heads):
    largest = 2 ** int(math.floor(math.log2(heads)))
    listed = [2.0 ** (-8.0 * (h + 1) / largest) for h in range(largest)]
    return listed + [2.0 ** (-4.0 * (2 * m + 1) / largest) for m in range(heads - largest)]


def thirds(value):
    high = value.astype(jnp.bfloat16)
    rest = value - high.astype(jnp.float32)
    middle = rest.astype(jnp.bfloat16)
    low = (rest - middle.astype(jnp.float32)).astype(jnp.bfloat16)
    parts = [p.astype(jnp.float32) for p in (high, middle, low)]
    return jnp.concatenate(parts, axis=0).astype(jnp.bfloat16)


def attend_kernel(
    meta, tok, left, right, qkv, w_k, w_v, w_out, gain, hidden, mixed, normed, rstd_out, pool, keys, values, dist
):
    tb, width = tok.shape
    ext = tb + 2 * WIN
    start, length = meta[0], meta[1]
    for source, low in ((left, 0), (right, WIN + tb)):
        rows = source[...]
        keys[pl.ds(low, WIN), :] = jnp.dot(rows, w_k[...], preferred_element_type=jnp.float32).astype(jnp.bfloat16)
        values[pl.ds(low, WIN), :] = jnp.dot(rows, w_v[...], preferred_element_type=jnp.float32).astype(jnp.bfloat16)
    keys[pl.ds(WIN, tb), :] = qkv[:, width : 2 * width]
    values[pl.ds(WIN, tb), :] = qkv[:, 2 * width :]
    i = lax.broadcasted_iota(jnp.int32, (tb, ext), 0)
    j = lax.broadcasted_iota(jnp.int32, (tb, ext), 1) - WIN
    away = jnp.abs(i - j)
    kpos = start + j
    seen = (away <= WIN) & (((kpos >= 0) & (kpos < length)) | (away == 0))
    dist[...] = jnp.where(seen, away.astype(jnp.float32), FAR)
    block = 128
    span = block + 2 * WIN
    half = lax.broadcasted_iota(jnp.int32, (block, 128), 1) < 64
    slopes = slopes_of(H)
    for pair in range(H // 2):
        cols = pl.ds(pair * 128, 128)
        for row in range(0, tb, block):
            query = qkv[pl.ds(row, block), cols] * jnp.bfloat16(0.125)
            key = keys[pl.ds(row, span), cols]
            value = values[pl.ds(row, span), cols]
            halves = []
            for part in range(2):
                own = jnp.where(half if part == 0 else ~half, query, jnp.bfloat16(0))
                score = lax.dot_general(own, key, NT, preferred_element_type=jnp.float32)
                score = score - slopes[2 * pair + part] * dist[pl.ds(row, block), pl.ds(row, span)]
                expo = jnp.exp(score - jnp.max(score, axis=1, keepdims=True))
                weights = (expo * (1.0 / jnp.sum(expo, axis=1, keepdims=True))).astype(jnp.bfloat16)
                halves.append(jnp.dot(weights, value, preferred_element_type=jnp.float32))
            mixed[pl.ds(row, block), cols] = jnp.where(half, halves[0], halves[1]).astype(jnp.bfloat16)
    summed = tok[...].astype(jnp.float32) + jnp.dot(mixed[...], w_out[...], preferred_element_type=jnp.float32)
    centred = summed - jnp.mean(summed, axis=1, keepdims=True)
    rstd = lax.rsqrt(jnp.mean(centred * centred, axis=1, keepdims=True) + 1e-05)
    unit = centred * rstd
    hidden_f = unit * gain[...]
    hidden[...] = hidden_f.astype(jnp.bfloat16)
    normed[...] = unit.astype(jnp.bfloat16)
    rstd_out[...] = jnp.broadcast_to(rstd, rstd_out.shape)
    keep = start + lax.broadcasted_iota(jnp.int32, (tb, 1), 0) < length
    pool[...] = jnp.sum(jnp.where(keep, hidden_f, 0.0), axis=0, keepdims=True)


def attend(meta, tok, left, right, qkv, w_qkv, w_out, gain):
    tb, width = tok.shape
    ext = tb + 2 * WIN
    full = lambda a: pl.BlockSpec(a.shape, lambda i: (0,) * len(a.shape))
    third = lambda k: pl.BlockSpec((width, width), lambda i: (0, k))
    out_shape = (bf16(tb, width), bf16(tb, width), bf16(tb, width), f32(tb, 128), f32(1, width))
    return call(
        attend_kernel,
        out_shape,
        [SMEM, full(tok), full(left), full(right), full(qkv), third(1), third(2), full(w_out), full(gain)],
        tuple(full(a) for a in out_shape),
        flops=4 * 2 * tb * ext * width,
        moved=8 * 2**20,
        grid=(1,),
        scratch_shapes=[
            pltpu.VMEM((ext, width), jnp.bfloat16),
            pltpu.VMEM((ext, width), jnp.bfloat16),
            pltpu.VMEM((tb, ext), jnp.float32),
        ],
        name="attend",
    )(meta, tok, left, right, qkv, w_qkv, w_qkv, w_out, gain)


def score_kernel(meta, sums, count, cache, emb_out, rinv_out, spread, state):
    docs, width = emb_out.shape
    pooled = sums[...] / count[:, 0:1]
    rinv = lax.rsqrt(jnp.sum(pooled * pooled, axis=1, keepdims=True) + 1e-06)
    emb = pooled * rinv
    emb_out[...] = emb[0:docs]
    rinv_out[...] = jnp.broadcast_to(rinv[0:docs], rinv_out.shape)
    twice = jnp.concatenate([emb[0:docs], emb[0:docs]], axis=0)
    all_docs = spread.shape[0]
    owner = lax.broadcasted_iota(jnp.int32, (all_docs, width), 0) // docs
    spread[...] = jnp.where(owner == meta[0], jnp.concatenate([twice] * (all_docs // (2 * docs)), axis=0), 0.0)
    rows = sums.shape[0]
    table = cache[...]
    products = lax.dot_general(thirds(emb), table, NT, preferred_element_type=jnp.float32)
    score = (products[0:rows] + products[rows : 2 * rows] + products[2 * rows :]) / TAU
    top = jnp.max(score, axis=1, keepdims=True)
    expo = jnp.exp(score - top)
    total = jnp.sum(expo, axis=1, keepdims=True)
    products = jnp.dot(thirds(expo), table, preferred_element_type=jnp.float32)
    mix = products[0:rows] + products[rows : 2 * rows] + products[2 * rows :]
    state[:, pl.ds(0, width)] = mix[0:docs]
    state[:, pl.ds(width, 128)] = jnp.broadcast_to(total[0:docs], (docs, 128))
    state[:, pl.ds(width + 128, 128)] = jnp.broadcast_to(top[0:docs], (docs, 128))


def score(meta, sums, count, cache, docs, all_docs):
    width = sums.shape[1]
    return call(
        score_kernel,
        (f32(docs, width), f32(docs, 128), f32(all_docs, width), f32(docs, width + 256)),
        [SMEM, VMEM, VMEM, VMEM],
        (VMEM, VMEM, VMEM, VMEM),
        moved=2 * 2**20,
        name="score",
    )(meta, sums, count, cache)


def merge(first, second, width):
    place = width + 128
    top_1, top_2 = first[:, place : place + 1], second[:, place : place + 1]
    top = jnp.maximum(top_1, top_2)
    joined = first * jnp.exp(top_1 - top) + second * jnp.exp(top_2 - top)
    column = lax.broadcasted_iota(jnp.int32, first.shape, 1)
    return jnp.where(column < place, joined, top)


def batch_scores(emb, everyone, first):
    docs, all_docs = emb.shape[0], everyone.shape[0]
    product = lax.dot_general(emb, everyone, NT, precision=HIGHEST, preferred_element_type=jnp.float32) / TAU
    row = lax.broadcasted_iota(jnp.int32, (docs, all_docs), 0)
    column = lax.broadcasted_iota(jnp.int32, (docs, all_docs), 1)
    return product, column == row + first


def lse_of(state, product, same, width):
    scores = jnp.where(same, -1e30, product)
    batch_top = jnp.max(scores, axis=1, keepdims=True)
    batch_total = jnp.sum(jnp.exp(scores - batch_top), axis=1, keepdims=True)
    total, top = state[:, width : width + 1], state[:, width + 128 : width + 129]
    peak = jnp.maximum(top, batch_top)
    return peak + jnp.log(total * jnp.exp(top - peak) + batch_total * jnp.exp(batch_top - peak))


def lse_kernel(meta, state, emb, everyone, target, lse_out):
    docs, width = emb.shape
    all_docs = everyone.shape[0]
    own = emb[...]
    product, same = batch_scores(own, everyone[...], meta[0] * docs)
    lse = lse_of(state[...], product, same, width)
    loss = lse - jnp.sum(own * target[docs : 2 * docs], axis=1, keepdims=True) / TAU
    pair = jnp.where(lax.broadcasted_iota(jnp.int32, (docs, 128), 1) < 64, lse, loss)
    twice = jnp.concatenate([pair, pair], axis=0)
    owner = lax.broadcasted_iota(jnp.int32, (all_docs, 128), 0) // docs
    lse_out[...] = jnp.where(owner == meta[0], jnp.concatenate([twice] * (all_docs // (2 * docs)), axis=0), 0.0)


def grad_kernel(
    meta, state, emb, rinv, everyone, target, lses, count, gain, normed, rstd, turned, keep_out, send_out, d_summed
):
    docs, width = emb.shape
    all_docs = everyone.shape[0]
    own, others = emb[...], everyone[...]
    product, same = batch_scores(own, others, meta[0] * docs)
    now = state[...]
    lse = lse_of(now, product, same, width)
    wide = (all_docs, all_docs)
    diagonal = lax.broadcasted_iota(jnp.int32, wide, 0) == lax.broadcasted_iota(jnp.int32, wide, 1)
    lse_row = jnp.sum(jnp.where(diagonal, lses[:, 0:1], 0.0), axis=0, keepdims=True)
    g_batch = jnp.where(same, 0.0, jnp.exp(product - lse) + jnp.exp(product - lse_row)) / all_docs
    from_cache = (now[:, 0:width] * jnp.exp(now[:, width + 128 : width + 129] - lse) - target[docs : 2 * docs]) / all_docs
    from_batch = jnp.dot(g_batch, others, precision=HIGHEST, preferred_element_type=jnp.float32)
    d_emb = (from_cache + from_batch) / TAU
    d_pooled = (d_emb - own * jnp.sum(own * d_emb, axis=1, keepdims=True)) * rinv[:, 0:1]
    dy = d_pooled / count[0:docs, 0:1] * gain[...]
    level = dy - jnp.mean(dy, axis=1, keepdims=True)
    tb = normed.shape[0] // docs
    for doc in range(docs):
        rows = pl.ds(doc * tb, tb)
        unit = normed[rows, :].astype(jnp.float32)
        along = jnp.mean(unit * dy[doc : doc + 1], axis=1, keepdims=True)
        keep = meta[1] + lax.broadcasted_iota(jnp.int32, (tb, 1), 0) < meta[2 + doc]
        scale = jnp.where(keep, rstd[rows, 0:1], 0.0)
        d_summed[rows, :] = (scale * (level[doc : doc + 1] - unit * along)).astype(jnp.bfloat16)
    half = width // 2
    keep_out[...] = jnp.dot(turned[0:half], d_summed[...], preferred_element_type=jnp.float32)
    send_out[...] = jnp.dot(turned[half:], d_summed[...], preferred_element_type=jnp.float32)


def sum_kernel(kind, count, *refs):
    terms, outs = refs[:count], refs[count:]
    total = terms[0][...].astype(jnp.float32)
    for term in terms[1:]:
        total = total + term[...].astype(jnp.float32)
    rows = outs[0].shape[0]
    for index, out in enumerate(outs):
        out[...] = total[index * rows : (index + 1) * rows].astype(out.dtype)


def sum_and_split(terms, kind, ways):
    rows, width = terms[0].shape
    piece = (rows // ways, width)
    shapes = (f32(*piece),) + (jax.ShapeDtypeStruct(piece, kind),) * (ways - 1)
    return call(
        functools.partial(sum_kernel, kind, len(terms)), shapes, [VMEM] * len(terms), (VMEM,) * ways, name="sum_split"
    )(*terms)


def shards(tokens, w_qkv, w_out, ln_gain, cache, positive, lengths):
    docs, tb, width = tokens.shape
    n_ctx, n_dp = lax.axis_size("ctx"), lax.axis_size("dp")
    dp, ctx = lax.axis_index("dp"), lax.axis_index("ctx")
    start = ctx * tb
    all_docs = n_dp * docs
    halos = []
    for doc in range(docs):
        left = lax.ppermute(tokens[doc], "ctx", [(i, i + 1) for i in range(n_ctx - 1)])
        right = lax.ppermute(tokens[doc], "ctx", [(i + 1, i) for i in range(n_ctx - 1)])
        halos.append((left, right))
    table, order = cache, [0]
    for bits in DP_STEPS:
        table = jnp.concatenate([table, swap(table, "dp", bits)], axis=0)
        order = order + [o ^ bits for o in order]
    cache_rows = cache.shape[0]
    places = jnp.array(order, jnp.int32)
    row_ids = (((dp ^ places) * n_ctx + ctx) * cache_rows)[:, None] + jnp.arange(cache_rows, dtype=jnp.int32)[None, :]
    mine = lax.dynamic_slice_in_dim(positive, dp * docs, docs, 0)
    hit = (mine[:, None] == row_ids.reshape(1, -1)).astype(jnp.bfloat16)
    target = jnp.dot(hit, table, preferred_element_type=jnp.float32)

    gain = ln_gain.reshape(1, width)
    qkv = jnp.dot(tokens.reshape(docs * tb, width), w_qkv, preferred_element_type=jnp.float32).astype(jnp.bfloat16)
    done = []
    for doc in range(docs):
        meta = jnp.stack([start, lengths[doc]]).astype(jnp.int32)
        done.append(attend(meta, tokens[doc], *halos[doc], qkv[doc * tb : (doc + 1) * tb], w_qkv, w_out, gain))
    hidden, mixed, normed, rstd, pool = (jnp.stack(parts) for parts in zip(*done))

    place = jnp.arange(width, dtype=jnp.int32)
    core = (ctx & 1) ^ (place // (width // 2))
    y = ((dp & 3) + place // (width // 8) % 4) & 3
    x = ((ctx >> 2) + place // (width // 32) % 4) & 3
    z = ((ctx & 2) + (dp >> 2) + place // (width // 128) % 4) & 3
    block = ((z & 1) * 4 + y) * n_ctx + x * 4 + (z >> 1) * 2 + core
    row_of = block * (width // 128) + place % (width // 128)
    chosen = (row_of[:, None] == place[None, :]).astype(jnp.bfloat16)
    turned = lax.dot_general(
        chosen, mixed.reshape(docs * tb, width), NT, preferred_element_type=jnp.float32
    ).astype(jnp.bfloat16)

    count = jnp.broadcast_to(jnp.tile(lengths.astype(jnp.float32), 2)[:, None], (2 * docs, 128))
    sums = jnp.concatenate([pool.reshape(docs, width), target], axis=0)
    for bits in CTX_STEPS:
        sums = sums + swap(sums, "ctx", bits)
    me = dp.astype(jnp.int32).reshape(1)
    emb, rinv, everyone, state = score(me, sums, count, table, docs, all_docs)
    for bits in DP_STEPS:
        everyone = everyone + swap(everyone, "dp", bits)
    for bits in CTX_STEPS:
        other = swap(state, "ctx", bits)
        lower = (ctx & (bits & -bits)) == 0
        state = merge(jnp.where(lower, state, other), jnp.where(lower, other, state), width)
    lses = call(lse_kernel, f32(all_docs, 128), [SMEM] + [VMEM] * 4, VMEM, name="lse")(me, state, emb, everyone, sums)
    for bits in DP_STEPS:
        lses = lses + swap(lses, "dp", bits)
    loss = jnp.mean(lses[:, 64])
    meta = jnp.concatenate([me, start.astype(jnp.int32).reshape(1), lengths])
    half = width // 2
    keep, send = call(
        grad_kernel,
        (f32(half, width), f32(half, width)),
        [SMEM] + [VMEM] * 11,
        (VMEM, VMEM),
        flops=2 * docs * tb * width * width,
        moved=8 * 2**20,
        scratch_shapes=[pltpu.VMEM((docs * tb, width), jnp.bfloat16)],
        name="grad",
    )(
        meta, state, emb, rinv, everyone, sums, lses, count, gain,
        normed.reshape(docs * tb, width), rstd.reshape(docs * tb, 128), turned,
    )
    keep, *sends = sum_and_split([keep, swap(send, "ctx", 1)], jnp.bfloat16, 4)
    along_y = lambda k: [(d, (d & 4) | ((d + k) & 3)) for d in range(n_dp)]
    got = [lax.ppermute(piece, "dp", along_y(k + 1)) for k, piece in enumerate(sends)]
    keep, *sends = sum_and_split([keep] + got, jnp.float32, 4)
    along_x = lambda k: [(c, (c + 4 * k) % n_ctx) for c in range(n_ctx)]
    got = [lax.ppermute(piece, "ctx", along_x(k + 1)) for k, piece in enumerate(sends)]
    keep, *sends = sum_and_split([keep] + got, jnp.float32, 4)

    def along_z(k):
        pairs = []
        for d in range(n_dp):
            for c in range(n_ctx):
                to = ((c & 2) + (d >> 2) + k) & 3
                pairs.append((d * n_ctx + c, ((to & 1) * 4 + (d & 3)) * n_ctx + (c & ~2) + (to & 2)))
        return pairs

    got = [lax.ppermute(piece, ("dp", "ctx"), along_z(k + 1)) for k, piece in enumerate(sends)]
    grad_out = keep + got[0] + got[1] + got[2]
    return (hidden, loss, grad_out)


def solution(mesh):
    placed = (P("dp", "ctx", None), P(), P(), P(), P(("dp", "ctx"), None), P(), P("dp"))
    return jax.shard_map(
        shards,
        mesh=mesh,
        in_specs=placed,
        out_specs=(P("dp", "ctx", None), P(), P(("dp", "ctx"), None)),
        check_vma=False,
    )
```

```python
import functools
import math

import jax
import jax.numpy as jnp
from jax import lax
from jax.experimental import pallas as pl
from jax.experimental.pallas import tpu as pltpu
from jax.sharding import PartitionSpec as P

H = 12
WIN = 256
TAU = 0.02
FAR = 1e32
CHUNK = 2
NT = (((1,), (1,)), ((), ()))
TN = (((0,), (0,)), ((), ()))
HIGHEST = lax.Precision.HIGHEST
VMEM = pl.BlockSpec(memory_space=pltpu.VMEM)
SMEM = pl.BlockSpec(memory_space=pltpu.SMEM)
ANY = pl.BlockSpec(memory_space=pl.ANY)


def swap(value, axis, bits):
    return lax.ppermute(value, axis, [(i, i ^ bits) for i in range(lax.axis_size(axis))])


def from_x(value, k):
    size = lax.axis_size("ctx")
    return lax.ppermute(value, "ctx", [((c + 4 * k) % size, c) for c in range(size)])


def from_y(value, k):
    return lax.ppermute(value, "dp", [((d & 4) | ((d + k) & 3), d) for d in range(lax.axis_size("dp"))])


def from_z(value, k):
    n_dp, n_ctx = lax.axis_size("dp"), lax.axis_size("ctx")
    pairs = []
    for d in range(n_dp):
        for c in range(n_ctx):
            z = ((c & 2) + (d >> 2) + k) & 3
            pairs.append((((z & 1) * 4 + (d & 3)) * n_ctx + (c & ~2) + (z & 2), d * n_ctx + c))
    return lax.ppermute(value, ("dp", "ctx"), pairs)


def around(value, fetch):
    return [value] + [fetch(value, k) for k in (1, 2, 3)]


def call(kernel, out_shape, in_specs, out_specs, limit=24, flops=0, moved=0, **keywords):
    return pl.pallas_call(
        kernel,
        out_shape=out_shape,
        in_specs=in_specs,
        out_specs=out_specs,
        compiler_params=pltpu.CompilerParams(vmem_limit_bytes=limit * 2**20),
        cost_estimate=pl.CostEstimate(flops=flops, bytes_accessed=moved, transcendentals=0),
        **keywords,
    )


def f32(*shape):
    return jax.ShapeDtypeStruct(shape, jnp.float32)


def bf16(*shape):
    return jax.ShapeDtypeStruct(shape, jnp.bfloat16)


def slopes_of(heads):
    largest = 2 ** int(math.floor(math.log2(heads)))
    listed = [2.0 ** (-8.0 * (h + 1) / largest) for h in range(largest)]
    return listed + [2.0 ** (-4.0 * (2 * m + 1) / largest) for m in range(heads - largest)]


def thirds(value):
    high = value.astype(jnp.bfloat16)
    rest = value - high.astype(jnp.float32)
    middle = rest.astype(jnp.bfloat16)
    low = (rest - middle.astype(jnp.float32)).astype(jnp.bfloat16)
    parts = [p.astype(jnp.float32) for p in (high, middle, low)]
    return jnp.concatenate(parts, axis=0).astype(jnp.bfloat16)


def folded(products):
    rows = products.shape[0] // 3
    return products[0:rows] + products[rows : 2 * rows] + products[2 * rows :]


def attend_kernel(
    first, me, lengths, tok, left, right, qk, v_turned, w_k, w_v_turned, w_out, gain, *refs
):
    hidden, mixed, normed, rstd_out, pool, keys, values, dist = refs[-8:]
    tb, width = tok.shape[1:]
    ext = tb + 2 * WIN
    start, length = me[1] * tb, lengths[first + pl.program_id(0)]
    rows = jnp.concatenate([left[0], right[0]], axis=0)
    new = jnp.dot(rows, w_k[...], preferred_element_type=jnp.float32).astype(jnp.bfloat16)
    keys[0:WIN] = new[0:WIN]
    keys[WIN : WIN + tb] = qk[0, :, width:]
    keys[WIN + tb :] = new[WIN:]
    new = lax.dot_general(w_v_turned[...], rows, NT, preferred_element_type=jnp.float32).astype(jnp.bfloat16)
    values[:, 0:WIN] = new[:, 0:WIN]
    values[:, WIN : WIN + tb] = v_turned[...]
    values[:, WIN + tb :] = new[:, WIN:]
    j = lax.broadcasted_iota(jnp.int32, (ext, tb), 0) - WIN
    away = jnp.abs(lax.broadcasted_iota(jnp.int32, (ext, tb), 1) - j)
    kpos = start + j
    seen = (away <= WIN) & (((kpos >= 0) & (kpos < length)) | (away == 0))
    dist[...] = jnp.where(seen, away.astype(jnp.float32), FAR)
    half = lax.broadcasted_iota(jnp.int32, (tb, 128), 1) < 64
    slopes = slopes_of(H)
    lanes = 128
    span = lanes + 2 * WIN
    for pair in range(H // 2):
        cols = pl.ds(pair * 128, 128)
        query = qk[0, :, cols] * jnp.bfloat16(0.125)
        zero = jnp.bfloat16(0)
        both = jnp.concatenate([jnp.where(half, query, zero), jnp.where(half, zero, query)], axis=0)
        scores = lax.dot_general(keys[:, cols], both, NT, preferred_element_type=jnp.float32)
        for part in range(2):
            columns = []
            for low in range(0, tb, lanes):
                score = scores[low : low + span, part * tb + low : part * tb + low + lanes]
                score = score - slopes[2 * pair + part] * dist[pl.ds(low, span), pl.ds(low, lanes)]
                expo = jnp.exp(score - jnp.max(score, axis=0, keepdims=True))
                weights = (expo * (1.0 / jnp.sum(expo, axis=0, keepdims=True))).astype(jnp.bfloat16)
                above, below = low, ext - span - low
                pieces = [weights]
                if above:
                    pieces = [jnp.zeros((above, lanes), jnp.bfloat16)] + pieces
                if below:
                    pieces = pieces + [jnp.zeros((below, lanes), jnp.bfloat16)]
                columns.append(jnp.concatenate(pieces, axis=0))
            weights = jnp.concatenate(columns, axis=1)
            head = pl.ds(pair * 128 + part * 64, 64)
            mixed[head, :] = jnp.dot(values[head, :], weights, preferred_element_type=jnp.float32).astype(jnp.bfloat16)
    summed = tok[0].astype(jnp.float32) + lax.dot_general(mixed[...], w_out[...], TN, preferred_element_type=jnp.float32)
    centred = summed - jnp.mean(summed, axis=1, keepdims=True)
    rstd = lax.rsqrt(jnp.mean(centred * centred, axis=1, keepdims=True) + 1e-05)
    unit = centred * rstd
    hidden_f = unit * gain[...]
    hidden[0] = hidden_f.astype(jnp.bfloat16)
    normed[0] = unit.astype(jnp.bfloat16)
    rstd_out[0] = jnp.broadcast_to(rstd, rstd_out.shape[1:])
    keep = start + lax.broadcasted_iota(jnp.int32, (tb, 1), 0) < length
    pool[0] = jnp.sum(jnp.where(keep, hidden_f, 0.0), axis=0, keepdims=True)


def attend(first, before, me, lengths, tokens, left, right, qk, v_turned, w_qkv, w_v_turned, w_out, gain):
    docs, tb, width = tokens.shape
    ext = tb + 2 * WIN
    here = lambda *s: pl.BlockSpec((1,) + s, lambda i: (first + i, 0, 0))
    chunk = lambda *s: pl.BlockSpec((1,) + s, lambda i: (i, 0, 0))
    column = pl.BlockSpec((width, tb), lambda i: (0, first + i))
    fixed = lambda s, at=(0, 0): pl.BlockSpec(s, lambda i: at, pipeline_mode=pl.Buffered(1))
    out_shape = (bf16(docs, tb, width), bf16(width, docs * tb), bf16(docs, tb, width), f32(docs, tb, 128), f32(docs, 1, width))
    in_specs = [
        SMEM, SMEM, here(tb, width), chunk(WIN, width), chunk(WIN, width), here(tb, 2 * width), column,
        fixed((width, width), (0, 1)), fixed((width, width)), fixed((width, width)), fixed((1, width)),
    ]
    operands = [me, lengths, tokens, left, right, qk, v_turned, w_qkv, w_v_turned, w_out, gain]
    aliases = {}
    if before is not None:
        aliases = {len(operands) + k: k for k in range(len(out_shape))}
        operands = operands + list(before)
        in_specs = in_specs + [ANY] * len(out_shape)
    return call(
        functools.partial(attend_kernel, first),
        out_shape,
        in_specs,
        (here(tb, width), column, here(tb, width), here(tb, 128), here(1, width)),
        limit=32,
        flops=CHUNK * 5 * 2 * tb * ext * width,
        moved=8 * 2**20,
        grid=(CHUNK,),
        scratch_shapes=[
            pltpu.VMEM((ext, width), jnp.bfloat16),
            pltpu.VMEM((width, ext), jnp.bfloat16),
            pltpu.VMEM((ext, tb), jnp.float32),
        ],
        input_output_aliases=aliases,
        name="attend",
    )(*operands)


def row_ids(me, k, rows, shape, dim):
    place = lax.broadcasted_iota(jnp.int32, shape, dim)
    y, z_lo = (me[0] + k) & 3, me[0] >> 2
    other = (place >= rows).astype(jnp.int32)
    owner = (z_lo + other - 2 * z_lo * other) * 4 + y
    return (owner * 16 + me[1]) * rows + place - other * rows


def target_kernel(docs, me, positive, *refs):
    pieces, out = refs[:4], refs[4]
    total = jnp.zeros(out.shape, jnp.float32)
    for k, piece in enumerate(pieces):
        rows = piece.shape[0]
        ids = row_ids(me, k, rows // 2, (8, rows), 1)
        doc = lax.broadcasted_iota(jnp.int32, (8, rows), 0)
        wanted = jnp.full((8, rows), -1, jnp.int32)
        for d in range(docs):
            wanted = jnp.where(doc == d, positive[me[0] * docs + d], wanted)
        hit = (ids == wanted).astype(jnp.float32).astype(jnp.bfloat16)
        total = total + jnp.dot(hit, piece[...], preferred_element_type=jnp.float32)[0:docs]
    out[...] = total


def norm_kernel(lengths, mine, other, emb_out, rinv_out, target_out):
    docs = emb_out.shape[0]
    both = mine[...] + other[...]
    row = lax.broadcasted_iota(jnp.int32, (docs, 128), 0)
    count = jnp.zeros((docs, 128), jnp.float32)
    for d in range(docs):
        count = jnp.where(row == d, lengths[d].astype(jnp.float32), count)
    pooled = both[0:docs] / count[:, 0:1]
    rinv = lax.rsqrt(jnp.sum(pooled * pooled, axis=1, keepdims=True) + 1e-06)
    emb_out[...] = pooled * rinv
    rinv_out[...] = jnp.broadcast_to(rinv, rinv_out.shape)
    target_out[...] = both[docs:]


def as_row(column):
    size = column.shape[0]
    same = lax.broadcasted_iota(jnp.int32, (size, size), 0) == lax.broadcasted_iota(jnp.int32, (size, size), 1)
    return jnp.sum(jnp.where(same, column, 0.0), axis=0, keepdims=True)


def score_kernel(docs, me, positive, e0, e1, e2, e3, t0, t1, t2, t3, everyone, state, expos):
    all_docs, width = everyone.shape
    y, z_lo = me[0] & 3, me[0] >> 2
    for k, piece in enumerate((e0, e1, e2, e3)):
        value = piece[...]
        turned = jnp.concatenate([value[docs:], value[0:docs]], axis=0)
        place = pl.multiple_of(((y + k) & 3) * 2 * docs, 2 * docs)
        everyone[pl.ds(place, 2 * docs), :] = jnp.where(z_lo == 1, turned, value)
    tables = (t0, t1, t2, t3)
    rows = t0.shape[0]
    emb = thirds(everyone[...])
    scores = [folded(lax.dot_general(emb, t[...], NT, preferred_element_type=jnp.float32)) / TAU for t in tables]
    tops = [jnp.max(s, axis=1, keepdims=True) for s in scores]
    top = jnp.maximum(jnp.maximum(tops[0], tops[2]), jnp.maximum(tops[1], tops[3]))
    totals, found = [], jnp.zeros((all_docs, 1), jnp.float32)
    for k, s in enumerate(scores):
        expo = jnp.exp(s - top)
        expos[:, k * rows : (k + 1) * rows] = expo
        halves = [jnp.sum(expo[:, h : h + rows // 2], axis=1, keepdims=True) for h in (0, rows // 2)]
        totals.append(halves[0] + halves[1])
        hit = row_ids(me, k, rows // 2, (all_docs, rows), 1) == positive[...]
        found = found + jnp.sum(jnp.where(hit, s, 0.0), axis=1, keepdims=True)
    total = (totals[0] + totals[2]) + (totals[1] + totals[3])
    place = pl.multiple_of(y * 2 * docs, 2 * docs)
    mine = thirds(expos[pl.ds(place, 2 * docs), :])
    mix = jnp.zeros((2 * docs, width), jnp.float32)
    for k, t in enumerate(tables):
        mix = mix + folded(jnp.dot(mine[:, k * rows : (k + 1) * rows], t[...], preferred_element_type=jnp.float32))
    column = lax.broadcasted_iota(jnp.int32, (docs, all_docs), 1)
    own = column == lax.broadcasted_iota(jnp.int32, (docs, all_docs), 0) + y * 2 * docs + z_lo * docs
    total_row, top_row, found_row = as_row(total), as_row(top), as_row(found)
    state[...] = jnp.zeros_like(state)
    state[0:docs, 0:width] = jnp.where(z_lo == 1, mix[docs:], mix[0:docs])
    for place, row in ((width, total_row), (width + 128, top_row)):
        value = jnp.sum(jnp.where(own, row, 0.0), axis=1, keepdims=True)
        state[0:docs, place : place + 128] = jnp.broadcast_to(value, (docs, 128))
    for index, row in enumerate((total_row, top_row, found_row)):
        state[docs + index : docs + index + 1, 0:all_docs] = row


def merge(docs, width, states):
    row = lax.broadcasted_iota(jnp.int32, states[0].shape, 0)
    column = lax.broadcasted_iota(jnp.int32, states[0].shape, 1)
    place = width + 128
    by_row = [s[:, place : place + 1] for s in states]
    by_lane = [s[docs + 1 : docs + 2, :] for s in states]
    top_row = functools.reduce(jnp.maximum, by_row)
    top_lane = functools.reduce(jnp.maximum, by_lane)
    terms = [
        s * jnp.exp(jnp.where(row == docs, b - top_lane, a - top_row)) for s, a, b in zip(states, by_row, by_lane)
    ]
    if len(terms) == 4:
        terms = [terms[0] + terms[2], terms[1] + terms[3]]
    joined = jnp.where((row < docs) & (column >= place), top_row, terms[0] + terms[1])
    return jnp.where(row == docs + 1, top_lane, joined)


def batch_kernel(docs, me, emb, everyone, product_out, stats):
    everything = everyone[...]
    all_docs = everything.shape[0]
    own = lax.dot_general(emb[...], everything, NT, precision=HIGHEST, preferred_element_type=jnp.float32) / TAU
    product = lax.dot_general(everything, everything, NT, precision=HIGHEST, preferred_element_type=jnp.float32) / TAU
    wide = (all_docs, all_docs)
    same = lax.broadcasted_iota(jnp.int32, wide, 0) == lax.broadcasted_iota(jnp.int32, wide, 1)
    product = jnp.where(same, -1e30, product)
    top = jnp.max(product, axis=0, keepdims=True)
    total = jnp.sum(jnp.exp(product - top), axis=0, keepdims=True)
    product_out[...] = own
    stats[...] = jnp.concatenate([top, total] * 4, axis=0)


def grad_kernel(
    me, lengths, state, emb, rinv, everyone, target, product, stats, gain, normed, rstd, turned,
    keep_out, send_out, loss_out, d_summed,
):
    docs, width = emb.shape
    all_docs = everyone.shape[0]
    y, z_lo = me[0] & 3, me[0] >> 2
    own, others, now = emb[...], everyone[...], state[...]
    total, top, found = (now[docs + k : docs + k + 1, 0:all_docs] for k in range(3))
    batch_top, batch_total = stats[0:1], stats[1:2]
    peak = jnp.maximum(top, batch_top)
    lse_row = peak + jnp.log(total * jnp.exp(top - peak) + batch_total * jnp.exp(batch_top - peak))
    loss_out[...] = jnp.broadcast_to(jnp.sum(lse_row - found, axis=1, keepdims=True) / all_docs, loss_out.shape)
    column = lax.broadcasted_iota(jnp.int32, (docs, all_docs), 1)
    same = column == lax.broadcasted_iota(jnp.int32, (docs, all_docs), 0) + y * 2 * docs + z_lo * docs
    lse = jnp.sum(jnp.where(same, lse_row, 0.0), axis=1, keepdims=True)
    scores = product[...]
    g_batch = jnp.where(same, 0.0, jnp.exp(scores - lse) + jnp.exp(scores - lse_row)) / all_docs
    mix = now[0:docs, 0:width] * jnp.exp(now[0:docs, width + 128 : width + 129] - lse)
    from_batch = jnp.dot(g_batch, others, precision=HIGHEST, preferred_element_type=jnp.float32)
    d_emb = ((mix - target[...]) / all_docs + from_batch) / TAU
    d_pooled = (d_emb - own * jnp.sum(own * d_emb, axis=1, keepdims=True)) * rinv[:, 0:1]
    tb = normed.shape[1]
    for doc in range(docs):
        dy = d_pooled[doc : doc + 1] / lengths[doc].astype(jnp.float32) * gain[...]
        level = dy - jnp.mean(dy, axis=1, keepdims=True)
        unit = normed[doc].astype(jnp.float32)
        along = jnp.mean(unit * dy, axis=1, keepdims=True)
        keep = me[1] * tb + lax.broadcasted_iota(jnp.int32, (tb, 1), 0) < lengths[doc]
        scale = jnp.where(keep, rstd[doc, :, 0:1], 0.0)
        d_summed[doc * tb : (doc + 1) * tb, :] = (scale * (level - unit * along)).astype(jnp.bfloat16)
    half = width // 2
    send_out[...] = jnp.dot(turned[half:], d_summed[...], preferred_element_type=jnp.float32)
    keep_out[...] = jnp.dot(turned[0:half], d_summed[...], preferred_element_type=jnp.float32)


def sum_kernel(count, *refs):
    terms, outs = refs[:count], refs[count:]
    total = terms[0][...].astype(jnp.float32)
    for term in terms[1:]:
        total = total + term[...].astype(jnp.float32)
    rows = outs[0].shape[0]
    for index, out in enumerate(outs):
        out[...] = total[index * rows : (index + 1) * rows].astype(out.dtype)


def sum_and_split(terms, kind):
    rows, width = terms[0].shape
    piece = (rows // 4, width)
    shapes = (f32(*piece),) + (jax.ShapeDtypeStruct(piece, kind),) * 3
    return call(
        functools.partial(sum_kernel, len(terms)), shapes, [VMEM] * len(terms), (VMEM,) * 4, limit=8, name="sum_split"
    )(*terms)


def shards(tokens, w_qkv, w_out, ln_gain, cache, positive, lengths):
    docs, tb, width = tokens.shape
    n_ctx, n_dp = lax.axis_size("ctx"), lax.axis_size("dp")
    devices = n_dp * n_ctx
    dp, ctx = lax.axis_index("dp"), lax.axis_index("ctx")
    me = jnp.stack([dp, ctx]).astype(jnp.int32)
    all_docs = n_dp * docs
    halos = []
    for first in range(0, docs, CHUNK):
        part = tokens[first : first + CHUNK]
        left = lax.ppermute(part, "ctx", [(i, i + 1) for i in range(n_ctx - 1)])
        right = lax.ppermute(part, "ctx", [(i + 1, i) for i in range(n_ctx - 1)])
        halos.append((left, right))
    tables = around(jnp.concatenate([cache, swap(cache, "dp", 4)], axis=0), from_y)
    target = call(
        functools.partial(target_kernel, docs), f32(docs, width), [SMEM, SMEM] + [VMEM] * 4, VMEM, name="target"
    )(me, positive, *tables)

    gain = ln_gain.reshape(1, width)
    flat = tokens.reshape(docs * tb, width)
    w_v_turned = w_qkv[:, 2 * width :].T
    qk = jnp.dot(flat, w_qkv[:, : 2 * width], preferred_element_type=jnp.float32).astype(jnp.bfloat16)
    v_turned = lax.dot_general(w_v_turned, flat, NT, preferred_element_type=jnp.float32).astype(jnp.bfloat16)
    qk = qk.reshape(docs, tb, 2 * width)
    done = None
    for index, (left, right) in enumerate(halos):
        done = attend(
            index * CHUNK, done, me, lengths, tokens, left, right, qk, v_turned, w_qkv, w_v_turned, w_out, gain
        )
    hidden, mixed, normed, rstd, pool = done

    place = jnp.arange(width, dtype=jnp.int32)
    each = width // devices
    core = (ctx & 1) ^ (place // (64 * each))
    y = ((dp & 3) + place // (16 * each) % 4) & 3
    x = ((ctx >> 2) + place // (4 * each) % 4) & 3
    z = ((ctx & 2) + (dp >> 2) + place // each % 4) & 3
    block = ((z & 1) * 4 + y) * n_ctx + x * 4 + (z >> 1) * 2 + core
    chosen = ((block * each + place % each)[:, None] == place[None, :]).astype(jnp.bfloat16)
    turned = jnp.dot(chosen, mixed, preferred_element_type=jnp.float32).astype(jnp.bfloat16)

    sums = jnp.concatenate([pool.reshape(docs, width), target], axis=0)
    sums = sums + swap(sums, "ctx", 1)
    terms = around(sums, from_x)
    sums = (terms[0] + terms[2]) + (terms[1] + terms[3])
    emb, rinv, target = call(
        norm_kernel,
        (f32(docs, width), f32(docs, 128), f32(docs, width)),
        [SMEM, VMEM, VMEM],
        (VMEM,) * 3,
        limit=4,
        name="norm",
    )(lengths, sums, swap(sums, "ctx", 2))
    embs = around(jnp.concatenate([emb, swap(emb, "dp", 4)], axis=0), from_y)
    wanted = positive.reshape(2, 4, docs).transpose(1, 0, 2).reshape(all_docs, 1)
    everyone, state = call(
        functools.partial(score_kernel, docs),
        (f32(all_docs, width), f32(2 * docs, width + 256)),
        [SMEM] + [VMEM] * 9,
        (VMEM, VMEM),
        moved=2 * 2**20,
        scratch_shapes=[pltpu.VMEM((all_docs, n_dp * cache.shape[0]), jnp.float32)],
        name="score",
    )(me, wanted, *embs, *tables)
    product, stats = call(
        functools.partial(batch_kernel, docs),
        (f32(docs, all_docs), f32(8, all_docs)),
        [SMEM, VMEM, VMEM],
        (VMEM, VMEM),
        limit=4,
        name="batch",
    )(me, emb, everyone)
    state = merge(docs, width, [state, swap(state, "ctx", 1)])
    state = merge(docs, width, around(state, from_x))
    state = merge(docs, width, [state, swap(state, "ctx", 2)])
    half = width // 2
    keep, send, loss = call(
        grad_kernel,
        (f32(half, width), f32(half, width), f32(8, 128)),
        [SMEM, SMEM] + [VMEM] * 11,
        (VMEM,) * 3,
        flops=2 * docs * tb * width * width,
        moved=8 * 2**20,
        scratch_shapes=[pltpu.VMEM((docs * tb, width), jnp.bfloat16)],
        name="grad",
    )(me, lengths, state, emb, rinv, everyone, target, product, stats, gain, normed, rstd, turned)
    keep, *sends = sum_and_split([keep, swap(send, "ctx", 1)], jnp.bfloat16)
    got = [from_y(piece, -(k + 1)) for k, piece in enumerate(sends)]
    keep, *sends = sum_and_split([keep] + got, jnp.float32)
    got = [from_x(piece, -(k + 1)) for k, piece in enumerate(sends)]
    keep, *sends = sum_and_split([keep] + got, jnp.float32)
    got = [from_z(piece, -(k + 1)) for k, piece in enumerate(sends)]
    return (hidden, loss[0, 0], keep + got[0] + got[1] + got[2])


def solution(mesh):
    placed = (P("dp", "ctx", None), P(), P(), P(), P(("dp", "ctx"), None), P(), P("dp"))
    return jax.shard_map(
        shards,
        mesh=mesh,
        in_specs=placed,
        out_specs=(P("dp", "ctx", None), P(), P(("dp", "ctx"), None)),
        check_vma=False,
    )
```

```python
import functools
import math

import jax
import jax.numpy as jnp
from jax import lax
from jax.experimental import pallas as pl
from jax.experimental.pallas import tpu as pltpu
from jax.sharding import PartitionSpec as P

H = 12
WIN = 256
TAU = 0.02
FAR = 1e32
CHUNK = 2
NT = (((1,), (1,)), ((), ()))
TN = (((0,), (0,)), ((), ()))
HIGHEST = lax.Precision.HIGHEST
VMEM = pl.BlockSpec(memory_space=pltpu.VMEM)
SMEM = pl.BlockSpec(memory_space=pltpu.SMEM)
ANY = pl.BlockSpec(memory_space=pl.ANY)


def swap(value, axis, bits):
    return lax.ppermute(value, axis, [(i, i ^ bits) for i in range(lax.axis_size(axis))])


def from_x(value, k):
    size = lax.axis_size("ctx")
    return lax.ppermute(value, "ctx", [((c + 4 * k) % size, c) for c in range(size)])


def from_y(value, k):
    return lax.ppermute(value, "dp", [((d & 4) | ((d + k) & 3), d) for d in range(lax.axis_size("dp"))])


def from_z(value, k):
    n_dp, n_ctx = lax.axis_size("dp"), lax.axis_size("ctx")
    pairs = []
    for d in range(n_dp):
        for c in range(n_ctx):
            z = ((c & 2) + (d >> 2) + k) & 3
            pairs.append((((z & 1) * 4 + (d & 3)) * n_ctx + (c & ~2) + (z & 2), d * n_ctx + c))
    return lax.ppermute(value, ("dp", "ctx"), pairs)


def around(value, fetch):
    return [value] + [fetch(value, k) for k in (1, 2, 3)]


def call(kernel, out_shape, in_specs, out_specs, limit=24, flops=0, moved=0, **keywords):
    return pl.pallas_call(
        kernel,
        out_shape=out_shape,
        in_specs=in_specs,
        out_specs=out_specs,
        compiler_params=pltpu.CompilerParams(vmem_limit_bytes=limit * 2**20),
        cost_estimate=pl.CostEstimate(flops=flops, bytes_accessed=moved, transcendentals=0),
        **keywords,
    )


def f32(*shape):
    return jax.ShapeDtypeStruct(shape, jnp.float32)


def bf16(*shape):
    return jax.ShapeDtypeStruct(shape, jnp.bfloat16)


def slopes_of(heads):
    largest = 2 ** int(math.floor(math.log2(heads)))
    listed = [2.0 ** (-8.0 * (h + 1) / largest) for h in range(largest)]
    return listed + [2.0 ** (-4.0 * (2 * m + 1) / largest) for m in range(heads - largest)]


def thirds(value):
    high = value.astype(jnp.bfloat16)
    rest = value - high.astype(jnp.float32)
    middle = rest.astype(jnp.bfloat16)
    low = (rest - middle.astype(jnp.float32)).astype(jnp.bfloat16)
    parts = [p.astype(jnp.float32) for p in (high, middle, low)]
    return jnp.concatenate(parts, axis=0).astype(jnp.bfloat16)


def folded(products):
    rows = products.shape[0] // 3
    return products[0:rows] + products[rows : 2 * rows] + products[2 * rows :]


def attend_kernel(
    first, me, lengths, tok, left, right, qk, v_turned, w_k, w_v_turned, w_out, gain, *refs
):
    hidden, mixed, normed, rstd_out, pool, keys, values, dist = refs[-8:]
    tb, width = tok.shape[1:]
    ext = tb + 2 * WIN
    start, length = me[1] * tb, lengths[first + pl.program_id(0)]
    rows = jnp.concatenate([left[0], right[0]], axis=0)
    new = jnp.dot(rows, w_k[...], preferred_element_type=jnp.float32).astype(jnp.bfloat16)
    keys[0:WIN] = new[0:WIN]
    keys[WIN : WIN + tb] = qk[0, :, width:]
    keys[WIN + tb :] = new[WIN:]
    new = lax.dot_general(w_v_turned[...], rows, NT, preferred_element_type=jnp.float32).astype(jnp.bfloat16)
    values[:, 0:WIN] = new[:, 0:WIN]
    values[:, WIN : WIN + tb] = v_turned[...]
    values[:, WIN + tb :] = new[:, WIN:]
    j = lax.broadcasted_iota(jnp.int32, (ext, tb), 0) - WIN
    away = jnp.abs(lax.broadcasted_iota(jnp.int32, (ext, tb), 1) - j)
    kpos = start + j
    seen = (away <= WIN) & (((kpos >= 0) & (kpos < length)) | (away == 0))
    dist[...] = jnp.where(seen, away.astype(jnp.float32), FAR)
    half = lax.broadcasted_iota(jnp.int32, (tb, 128), 1) < 64
    slopes = slopes_of(H)
    lanes = 128
    span = lanes + 2 * WIN
    for pair in range(H // 2):
        cols = pl.ds(pair * 128, 128)
        query = qk[0, :, cols] * jnp.bfloat16(0.125)
        zero = jnp.bfloat16(0)
        both = jnp.concatenate([jnp.where(half, query, zero), jnp.where(half, zero, query)], axis=0)
        scores = lax.dot_general(keys[:, cols], both, NT, preferred_element_type=jnp.float32)
        for part in range(2):
            columns = []
            for low in range(0, tb, lanes):
                score = scores[low : low + span, part * tb + low : part * tb + low + lanes]
                score = score - slopes[2 * pair + part] * dist[pl.ds(low, span), pl.ds(low, lanes)]
                expo = jnp.exp(score - jnp.max(score, axis=0, keepdims=True))
                weights = (expo * (1.0 / jnp.sum(expo, axis=0, keepdims=True))).astype(jnp.bfloat16)
                above, below = low, ext - span - low
                pieces = [weights]
                if above:
                    pieces = [jnp.zeros((above, lanes), jnp.bfloat16)] + pieces
                if below:
                    pieces = pieces + [jnp.zeros((below, lanes), jnp.bfloat16)]
                columns.append(jnp.concatenate(pieces, axis=0))
            weights = jnp.concatenate(columns, axis=1)
            head = pl.ds(pair * 128 + part * 64, 64)
            mixed[head, :] = jnp.dot(values[head, :], weights, preferred_element_type=jnp.float32).astype(jnp.bfloat16)
    summed = tok[0].astype(jnp.float32) + lax.dot_general(mixed[...], w_out[...], TN, preferred_element_type=jnp.float32)
    centred = summed - jnp.mean(summed, axis=1, keepdims=True)
    rstd = lax.rsqrt(jnp.mean(centred * centred, axis=1, keepdims=True) + 1e-05)
    unit = centred * rstd
    hidden_f = unit * gain[...]
    hidden[0] = hidden_f.astype(jnp.bfloat16)
    normed[0] = unit.astype(jnp.bfloat16)
    rstd_out[0] = jnp.broadcast_to(rstd, rstd_out.shape[1:])
    keep = start + lax.broadcasted_iota(jnp.int32, (tb, 1), 0) < length
    pool[0] = jnp.sum(jnp.where(keep, hidden_f, 0.0), axis=0, keepdims=True) / length.astype(jnp.float32)


def attend(first, before, me, lengths, tokens, left, right, qk, v_turned, w_qkv, w_v_turned, w_out, gain):
    docs, tb, width = tokens.shape
    ext = tb + 2 * WIN
    here = lambda *s: pl.BlockSpec((1,) + s, lambda i: (first + i, 0, 0))
    chunk = lambda *s: pl.BlockSpec((1,) + s, lambda i: (i, 0, 0))
    column = pl.BlockSpec((width, tb), lambda i: (0, first + i))
    fixed = lambda s, at=(0, 0): pl.BlockSpec(s, lambda i: at, pipeline_mode=pl.Buffered(1))
    out_shape = (bf16(docs, tb, width), bf16(width, docs * tb), bf16(docs, tb, width), f32(docs, tb, 128), f32(docs, 1, width))
    in_specs = [
        SMEM, SMEM, here(tb, width), chunk(WIN, width), chunk(WIN, width), here(tb, 2 * width), column,
        fixed((width, width), (0, 1)), fixed((width, width)), fixed((width, width)), fixed((1, width)),
    ]
    operands = [me, lengths, tokens, left, right, qk, v_turned, w_qkv, w_v_turned, w_out, gain]
    aliases = {}
    if before is not None:
        aliases = {len(operands) + k: k for k in range(len(out_shape))}
        operands = operands + list(before)
        in_specs = in_specs + [ANY] * len(out_shape)
    return call(
        functools.partial(attend_kernel, first),
        out_shape,
        in_specs,
        (here(tb, width), column, here(tb, width), here(tb, 128), here(1, width)),
        limit=32,
        flops=CHUNK * 5 * 2 * tb * ext * width,
        moved=8 * 2**20,
        grid=(CHUNK,),
        scratch_shapes=[
            pltpu.VMEM((ext, width), jnp.bfloat16),
            pltpu.VMEM((width, ext), jnp.bfloat16),
            pltpu.VMEM((ext, tb), jnp.float32),
        ],
        input_output_aliases=aliases,
        name="attend",
    )(*operands)


def row_ids(me, k, rows, shape, dim):
    place = lax.broadcasted_iota(jnp.int32, shape, dim)
    y, z_lo = (me[0] + k) & 3, me[0] >> 2
    other = (place >= rows).astype(jnp.int32)
    owner = (z_lo + other - 2 * z_lo * other) * 4 + y
    return (owner * 16 + me[1]) * rows + place - other * rows


def target_kernel(docs, me, positive, *refs):
    pieces, out = refs[:4], refs[4]
    total = jnp.zeros(out.shape, jnp.float32)
    for k, piece in enumerate(pieces):
        rows = piece.shape[0]
        ids = row_ids(me, k, rows // 2, (8, rows), 1)
        doc = lax.broadcasted_iota(jnp.int32, (8, rows), 0)
        wanted = jnp.full((8, rows), -1, jnp.int32)
        for d in range(docs):
            wanted = jnp.where(doc == d, positive[me[0] * docs + d], wanted)
        hit = (ids == wanted).astype(jnp.float32).astype(jnp.bfloat16)
        total = total + jnp.dot(hit, piece[...], preferred_element_type=jnp.float32)[0:docs]
    out[...] = total


def turn_kernel(me, mixed, out):
    width = out.shape[0]
    place = lax.broadcasted_iota(jnp.int32, (width, 1), 0)
    dp, ctx = me[0], me[1]
    each = width // 128
    core = (ctx & 1) ^ (place // (64 * each))
    y = ((dp & 3) + place // (16 * each) % 4) & 3
    x = ((ctx >> 2) + place // (4 * each) % 4) & 3
    z = ((ctx & 2) + (dp >> 2) + place // each % 4) & 3
    block = ((z & 1) * 4 + y) * 16 + x * 4 + (z >> 1) * 2 + core
    chosen = block * each + place % each == lax.broadcasted_iota(jnp.int32, (width, width), 1)
    chosen = jnp.where(chosen, 1.0, 0.0).astype(jnp.bfloat16)
    out[...] = jnp.dot(chosen, mixed[...], preferred_element_type=jnp.float32).astype(jnp.bfloat16)


def norm_kernel(s0, s1, s2, s3, emb_out, rinv_out, target_out):
    docs = target_out.shape[0]
    own, other = s0[...] + s2[...], s1[0:docs] + s3[0:docs]
    pooled = jnp.concatenate([own[0:docs], other], axis=0)
    rinv = lax.rsqrt(jnp.sum(pooled * pooled, axis=1, keepdims=True) + 1e-06)
    emb_out[...] = pooled * rinv
    rinv_out[...] = jnp.broadcast_to(rinv, rinv_out.shape)
    target_out[...] = own[docs:]


def as_row(column):
    size = column.shape[0]
    same = lax.broadcasted_iota(jnp.int32, (size, size), 0) == lax.broadcasted_iota(jnp.int32, (size, size), 1)
    return jnp.sum(jnp.where(same, column, 0.0), axis=0, keepdims=True)


def score_kernel(docs, me, positive, e0, e1, e2, e3, t0, t1, t2, t3, everyone, state, expos):
    all_docs, width = everyone.shape
    y, z_lo = me[0] & 3, me[0] >> 2
    for k, piece in enumerate((e0, e1, e2, e3)):
        value = piece[...]
        turned = jnp.concatenate([value[docs:], value[0:docs]], axis=0)
        place = pl.multiple_of(((y + k) & 3) * 2 * docs, 2 * docs)
        everyone[pl.ds(place, 2 * docs), :] = jnp.where(z_lo == 1, turned, value)
    tables = (t0, t1, t2, t3)
    rows = t0.shape[0]
    emb = thirds(everyone[...])
    scores = [folded(lax.dot_general(emb, t[...], NT, preferred_element_type=jnp.float32)) / TAU for t in tables]
    tops = [jnp.max(s, axis=1, keepdims=True) for s in scores]
    top = jnp.maximum(jnp.maximum(tops[0], tops[2]), jnp.maximum(tops[1], tops[3]))
    totals, found = [], jnp.zeros((all_docs, 1), jnp.float32)
    for k, s in enumerate(scores):
        expo = jnp.exp(s - top)
        expos[:, k * rows : (k + 1) * rows] = expo
        halves = [jnp.sum(expo[:, h : h + rows // 2], axis=1, keepdims=True) for h in (0, rows // 2)]
        totals.append(halves[0] + halves[1])
        hit = row_ids(me, k, rows // 2, (all_docs, rows), 1) == positive[...]
        found = found + jnp.sum(jnp.where(hit, s, 0.0), axis=1, keepdims=True)
    total = (totals[0] + totals[2]) + (totals[1] + totals[3])
    place = pl.multiple_of(y * 2 * docs, 2 * docs)
    mine = thirds(expos[pl.ds(place, 2 * docs), :])
    mix = jnp.zeros((2 * docs, width), jnp.float32)
    for k, t in enumerate(tables):
        mix = mix + folded(jnp.dot(mine[:, k * rows : (k + 1) * rows], t[...], preferred_element_type=jnp.float32))
    column = lax.broadcasted_iota(jnp.int32, (docs, all_docs), 1)
    own = column == lax.broadcasted_iota(jnp.int32, (docs, all_docs), 0) + y * 2 * docs + z_lo * docs
    total_row, top_row, found_row = as_row(total), as_row(top), as_row(found)
    state[...] = jnp.zeros_like(state)
    state[0:docs, 0:width] = jnp.where(z_lo == 1, mix[docs:], mix[0:docs])
    for place, row in ((width, total_row), (width + 128, top_row)):
        value = jnp.sum(jnp.where(own, row, 0.0), axis=1, keepdims=True)
        state[0:docs, place : place + 128] = jnp.broadcast_to(value, (docs, 128))
    for index, row in enumerate((total_row, top_row, found_row)):
        state[docs + index : docs + index + 1, 0:all_docs] = row


def merge(docs, width, states):
    row = lax.broadcasted_iota(jnp.int32, states[0].shape, 0)
    column = lax.broadcasted_iota(jnp.int32, states[0].shape, 1)
    place = width + 128
    by_row = [s[:, place : place + 1] for s in states]
    by_lane = [s[docs + 1 : docs + 2, :] for s in states]
    top_row = functools.reduce(jnp.maximum, by_row)
    top_lane = functools.reduce(jnp.maximum, by_lane)
    terms = [
        s * jnp.exp(jnp.where(row == docs, b - top_lane, a - top_row)) for s, a, b in zip(states, by_row, by_lane)
    ]
    if len(terms) == 4:
        terms = [terms[0] + terms[2], terms[1] + terms[3]]
    joined = jnp.where((row < docs) & (column >= place), top_row, terms[0] + terms[1])
    return jnp.where(row == docs + 1, top_lane, joined)


def batch_kernel(docs, me, emb, everyone, product_out, stats):
    everything = everyone[...]
    all_docs = everything.shape[0]
    own = lax.dot_general(emb[...], everything, NT, precision=HIGHEST, preferred_element_type=jnp.float32) / TAU
    product = lax.dot_general(everything, everything, NT, precision=HIGHEST, preferred_element_type=jnp.float32) / TAU
    wide = (all_docs, all_docs)
    same = lax.broadcasted_iota(jnp.int32, wide, 0) == lax.broadcasted_iota(jnp.int32, wide, 1)
    product = jnp.where(same, -1e30, product)
    top = jnp.max(product, axis=0, keepdims=True)
    total = jnp.sum(jnp.exp(product - top), axis=0, keepdims=True)
    product_out[...] = own
    stats[...] = jnp.concatenate([top, total] * 4, axis=0)


def grad_kernel(
    me, lengths, state, other, emb, rinv, everyone, target, product, stats, gain, normed, rstd, turned,
    keep_out, send_out, loss_out, d_summed,
):
    docs, width = target.shape
    all_docs = everyone.shape[0]
    y, z_lo = me[0] & 3, me[0] >> 2
    own, others = emb[0:docs], everyone[...]
    now = merge(docs, width, [state[...], other[...]])
    total, top, found = (now[docs + k : docs + k + 1, 0:all_docs] for k in range(3))
    batch_top, batch_total = stats[0:1], stats[1:2]
    peak = jnp.maximum(top, batch_top)
    lse_row = peak + jnp.log(total * jnp.exp(top - peak) + batch_total * jnp.exp(batch_top - peak))
    loss_out[...] = jnp.broadcast_to(jnp.sum(lse_row - found, axis=1, keepdims=True) / all_docs, loss_out.shape)
    column = lax.broadcasted_iota(jnp.int32, (docs, all_docs), 1)
    same = column == lax.broadcasted_iota(jnp.int32, (docs, all_docs), 0) + y * 2 * docs + z_lo * docs
    lse = jnp.sum(jnp.where(same, lse_row, 0.0), axis=1, keepdims=True)
    scores = product[0:docs]
    g_batch = jnp.where(same, 0.0, jnp.exp(scores - lse) + jnp.exp(scores - lse_row)) / all_docs
    mix = now[0:docs, 0:width] * jnp.exp(now[0:docs, width + 128 : width + 129] - lse)
    from_batch = jnp.dot(g_batch, others, precision=HIGHEST, preferred_element_type=jnp.float32)
    d_emb = ((mix - target[...]) / all_docs + from_batch) / TAU
    d_pooled = (d_emb - own * jnp.sum(own * d_emb, axis=1, keepdims=True)) * rinv[0:docs, 0:1]
    tb = normed.shape[1]
    for doc in range(docs):
        dy = d_pooled[doc : doc + 1] / lengths[doc].astype(jnp.float32) * gain[...]
        level = dy - jnp.mean(dy, axis=1, keepdims=True)
        unit = normed[doc].astype(jnp.float32)
        along = jnp.mean(unit * dy, axis=1, keepdims=True)
        keep = me[1] * tb + lax.broadcasted_iota(jnp.int32, (tb, 1), 0) < lengths[doc]
        scale = jnp.where(keep, rstd[doc, :, 0:1], 0.0)
        d_summed[doc * tb : (doc + 1) * tb, :] = (scale * (level - unit * along)).astype(jnp.bfloat16)
    half = width // 2
    send_out[...] = jnp.dot(turned[half:], d_summed[...], preferred_element_type=jnp.float32)
    keep_out[...] = jnp.dot(turned[0:half], d_summed[...], preferred_element_type=jnp.float32)


def sum_kernel(count, *refs):
    terms, outs = refs[:count], refs[count:]
    total = terms[0][...].astype(jnp.float32)
    for term in terms[1:]:
        total = total + term[...].astype(jnp.float32)
    rows = outs[0].shape[0]
    for index, out in enumerate(outs):
        out[...] = total[index * rows : (index + 1) * rows].astype(out.dtype)


def sum_and_split(terms, kind):
    rows, width = terms[0].shape
    piece = (rows // 4, width)
    shapes = (f32(*piece),) + (jax.ShapeDtypeStruct(piece, kind),) * 3
    return call(
        functools.partial(sum_kernel, len(terms)), shapes, [VMEM] * len(terms), (VMEM,) * 4, limit=8, name="sum_split"
    )(*terms)


def shards(tokens, w_qkv, w_out, ln_gain, cache, positive, lengths):
    docs, tb, width = tokens.shape
    n_ctx, n_dp = lax.axis_size("ctx"), lax.axis_size("dp")
    dp, ctx = lax.axis_index("dp"), lax.axis_index("ctx")
    me = jnp.stack([dp, ctx]).astype(jnp.int32)
    all_docs = n_dp * docs
    halos = []
    parts = [tokens[first : first + CHUNK] for first in range(0, docs, CHUNK)]
    *parts, cache = lax.optimization_barrier((*parts, cache))
    for part in parts:
        left = lax.ppermute(part, "ctx", [(i, (i + 1) % n_ctx) for i in range(n_ctx)])
        right = lax.ppermute(part, "ctx", [((i + 1) % n_ctx, i) for i in range(n_ctx)])
        halos.append((left, right))
    tables = around(jnp.concatenate([cache, swap(cache, "dp", 4)], axis=0), from_y)
    gain = ln_gain.reshape(1, width)
    flat = tokens.reshape(docs * tb, width)
    w_v_turned = w_qkv[:, 2 * width :].T
    qk = jnp.dot(flat, w_qkv[:, : 2 * width], preferred_element_type=jnp.float32).astype(jnp.bfloat16)
    v_turned = lax.dot_general(w_v_turned, flat, NT, preferred_element_type=jnp.float32).astype(jnp.bfloat16)
    qk = qk.reshape(docs, tb, 2 * width)
    done = None
    for index, (left, right) in enumerate(halos):
        if index == 1:
            *done, pool = done
            pool, after = lax.optimization_barrier((pool, positive))
            done = [*done, pool]
            target = call(
                functools.partial(target_kernel, docs), f32(docs, width), [SMEM, SMEM] + [VMEM] * 4, VMEM, name="target"
            )(me, after, *tables)
        done = attend(
            index * CHUNK, done, me, lengths, tokens, left, right, qk, v_turned, w_qkv, w_v_turned, w_out, gain
        )
    hidden, mixed, normed, rstd, pool = done

    turned = call(
        turn_kernel,
        bf16(width, docs * tb),
        [SMEM, VMEM],
        VMEM,
        flops=2 * docs * tb * width * width,
        moved=4 * 2**20,
        name="turn",
    )(me, mixed)

    sums = jnp.concatenate([pool.reshape(docs, width), target], axis=0)
    sums = sums + swap(sums, "ctx", 1)
    terms = around(sums, from_x)
    sums = (terms[0] + terms[2]) + (terms[1] + terms[3])
    emb, rinv, target = call(
        norm_kernel,
        (f32(2 * docs, width), f32(2 * docs, 128), f32(docs, width)),
        [VMEM] * 4,
        (VMEM,) * 3,
        limit=4,
        name="norm",
    )(*around(sums, from_z))
    embs = around(emb, from_y)
    wanted = positive.reshape(2, 4, docs).transpose(1, 0, 2).reshape(all_docs, 1)
    everyone, state = call(
        functools.partial(score_kernel, docs),
        (f32(all_docs, width), f32(2 * docs, width + 256)),
        [SMEM] + [VMEM] * 9,
        (VMEM, VMEM),
        moved=2 * 2**20,
        scratch_shapes=[pltpu.VMEM((all_docs, n_dp * cache.shape[0]), jnp.float32)],
        name="score",
    )(me, wanted, *embs, *tables)
    product, stats = call(
        functools.partial(batch_kernel, docs),
        (f32(2 * docs, all_docs), f32(8, all_docs)),
        [SMEM, VMEM, VMEM],
        (VMEM, VMEM),
        limit=4,
        name="batch",
    )(me, emb, everyone)
    state = merge(docs, width, [state, swap(state, "ctx", 1)])
    state = merge(docs, width, around(state, from_x))
    half = width // 2
    keep, send, loss = call(
        grad_kernel,
        (f32(half, width), f32(half, width), f32(8, 128)),
        [SMEM, SMEM] + [VMEM] * 12,
        (VMEM,) * 3,
        flops=2 * docs * tb * width * width,
        moved=8 * 2**20,
        scratch_shapes=[pltpu.VMEM((docs * tb, width), jnp.bfloat16)],
        name="grad",
    )(
        me, lengths, state, swap(state, "ctx", 2), emb, rinv, everyone, target, product, stats, gain, normed, rstd, turned,
    )
    keep, *sends = sum_and_split([keep, swap(send, "ctx", 1)], jnp.bfloat16)
    got = [from_y(piece, -(k + 1)) for k, piece in enumerate(sends)]
    keep, *sends = sum_and_split([keep] + got, jnp.float32)
    got = [from_x(piece, -(k + 1)) for k, piece in enumerate(sends)]
    keep, *sends = sum_and_split([keep] + got, jnp.float32)
    got = [from_z(piece, -(k + 1)) for k, piece in enumerate(sends)]
    return (hidden, loss[0, 0], keep + got[0] + got[1] + got[2])


def solution(mesh):
    placed = (P("dp", "ctx", None), P(), P(), P(), P(("dp", "ctx"), None), P(), P("dp"))
    return jax.shard_map(
        shards,
        mesh=mesh,
        in_specs=placed,
        out_specs=(P("dp", "ctx", None), P(), P(("dp", "ctx"), None)),
        check_vma=False,
    )
```

```python
import functools
import math

import jax
import jax.numpy as jnp
from jax import lax
from jax.experimental import pallas as pl
from jax.experimental.pallas import tpu as pltpu
from jax.sharding import PartitionSpec as P

H = 12
WIN = 256
TAU = 0.02
FAR = 1e32
CHUNK = 2
NT = (((1,), (1,)), ((), ()))
TN = (((0,), (0,)), ((), ()))
HIGHEST = lax.Precision.HIGHEST
VMEM = pl.BlockSpec(memory_space=pltpu.VMEM)
SMEM = pl.BlockSpec(memory_space=pltpu.SMEM)
ANY = pl.BlockSpec(memory_space=pl.ANY)


def swap(value, axis, bits):
    return lax.ppermute(value, axis, [(i, i ^ bits) for i in range(lax.axis_size(axis))])


def from_x(value, k):
    size = lax.axis_size("ctx")
    return lax.ppermute(value, "ctx", [((c + 4 * k) % size, c) for c in range(size)])


def from_y(value, k):
    return lax.ppermute(value, "dp", [((d & 4) | ((d + k) & 3), d) for d in range(lax.axis_size("dp"))])


def from_z(value, k):
    n_dp, n_ctx = lax.axis_size("dp"), lax.axis_size("ctx")
    pairs = []
    for d in range(n_dp):
        for c in range(n_ctx):
            z = ((c & 2) + (d >> 2) + k) & 3
            pairs.append((((z & 1) * 4 + (d & 3)) * n_ctx + (c & ~2) + (z & 2), d * n_ctx + c))
    return lax.ppermute(value, ("dp", "ctx"), pairs)


def from_plane(value, k, last):
    n_dp, n_ctx = lax.axis_size("dp"), lax.axis_size("ctx")
    pairs = []
    for d in range(n_dp):
        for c in range(n_ctx):
            along_y = (c & 1 == 1) == last
            source = ((d & 4) | ((d + k) & 3), c) if along_y else (d, (c + 4 * k) % n_ctx)
            pairs.append((source[0] * n_ctx + source[1], d * n_ctx + c))
    return lax.ppermute(value, ("dp", "ctx"), pairs)


def around(value, fetch):
    return [value] + [fetch(value, k) for k in (1, 2, 3)]


def here():
    return lax.axis_index("dp"), lax.axis_index("ctx")


def in_hbm(value):
    return pltpu.with_memory_space_constraint(value, pltpu.HBM)


def call(kernel, out_shape, in_specs, out_specs, limit=16, flops=0, moved=0, **keywords):
    return pl.pallas_call(
        kernel,
        out_shape=out_shape,
        in_specs=in_specs,
        out_specs=out_specs,
        compiler_params=pltpu.CompilerParams(vmem_limit_bytes=limit * 2**20),
        cost_estimate=pl.CostEstimate(flops=flops, bytes_accessed=moved, transcendentals=0),
        **keywords,
    )


def f32(*shape):
    return jax.ShapeDtypeStruct(shape, jnp.float32)


def bf16(*shape):
    return jax.ShapeDtypeStruct(shape, jnp.bfloat16)


def slopes_of(heads):
    largest = 2 ** int(math.floor(math.log2(heads)))
    listed = [2.0 ** (-8.0 * (h + 1) / largest) for h in range(largest)]
    return listed + [2.0 ** (-4.0 * (2 * m + 1) / largest) for m in range(heads - largest)]


def thirds(value):
    high = value.astype(jnp.bfloat16)
    rest = value - high.astype(jnp.float32)
    middle = rest.astype(jnp.bfloat16)
    low = (rest - middle.astype(jnp.float32)).astype(jnp.bfloat16)
    parts = [p.astype(jnp.float32) for p in (high, middle, low)]
    return jnp.concatenate(parts, axis=0).astype(jnp.bfloat16)


def folded(products):
    rows = products.shape[0] // 3
    return products[0:rows] + products[rows : 2 * rows] + products[2 * rows :]


def attend_kernel(
    first, lengths, tok, left, right, qk, v_turned, w_k, w_v_turned, w_out, gain, *refs
):
    hidden, mixed, normed, rstd_out, pool, keys, values, dist = refs[-8:]
    tb, width = tok.shape[1:]
    ext = tb + 2 * WIN
    start, length = lax.axis_index("ctx") * tb, lengths[first + pl.program_id(0)]
    rows = jnp.concatenate([left[0], right[0]], axis=0)
    new = jnp.dot(rows, w_k[...], preferred_element_type=jnp.float32).astype(jnp.bfloat16)
    keys[0:WIN] = new[0:WIN]
    keys[WIN : WIN + tb] = qk[0, :, width:]
    keys[WIN + tb :] = new[WIN:]
    new = lax.dot_general(w_v_turned[...], rows, NT, preferred_element_type=jnp.float32).astype(jnp.bfloat16)
    values[:, 0:WIN] = new[:, 0:WIN]
    values[:, WIN : WIN + tb] = v_turned[...]
    values[:, WIN + tb :] = new[:, WIN:]
    j = lax.broadcasted_iota(jnp.int32, (ext, tb), 0) - WIN
    away = jnp.abs(lax.broadcasted_iota(jnp.int32, (ext, tb), 1) - j)
    kpos = start + j
    seen = (away <= WIN) & (((kpos >= 0) & (kpos < length)) | (away == 0))
    dist[...] = jnp.where(seen, away.astype(jnp.float32), FAR)
    half = lax.broadcasted_iota(jnp.int32, (tb, 128), 1) < 64
    slopes = slopes_of(H)
    lanes = 128
    span = lanes + 2 * WIN
    for pair in range(H // 2):
        cols = pl.ds(pair * 128, 128)
        query = qk[0, :, cols] * jnp.bfloat16(0.125)
        zero = jnp.bfloat16(0)
        both = jnp.concatenate([jnp.where(half, query, zero), jnp.where(half, zero, query)], axis=0)
        scores = lax.dot_general(keys[:, cols], both, NT, preferred_element_type=jnp.float32)
        for part in range(2):
            columns = []
            for low in range(0, tb, lanes):
                score = scores[low : low + span, part * tb + low : part * tb + low + lanes]
                score = score - slopes[2 * pair + part] * dist[pl.ds(low, span), pl.ds(low, lanes)]
                expo = jnp.exp(score - jnp.max(score, axis=0, keepdims=True))
                weights = (expo * (1.0 / jnp.sum(expo, axis=0, keepdims=True))).astype(jnp.bfloat16)
                above, below = low, ext - span - low
                pieces = [weights]
                if above:
                    pieces = [jnp.zeros((above, lanes), jnp.bfloat16)] + pieces
                if below:
                    pieces = pieces + [jnp.zeros((below, lanes), jnp.bfloat16)]
                columns.append(jnp.concatenate(pieces, axis=0))
            weights = jnp.concatenate(columns, axis=1)
            head = pl.ds(pair * 128 + part * 64, 64)
            mixed[head, :] = jnp.dot(values[head, :], weights, preferred_element_type=jnp.float32).astype(jnp.bfloat16)
    summed = tok[0].astype(jnp.float32) + lax.dot_general(mixed[...], w_out[...], TN, preferred_element_type=jnp.float32)
    centred = summed - jnp.mean(summed, axis=1, keepdims=True)
    rstd = lax.rsqrt(jnp.mean(centred * centred, axis=1, keepdims=True) + 1e-05)
    unit = centred * rstd
    hidden_f = unit * gain[...].reshape(1, width)
    hidden[0] = hidden_f.astype(jnp.bfloat16)
    normed[0] = unit.astype(jnp.bfloat16)
    rstd_out[0] = jnp.broadcast_to(rstd, rstd_out.shape[1:])
    keep = start + lax.broadcasted_iota(jnp.int32, (tb, 1), 0) < length
    pool[0] = jnp.sum(jnp.where(keep, hidden_f, 0.0), axis=0, keepdims=True) / length.astype(jnp.float32)


def attend(first, before, lengths, tokens, left, right, qk, v_turned, w_qkv, w_v_turned, w_out, gain):
    docs, tb, width = tokens.shape
    ext = tb + 2 * WIN
    at = lambda *s: pl.BlockSpec((1,) + s, lambda i: (first + i, 0, 0))
    chunk = lambda *s: pl.BlockSpec((1,) + s, lambda i: (i, 0, 0))
    column = pl.BlockSpec((width, tb), lambda i: (0, first + i))
    fixed = lambda s, place=(0, 0): pl.BlockSpec(s, lambda i: place, pipeline_mode=pl.Buffered(1))
    out_shape = (bf16(docs, tb, width), bf16(width, docs * tb), bf16(docs, tb, width), f32(docs, tb, 128), f32(docs, 1, width))
    in_specs = [
        SMEM, at(tb, width), chunk(WIN, width), chunk(WIN, width), at(tb, 2 * width), column,
        fixed((width, width), (0, 1)), fixed((width, width)), fixed((width, width)), VMEM,
    ]
    operands = [lengths, tokens, left, right, qk, v_turned, w_qkv, w_v_turned, w_out, gain]
    aliases = {}
    if before is not None:
        aliases = {len(operands) + k: k for k in range(len(out_shape))}
        operands = operands + list(before)
        in_specs = in_specs + [ANY] * len(out_shape)
    return call(
        functools.partial(attend_kernel, first),
        out_shape,
        in_specs,
        (at(tb, width), column, at(tb, width), at(tb, 128), at(1, width)),
        limit=30,
        flops=CHUNK * 5 * 2 * tb * ext * width,
        moved=8 * 2**20,
        grid=(CHUNK,),
        scratch_shapes=[
            pltpu.VMEM((ext, width), jnp.bfloat16),
            pltpu.VMEM((width, ext), jnp.bfloat16),
            pltpu.VMEM((ext, tb), jnp.float32),
        ],
        input_output_aliases=aliases,
        name="attend",
    )(*operands)


def prepare_kernel(tok, w, qk, v_turned, w_v_turned):
    width = tok.shape[2]

    @pl.when(pl.program_id(0) == 0)
    def _():
        w_v_turned[...] = w[:, 2 * width :].T

    rows = tok[0]
    qk[0] = jnp.dot(rows, w[:, 0 : 2 * width], preferred_element_type=jnp.float32).astype(jnp.bfloat16)
    v_turned[...] = lax.dot_general(w_v_turned[...], rows, NT, preferred_element_type=jnp.float32).astype(jnp.bfloat16)


def prepare(tokens, w_qkv):
    docs, tb, width = tokens.shape
    return call(
        prepare_kernel,
        (bf16(docs, tb, 2 * width), bf16(width, docs * tb), bf16(width, width)),
        [
            pl.BlockSpec((1, tb, width), lambda i: (i, 0, 0)),
            pl.BlockSpec(w_qkv.shape, lambda i: (0, 0), pipeline_mode=pl.Buffered(1)),
        ],
        (
            pl.BlockSpec((1, tb, 2 * width), lambda i: (i, 0, 0)),
            pl.BlockSpec((width, tb), lambda i: (0, i)),
            pl.BlockSpec((width, width), lambda i: (0, 0)),
        ),
        flops=2 * docs * tb * width * 3 * width,
        moved=11 * 2**20,
        grid=(docs,),
        name="prepare",
    )(tokens, w_qkv)


def row_ids(k, rows, shape, dim):
    place = lax.broadcasted_iota(jnp.int32, shape, dim)
    dp, ctx = here()
    y, z_lo = (dp + k) & 3, dp >> 2
    other = (place >= rows).astype(jnp.int32)
    owner = (z_lo + other - 2 * z_lo * other) * 4 + y
    return (owner * 16 + ctx) * rows + place - other * rows


def stack_kernel(*refs):
    low = 0
    for ref in refs[:-1]:
        refs[-1][low : low + ref.shape[0], :] = ref[...]
        low += ref.shape[0]


def add_kernel(*refs):
    terms = [ref[...] for ref in refs[:-1]]
    if len(terms) == 4:
        terms = [terms[0] + terms[2], terms[1] + terms[3]]
    refs[-1][...] = terms[0] + terms[1]


def add(terms):
    return call(add_kernel, f32(*terms[0].shape), [VMEM] * len(terms), VMEM, limit=4, name="add")(*terms)


def merge_kernel(docs, width, *refs):
    refs[-1][...] = merge(docs, width, [ref[...] for ref in refs[:-1]])


def merged(docs, width, states):
    kernel = functools.partial(merge_kernel, docs, width)
    return call(kernel, f32(*states[0].shape), [VMEM] * len(states), VMEM, limit=4, name="merge")(*states)


def target_kernel(docs, positive, *refs):
    pieces, out = refs[:4], refs[4]
    total = jnp.zeros(out.shape, jnp.float32)
    for k, piece in enumerate(pieces):
        rows = piece.shape[0]
        ids = row_ids(k, rows // 2, (8, rows), 1)
        doc = lax.broadcasted_iota(jnp.int32, (8, rows), 0)
        wanted = jnp.full((8, rows), -1, jnp.int32)
        for d in range(docs):
            wanted = jnp.where(doc == d, positive[lax.axis_index("dp") * docs + d], wanted)
        hit = (ids == wanted).astype(jnp.float32).astype(jnp.bfloat16)
        total = total + jnp.dot(hit, piece[...], preferred_element_type=jnp.float32)[0:docs]
    out[...] = total


def turn_kernel(mixed, out):
    width = out.shape[0]
    place = lax.broadcasted_iota(jnp.int32, (width, 1), 0)
    dp, ctx = here()
    each = width // 128
    core = (ctx & 1) ^ (place // (64 * each))
    first, second = place // (16 * each) % 4, place // (4 * each) % 4
    y = ((dp & 3) + jnp.where(core == 0, first, second)) & 3
    x = ((ctx >> 2) + jnp.where(core == 0, second, first)) & 3
    z = ((ctx & 2) + (dp >> 2) + place // each % 4) & 3
    block = ((z & 1) * 4 + y) * 16 + x * 4 + (z >> 1) * 2 + core
    chosen = block * each + place % each == lax.broadcasted_iota(jnp.int32, (width, width), 1)
    chosen = jnp.where(chosen, 1.0, 0.0).astype(jnp.bfloat16)
    out[...] = jnp.dot(chosen, mixed[...], preferred_element_type=jnp.float32).astype(jnp.bfloat16)


def norm_kernel(s0, s1, s2, s3, emb_out, rinv_out, target_out):
    docs = target_out.shape[0]
    own, other = s0[...] + s2[...], s1[0:docs] + s3[0:docs]
    pooled = jnp.concatenate([own[0:docs], other], axis=0)
    rinv = lax.rsqrt(jnp.sum(pooled * pooled, axis=1, keepdims=True) + 1e-06)
    emb_out[...] = pooled * rinv
    rinv_out[...] = jnp.broadcast_to(rinv, rinv_out.shape)
    target_out[...] = own[docs:]


def as_row(column):
    size = column.shape[0]
    same = lax.broadcasted_iota(jnp.int32, (size, size), 0) == lax.broadcasted_iota(jnp.int32, (size, size), 1)
    return jnp.sum(jnp.where(same, column, 0.0), axis=0, keepdims=True)


def score_kernel(docs, positive, e0, e1, e2, e3, t0, t1, t2, t3, everyone, state, expos):
    all_docs, width = everyone.shape
    dp, _ = here()
    y, z_lo = dp & 3, dp >> 2
    for k, piece in enumerate((e0, e1, e2, e3)):
        value = piece[...]
        turned = jnp.concatenate([value[docs:], value[0:docs]], axis=0)
        place = pl.multiple_of(((y + k) & 3) * 2 * docs, 2 * docs)
        everyone[pl.ds(place, 2 * docs), :] = jnp.where(z_lo == 1, turned, value)
    tables = (t0, t1, t2, t3)
    rows = t0.shape[0]
    emb = thirds(everyone[...])
    scores = [folded(lax.dot_general(emb, t[...], NT, preferred_element_type=jnp.float32)) / TAU for t in tables]
    tops = [jnp.max(s, axis=1, keepdims=True) for s in scores]
    top = jnp.maximum(jnp.maximum(tops[0], tops[2]), jnp.maximum(tops[1], tops[3]))
    row = lax.broadcasted_iota(jnp.int32, (all_docs, 128), 0)
    wanted = jnp.zeros((all_docs, 128), jnp.int32)
    for doc in range(all_docs):
        z, rest = divmod(doc, all_docs // 2)
        wanted = jnp.where(row == rest // docs * 2 * docs + z * docs + rest % docs, positive[doc], wanted)
    totals, found = [], jnp.zeros((all_docs, 1), jnp.float32)
    for k, s in enumerate(scores):
        expo = jnp.exp(s - top)
        expos[:, k * rows : (k + 1) * rows] = expo
        halves = [jnp.sum(expo[:, h : h + rows // 2], axis=1, keepdims=True) for h in (0, rows // 2)]
        totals.append(halves[0] + halves[1])
        hit = row_ids(k, rows // 2, (all_docs, rows), 1) == wanted[:, 0:1]
        found = found + jnp.sum(jnp.where(hit, s, 0.0), axis=1, keepdims=True)
    total = (totals[0] + totals[2]) + (totals[1] + totals[3])
    place = pl.multiple_of(y * 2 * docs, 2 * docs)
    mine = thirds(expos[pl.ds(place, 2 * docs), :])
    mix = jnp.zeros((2 * docs, width), jnp.float32)
    for k, t in enumerate(tables):
        mix = mix + folded(jnp.dot(mine[:, k * rows : (k + 1) * rows], t[...], preferred_element_type=jnp.float32))
    column = lax.broadcasted_iota(jnp.int32, (docs, all_docs), 1)
    own = column == lax.broadcasted_iota(jnp.int32, (docs, all_docs), 0) + y * 2 * docs + z_lo * docs
    total_row, top_row, found_row = as_row(total), as_row(top), as_row(found)
    state[...] = jnp.zeros_like(state)
    state[0:docs, 0:width] = jnp.where(z_lo == 1, mix[docs:], mix[0:docs])
    for place, row in ((width, total_row), (width + 128, top_row)):
        value = jnp.sum(jnp.where(own, row, 0.0), axis=1, keepdims=True)
        state[0:docs, place : place + 128] = jnp.broadcast_to(value, (docs, 128))
    for index, row in enumerate((total_row, top_row, found_row)):
        state[docs + index : docs + index + 1, 0:all_docs] = row


def merge(docs, width, states):
    row = lax.broadcasted_iota(jnp.int32, states[0].shape, 0)
    column = lax.broadcasted_iota(jnp.int32, states[0].shape, 1)
    place = width + 128
    by_row = [s[:, place : place + 1] for s in states]
    by_lane = [s[docs + 1 : docs + 2, :] for s in states]
    top_row = functools.reduce(jnp.maximum, by_row)
    top_lane = functools.reduce(jnp.maximum, by_lane)
    terms = [
        s * jnp.exp(jnp.where(row == docs, b - top_lane, a - top_row)) for s, a, b in zip(states, by_row, by_lane)
    ]
    if len(terms) == 4:
        terms = [terms[0] + terms[2], terms[1] + terms[3]]
    joined = jnp.where((row < docs) & (column >= place), top_row, terms[0] + terms[1])
    return jnp.where(row == docs + 1, top_lane, joined)


def batch_kernel(docs, emb, everyone, product_out, stats):
    everything = everyone[...]
    all_docs = everything.shape[0]
    own = lax.dot_general(emb[...], everything, NT, precision=HIGHEST, preferred_element_type=jnp.float32) / TAU
    product = lax.dot_general(everything, everything, NT, precision=HIGHEST, preferred_element_type=jnp.float32) / TAU
    wide = (all_docs, all_docs)
    same = lax.broadcasted_iota(jnp.int32, wide, 0) == lax.broadcasted_iota(jnp.int32, wide, 1)
    product = jnp.where(same, -1e30, product)
    top = jnp.max(product, axis=0, keepdims=True)
    total = jnp.sum(jnp.exp(product - top), axis=0, keepdims=True)
    product_out[...] = own
    stats[...] = jnp.concatenate([top, total] * 4, axis=0)


def grad_kernel(
    lengths, state, other, emb, rinv, everyone, target, product, stats, gain, normed, rstd, turned,
    keep_out, send_out, loss_out, d_summed,
):
    docs, width = target.shape
    all_docs = everyone.shape[0]
    dp, _ = here()
    y, z_lo = dp & 3, dp >> 2
    own, others = emb[0:docs], everyone[...]
    now = merge(docs, width, [state[...], other[...]])
    total, top, found = (now[docs + k : docs + k + 1, 0:all_docs] for k in range(3))
    batch_top, batch_total = stats[0:1], stats[1:2]
    peak = jnp.maximum(top, batch_top)
    lse_row = peak + jnp.log(total * jnp.exp(top - peak) + batch_total * jnp.exp(batch_top - peak))
    loss_out[...] = jnp.broadcast_to(jnp.sum(lse_row - found, axis=1, keepdims=True) / all_docs, loss_out.shape)
    column = lax.broadcasted_iota(jnp.int32, (docs, all_docs), 1)
    same = column == lax.broadcasted_iota(jnp.int32, (docs, all_docs), 0) + y * 2 * docs + z_lo * docs
    lse = jnp.sum(jnp.where(same, lse_row, 0.0), axis=1, keepdims=True)
    scores = product[0:docs]
    g_batch = jnp.where(same, 0.0, jnp.exp(scores - lse) + jnp.exp(scores - lse_row)) / all_docs
    mix = now[0:docs, 0:width] * jnp.exp(now[0:docs, width + 128 : width + 129] - lse)
    from_batch = jnp.dot(g_batch, others, precision=HIGHEST, preferred_element_type=jnp.float32)
    d_emb = ((mix - target[...]) / all_docs + from_batch) / TAU
    d_pooled = (d_emb - own * jnp.sum(own * d_emb, axis=1, keepdims=True)) * rinv[0:docs, 0:1]
    tb = normed.shape[1]
    for doc in range(docs):
        dy = d_pooled[doc : doc + 1] / lengths[doc].astype(jnp.float32) * gain[...].reshape(1, width)
        level = dy - jnp.mean(dy, axis=1, keepdims=True)
        unit = normed[doc].astype(jnp.float32)
        along = jnp.mean(unit * dy, axis=1, keepdims=True)
        keep = lax.axis_index("ctx") * tb + lax.broadcasted_iota(jnp.int32, (tb, 1), 0) < lengths[doc]
        scale = jnp.where(keep, rstd[doc, :, 0:1], 0.0)
        d_summed[doc * tb : (doc + 1) * tb, :] = (scale * (level - unit * along)).astype(jnp.bfloat16)
    half = width // 2
    send_out[...] = jnp.dot(turned[half:], d_summed[...], preferred_element_type=jnp.float32)
    keep_out[...] = jnp.dot(turned[0:half], d_summed[...], preferred_element_type=jnp.float32)


def sum_kernel(count, *refs):
    terms, outs = refs[:count], refs[count:]
    total = terms[0][...].astype(jnp.float32)
    for term in terms[1:]:
        total = total + term[...].astype(jnp.float32)
    rows = outs[0].shape[0]
    for index, out in enumerate(outs):
        out[...] = total[index * rows : (index + 1) * rows].astype(out.dtype)


def sum_and_split(terms, kind):
    rows, width = terms[0].shape
    piece = (rows // 4, width)
    shapes = (f32(*piece),) + (jax.ShapeDtypeStruct(piece, kind),) * 3
    return call(
        functools.partial(sum_kernel, len(terms)), shapes, [VMEM] * len(terms), (VMEM,) * 4, limit=8, name="sum_split"
    )(*terms)


def shards(tokens, w_qkv, w_out, ln_gain, cache, positive, lengths):
    docs, tb, width = tokens.shape
    n_ctx, n_dp = lax.axis_size("ctx"), lax.axis_size("dp")
    all_docs = n_dp * docs
    swapped = swap(cache, "dp", 4)
    halos = []
    for first in range(0, docs, CHUNK):
        part = tokens[first : first + CHUNK]
        left = lax.ppermute(part, "ctx", [(i, (i + 1) % n_ctx) for i in range(n_ctx)])
        right = lax.ppermute(part, "ctx", [((i + 1) % n_ctx, i) for i in range(n_ctx)])
        halos.append((left, right))
    gain = ln_gain
    qk, v_turned, w_v_turned = prepare(in_hbm(tokens), in_hbm(w_qkv))
    swapped, w_v_turned = lax.optimization_barrier((swapped, w_v_turned))
    rows = cache.shape[0]
    table = call(stack_kernel, bf16(2 * rows, width), [VMEM, VMEM], VMEM, limit=4, name="stack")(cache, swapped)
    tables = around(table, from_y)
    done = None
    for index, (left, right) in enumerate(halos):
        if index == 1:
            *done, pool = done
            pool, after = lax.optimization_barrier((pool, positive))
            done = [*done, pool]
            target = call(
                functools.partial(target_kernel, docs), f32(docs, width), [SMEM] + [VMEM] * 4, VMEM, name="target"
            )(after, *tables)
        done = attend(
            index * CHUNK, done, lengths, tokens, left, right, qk, v_turned, w_qkv, w_v_turned, w_out, gain
        )
    hidden, mixed, normed, rstd, pool = done

    turned = call(
        turn_kernel,
        bf16(width, docs * tb),
        [VMEM],
        VMEM,
        flops=2 * docs * tb * width * width,
        moved=4 * 2**20,
        name="turn",
    )(mixed)

    sums = call(stack_kernel, f32(2 * docs, width), [VMEM, VMEM], VMEM, limit=4, name="stack")(
        pool.reshape(docs, width), target
    )
    sums = add([sums, swap(sums, "ctx", 1)])
    sums = add(around(sums, from_x))
    emb, rinv, target = call(
        norm_kernel,
        (f32(2 * docs, width), f32(2 * docs, 128), f32(docs, width)),
        [VMEM] * 4,
        (VMEM,) * 3,
        limit=4,
        name="norm",
    )(*around(sums, from_z))
    embs = around(emb, from_y)
    everyone, state = call(
        functools.partial(score_kernel, docs),
        (f32(all_docs, width), f32(2 * docs, width + 256)),
        [SMEM] + [VMEM] * 8,
        (VMEM, VMEM),
        moved=2 * 2**20,
        scratch_shapes=[pltpu.VMEM((all_docs, n_dp * cache.shape[0]), jnp.float32)],
        name="score",
    )(positive, *embs, *tables)
    product, stats = call(
        functools.partial(batch_kernel, docs),
        (f32(2 * docs, all_docs), f32(8, all_docs)),
        [VMEM, VMEM],
        (VMEM, VMEM),
        limit=4,
        name="batch",
    )(emb, everyone)
    state = merged(docs, width, [state, swap(state, "ctx", 1)])
    state = merged(docs, width, around(state, from_x))
    half = width // 2
    keep, send, loss = call(
        grad_kernel,
        (f32(half, width), f32(half, width), f32(8, 128)),
        [SMEM] + [VMEM] * 12,
        (VMEM,) * 3,
        flops=2 * docs * tb * width * width,
        moved=8 * 2**20,
        scratch_shapes=[pltpu.VMEM((docs * tb, width), jnp.bfloat16)],
        name="grad",
    )(
        lengths, state, swap(state, "ctx", 2), emb, rinv, everyone, target, product, stats, gain, normed, rstd, turned,
    )
    keep, *sends = sum_and_split([keep, swap(send, "ctx", 1)], jnp.bfloat16)
    got = [from_plane(piece, -(k + 1), False) for k, piece in enumerate(sends)]
    keep, *sends = sum_and_split([keep] + got, jnp.float32)
    got = [from_plane(piece, -(k + 1), True) for k, piece in enumerate(sends)]
    keep, *sends = sum_and_split([keep] + got, jnp.float32)
    got = [from_z(piece, -(k + 1)) for k, piece in enumerate(sends)]
    return (hidden, loss[0, 0], add([keep] + got))


def solution(mesh):
    placed = (P("dp", "ctx", None), P(), P(), P(), P(("dp", "ctx"), None), P(), P("dp"))
    return jax.shard_map(
        shards,
        mesh=mesh,
        in_specs=placed,
        out_specs=(P("dp", "ctx", None), P(), P(("dp", "ctx"), None)),
        check_vma=False,
    )
```

```python
import functools
import math

import jax
import jax.numpy as jnp
from jax import lax
from jax.experimental import pallas as pl
from jax.experimental.pallas import tpu as pltpu
from jax.sharding import PartitionSpec as P

H = 12
WIN = 256
TAU = 0.02
FAR = 1e32
CHUNK = 2
NT = (((1,), (1,)), ((), ()))
TN = (((0,), (0,)), ((), ()))
HIGHEST = lax.Precision.HIGHEST
VMEM = pl.BlockSpec(memory_space=pltpu.VMEM)
SMEM = pl.BlockSpec(memory_space=pltpu.SMEM)
ANY = pl.BlockSpec(memory_space=pl.ANY)


def swap(value, axis, bits):
    return lax.ppermute(value, axis, [(i, i ^ bits) for i in range(lax.axis_size(axis))])


def from_x(value, k):
    size = lax.axis_size("ctx")
    return lax.ppermute(value, "ctx", [((c + 4 * k) % size, c) for c in range(size)])


def from_y(value, k):
    return lax.ppermute(value, "dp", [((d & 4) | ((d + k) & 3), d) for d in range(lax.axis_size("dp"))])


def from_z(value, k):
    n_dp, n_ctx = lax.axis_size("dp"), lax.axis_size("ctx")
    pairs = []
    for d in range(n_dp):
        for c in range(n_ctx):
            z = ((c & 2) + (d >> 2) + k) & 3
            pairs.append((((z & 1) * 4 + (d & 3)) * n_ctx + (c & ~2) + (z & 2), d * n_ctx + c))
    return lax.ppermute(value, ("dp", "ctx"), pairs)


def from_plane(value, k, last):
    n_dp, n_ctx = lax.axis_size("dp"), lax.axis_size("ctx")
    pairs = []
    for d in range(n_dp):
        for c in range(n_ctx):
            along_y = (c & 1 == 1) == last
            source = ((d & 4) | ((d + k) & 3), c) if along_y else (d, (c + 4 * k) % n_ctx)
            pairs.append((source[0] * n_ctx + source[1], d * n_ctx + c))
    return lax.ppermute(value, ("dp", "ctx"), pairs)


def around(value, fetch):
    return [value] + [fetch(value, k) for k in (1, 2, 3)]


def here():
    return lax.axis_index("dp"), lax.axis_index("ctx")


def in_hbm(value):
    return pltpu.with_memory_space_constraint(value, pltpu.HBM)


def call(kernel, out_shape, in_specs, out_specs, limit=16, flops=0, moved=0, **keywords):
    return pl.pallas_call(
        kernel,
        out_shape=out_shape,
        in_specs=in_specs,
        out_specs=out_specs,
        compiler_params=pltpu.CompilerParams(vmem_limit_bytes=limit * 2**20),
        cost_estimate=pl.CostEstimate(flops=flops, bytes_accessed=moved, transcendentals=0),
        **keywords,
    )


def f32(*shape):
    return jax.ShapeDtypeStruct(shape, jnp.float32)


def bf16(*shape):
    return jax.ShapeDtypeStruct(shape, jnp.bfloat16)


def slopes_of(heads):
    largest = 2 ** int(math.floor(math.log2(heads)))
    listed = [2.0 ** (-8.0 * (h + 1) / largest) for h in range(largest)]
    return listed + [2.0 ** (-4.0 * (2 * m + 1) / largest) for m in range(heads - largest)]


def thirds(value):
    high = value.astype(jnp.bfloat16)
    rest = value - high.astype(jnp.float32)
    middle = rest.astype(jnp.bfloat16)
    low = (rest - middle.astype(jnp.float32)).astype(jnp.bfloat16)
    parts = [p.astype(jnp.float32) for p in (high, middle, low)]
    return jnp.concatenate(parts, axis=0).astype(jnp.bfloat16)


def folded(products):
    rows = products.shape[0] // 3
    return products[0:rows] + products[rows : 2 * rows] + products[2 * rows :]


def attend_kernel(
    first, lengths, tok, left, right, qk, v_turned, w_k, w_v_turned, w_out, gain, *refs
):
    hidden, mixed, normed, rstd_out, pool, keys, values, dist = refs[-8:]
    tb, width = tok.shape[1:]
    ext = tb + 2 * WIN
    start, length = lax.axis_index("ctx") * tb, lengths[first + pl.program_id(0)]
    rows = jnp.concatenate([left[0], right[0]], axis=0)
    new = jnp.dot(rows, w_k[...], preferred_element_type=jnp.float32).astype(jnp.bfloat16)
    keys[0:WIN] = new[0:WIN]
    keys[WIN : WIN + tb] = qk[0, :, width:]
    keys[WIN + tb :] = new[WIN:]
    new = lax.dot_general(w_v_turned[...], rows, NT, preferred_element_type=jnp.float32).astype(jnp.bfloat16)
    values[:, 0:WIN] = new[:, 0:WIN]
    values[:, WIN : WIN + tb] = v_turned[...]
    values[:, WIN + tb :] = new[:, WIN:]
    j = lax.broadcasted_iota(jnp.int32, (ext, tb), 0) - WIN
    away = jnp.abs(lax.broadcasted_iota(jnp.int32, (ext, tb), 1) - j)
    kpos = start + j
    seen = (away <= WIN) & (((kpos >= 0) & (kpos < length)) | (away == 0))
    dist[...] = jnp.where(seen, away.astype(jnp.float32), FAR)
    half = lax.broadcasted_iota(jnp.int32, (tb, 128), 1) < 64
    slopes = slopes_of(H)
    lanes = 128
    span = lanes + 2 * WIN
    for pair in range(H // 2):
        cols = pl.ds(pair * 128, 128)
        query = qk[0, :, cols] * jnp.bfloat16(0.125)
        zero = jnp.bfloat16(0)
        both = jnp.concatenate([jnp.where(half, query, zero), jnp.where(half, zero, query)], axis=0)
        scores = lax.dot_general(keys[:, cols], both, NT, preferred_element_type=jnp.float32)
        for part in range(2):
            columns = []
            for low in range(0, tb, lanes):
                score = scores[low : low + span, part * tb + low : part * tb + low + lanes]
                score = score - slopes[2 * pair + part] * dist[pl.ds(low, span), pl.ds(low, lanes)]
                expo = jnp.exp(score - jnp.max(score, axis=0, keepdims=True))
                weights = (expo * (1.0 / jnp.sum(expo, axis=0, keepdims=True))).astype(jnp.bfloat16)
                above, below = low, ext - span - low
                pieces = [weights]
                if above:
                    pieces = [jnp.zeros((above, lanes), jnp.bfloat16)] + pieces
                if below:
                    pieces = pieces + [jnp.zeros((below, lanes), jnp.bfloat16)]
                columns.append(jnp.concatenate(pieces, axis=0))
            weights = jnp.concatenate(columns, axis=1)
            head = pl.ds(pair * 128 + part * 64, 64)
            mixed[head, :] = jnp.dot(values[head, :], weights, preferred_element_type=jnp.float32).astype(jnp.bfloat16)
    summed = tok[0].astype(jnp.float32) + lax.dot_general(mixed[...], w_out[...], TN, preferred_element_type=jnp.float32)
    centred = summed - jnp.mean(summed, axis=1, keepdims=True)
    rstd = lax.rsqrt(jnp.mean(centred * centred, axis=1, keepdims=True) + 1e-05)
    unit = centred * rstd
    hidden_f = unit * gain[...].reshape(1, width)
    hidden[0] = hidden_f.astype(jnp.bfloat16)
    normed[0] = unit.astype(jnp.bfloat16)
    rstd_out[0] = jnp.broadcast_to(rstd, rstd_out.shape[1:])
    keep = start + lax.broadcasted_iota(jnp.int32, (tb, 1), 0) < length
    pool[0] = jnp.sum(jnp.where(keep, hidden_f, 0.0), axis=0, keepdims=True) / length.astype(jnp.float32)


def attend(first, before, lengths, tokens, left, right, qk, v_turned, w_qkv, w_v_turned, w_out, gain):
    docs, tb, width = tokens.shape
    ext = tb + 2 * WIN
    at = lambda *s: pl.BlockSpec((1,) + s, lambda i: (first + i, 0, 0))
    chunk = lambda *s: pl.BlockSpec((1,) + s, lambda i: (i, 0, 0))
    column = pl.BlockSpec((width, tb), lambda i: (0, first + i))
    fixed = lambda s, place=(0, 0): pl.BlockSpec(s, lambda i: place, pipeline_mode=pl.Buffered(1))
    out_shape = (bf16(docs, tb, width), bf16(width, docs * tb), bf16(docs, tb, width), f32(docs, tb, 128), f32(docs, 1, width))
    in_specs = [
        SMEM, at(tb, width), chunk(WIN, width), chunk(WIN, width), at(tb, 2 * width), column,
        fixed((width, width), (0, 1)), fixed((width, width)), fixed((width, width)), VMEM,
    ]
    operands = [lengths, tokens, left, right, qk, v_turned, w_qkv, w_v_turned, w_out, gain]
    aliases = {}
    if before is not None:
        aliases = {len(operands) + k: k for k in range(len(out_shape))}
        operands = operands + list(before)
        in_specs = in_specs + [ANY] * len(out_shape)
    return call(
        functools.partial(attend_kernel, first),
        out_shape,
        in_specs,
        (at(tb, width), column, at(tb, width), at(tb, 128), at(1, width)),
        limit=30,
        flops=CHUNK * 5 * 2 * tb * ext * width,
        moved=8 * 2**20,
        grid=(CHUNK,),
        scratch_shapes=[
            pltpu.VMEM((ext, width), jnp.bfloat16),
            pltpu.VMEM((width, ext), jnp.bfloat16),
            pltpu.VMEM((ext, tb), jnp.float32),
        ],
        input_output_aliases=aliases,
        name="attend",
    )(*operands)


def prepare_kernel(tok, w, qk, v_turned, w_v_turned, late):
    width = tok.shape[2]
    late[...] = tok[...]

    @pl.when(pl.program_id(0) == 0)
    def _():
        w_v_turned[...] = w[:, 2 * width :].T

    rows = tok[0]
    qk[0] = jnp.dot(rows, w[:, 0 : 2 * width], preferred_element_type=jnp.float32).astype(jnp.bfloat16)
    v_turned[...] = lax.dot_general(w_v_turned[...], rows, NT, preferred_element_type=jnp.float32).astype(jnp.bfloat16)


def prepare(tokens, w_qkv):
    docs, tb, width = tokens.shape
    return call(
        prepare_kernel,
        (bf16(docs, tb, 2 * width), bf16(width, docs * tb), bf16(width, width), bf16(docs - CHUNK, tb, width)),
        [
            pl.BlockSpec((1, tb, width), lambda i: (i, 0, 0)),
            pl.BlockSpec(w_qkv.shape, lambda i: (0, 0), pipeline_mode=pl.Buffered(1)),
        ],
        (
            pl.BlockSpec((1, tb, 2 * width), lambda i: (i, 0, 0)),
            pl.BlockSpec((width, tb), lambda i: (0, i)),
            pl.BlockSpec((width, width), lambda i: (0, 0)),
            pl.BlockSpec((1, tb, width), lambda i: (jnp.maximum(i - CHUNK, 0), 0, 0)),
        ),
        flops=2 * docs * tb * width * 3 * width,
        moved=11 * 2**20,
        grid=(docs,),
        name="prepare",
    )(tokens, w_qkv)


def row_ids(k, rows, shape, dim):
    place = lax.broadcasted_iota(jnp.int32, shape, dim)
    dp, ctx = here()
    y, z_lo = (dp + k) & 3, dp >> 2
    other = (place >= rows).astype(jnp.int32)
    owner = (z_lo + other - 2 * z_lo * other) * 4 + y
    return (owner * 16 + ctx) * rows + place - other * rows


def stack_kernel(*refs):
    low = 0
    for ref in refs[:-1]:
        refs[-1][low : low + ref.shape[0], :] = ref[...]
        low += ref.shape[0]


def add_kernel(*refs):
    terms = [ref[...] for ref in refs[:-1]]
    if len(terms) == 4:
        terms = [terms[0] + terms[2], terms[1] + terms[3]]
    refs[-1][...] = terms[0] + terms[1]


def add(terms):
    return call(add_kernel, f32(*terms[0].shape), [VMEM] * len(terms), VMEM, limit=4, name="add")(*terms)


def merge_kernel(docs, width, *refs):
    refs[-1][...] = merge(docs, width, [ref[...] for ref in refs[:-1]])


def merged(docs, width, states):
    kernel = functools.partial(merge_kernel, docs, width)
    return call(kernel, f32(*states[0].shape), [VMEM] * len(states), VMEM, limit=4, name="merge")(*states)


def target_kernel(docs, positive, *refs):
    pieces, out = refs[:4], refs[4]
    total = jnp.zeros(out.shape, jnp.float32)
    for k, piece in enumerate(pieces):
        rows = piece.shape[0]
        ids = row_ids(k, rows // 2, (8, rows), 1)
        doc = lax.broadcasted_iota(jnp.int32, (8, rows), 0)
        wanted = jnp.full((8, rows), -1, jnp.int32)
        for d in range(docs):
            wanted = jnp.where(doc == d, positive[lax.axis_index("dp") * docs + d], wanted)
        hit = (ids == wanted).astype(jnp.float32).astype(jnp.bfloat16)
        total = total + jnp.dot(hit, piece[...], preferred_element_type=jnp.float32)[0:docs]
    out[...] = total


def turn_kernel(mixed, out):
    width = out.shape[0]
    place = lax.broadcasted_iota(jnp.int32, (width, 1), 0)
    dp, ctx = here()
    each = width // 128
    core = (ctx & 1) ^ (place // (64 * each))
    first, second = place // (16 * each) % 4, place // (4 * each) % 4
    y = ((dp & 3) + jnp.where(core == 0, first, second)) & 3
    x = ((ctx >> 2) + jnp.where(core == 0, second, first)) & 3
    z = ((ctx & 2) + (dp >> 2) + place // each % 4) & 3
    block = ((z & 1) * 4 + y) * 16 + x * 4 + (z >> 1) * 2 + core
    chosen = block * each + place % each == lax.broadcasted_iota(jnp.int32, (width, width), 1)
    chosen = jnp.where(chosen, 1.0, 0.0).astype(jnp.bfloat16)
    out[...] = jnp.dot(chosen, mixed[...], preferred_element_type=jnp.float32).astype(jnp.bfloat16)


def norm_kernel(s0, s1, s2, s3, emb_out, rinv_out, target_out):
    docs = target_out.shape[0]
    own, other = s0[...] + s2[...], s1[0:docs] + s3[0:docs]
    pooled = jnp.concatenate([own[0:docs], other], axis=0)
    rinv = lax.rsqrt(jnp.sum(pooled * pooled, axis=1, keepdims=True) + 1e-06)
    emb_out[...] = pooled * rinv
    rinv_out[...] = jnp.broadcast_to(rinv, rinv_out.shape)
    target_out[...] = own[docs:]


def as_row(column):
    size = column.shape[0]
    same = lax.broadcasted_iota(jnp.int32, (size, size), 0) == lax.broadcasted_iota(jnp.int32, (size, size), 1)
    return jnp.sum(jnp.where(same, column, 0.0), axis=0, keepdims=True)


def score_kernel(docs, positive, e0, e1, e2, e3, t0, t1, t2, t3, everyone, state, expos):
    all_docs, width = everyone.shape
    dp, _ = here()
    y, z_lo = dp & 3, dp >> 2
    for k, piece in enumerate((e0, e1, e2, e3)):
        value = piece[...]
        turned = jnp.concatenate([value[docs:], value[0:docs]], axis=0)
        place = pl.multiple_of(((y + k) & 3) * 2 * docs, 2 * docs)
        everyone[pl.ds(place, 2 * docs), :] = jnp.where(z_lo == 1, turned, value)
    tables = (t0, t1, t2, t3)
    rows = t0.shape[0]
    emb = thirds(everyone[...])
    scores = [folded(lax.dot_general(emb, t[...], NT, preferred_element_type=jnp.float32)) / TAU for t in tables]
    tops = [jnp.max(s, axis=1, keepdims=True) for s in scores]
    top = jnp.maximum(jnp.maximum(tops[0], tops[2]), jnp.maximum(tops[1], tops[3]))
    row = lax.broadcasted_iota(jnp.int32, (all_docs, 128), 0)
    wanted = jnp.zeros((all_docs, 128), jnp.int32)
    for doc in range(all_docs):
        z, rest = divmod(doc, all_docs // 2)
        wanted = jnp.where(row == rest // docs * 2 * docs + z * docs + rest % docs, positive[doc], wanted)
    totals, found = [], jnp.zeros((all_docs, 1), jnp.float32)
    for k, s in enumerate(scores):
        expo = jnp.exp(s - top)
        expos[:, k * rows : (k + 1) * rows] = expo
        halves = [jnp.sum(expo[:, h : h + rows // 2], axis=1, keepdims=True) for h in (0, rows // 2)]
        totals.append(halves[0] + halves[1])
        hit = row_ids(k, rows // 2, (all_docs, rows), 1) == wanted[:, 0:1]
        found = found + jnp.sum(jnp.where(hit, s, 0.0), axis=1, keepdims=True)
    total = (totals[0] + totals[2]) + (totals[1] + totals[3])
    place = pl.multiple_of(y * 2 * docs, 2 * docs)
    mine = thirds(expos[pl.ds(place, 2 * docs), :])
    mix = jnp.zeros((2 * docs, width), jnp.float32)
    for k, t in enumerate(tables):
        mix = mix + folded(jnp.dot(mine[:, k * rows : (k + 1) * rows], t[...], preferred_element_type=jnp.float32))
    column = lax.broadcasted_iota(jnp.int32, (docs, all_docs), 1)
    own = column == lax.broadcasted_iota(jnp.int32, (docs, all_docs), 0) + y * 2 * docs + z_lo * docs
    total_row, top_row, found_row = as_row(total), as_row(top), as_row(found)
    state[...] = jnp.zeros_like(state)
    state[0:docs, 0:width] = jnp.where(z_lo == 1, mix[docs:], mix[0:docs])
    for place, row in ((width, total_row), (width + 128, top_row)):
        value = jnp.sum(jnp.where(own, row, 0.0), axis=1, keepdims=True)
        state[0:docs, place : place + 128] = jnp.broadcast_to(value, (docs, 128))
    for index, row in enumerate((total_row, top_row, found_row)):
        state[docs + index : docs + index + 1, 0:all_docs] = row


def merge(docs, width, states):
    row = lax.broadcasted_iota(jnp.int32, states[0].shape, 0)
    column = lax.broadcasted_iota(jnp.int32, states[0].shape, 1)
    place = width + 128
    by_row = [s[:, place : place + 1] for s in states]
    by_lane = [s[docs + 1 : docs + 2, :] for s in states]
    top_row = functools.reduce(jnp.maximum, by_row)
    top_lane = functools.reduce(jnp.maximum, by_lane)
    terms = [
        s * jnp.exp(jnp.where(row == docs, b - top_lane, a - top_row)) for s, a, b in zip(states, by_row, by_lane)
    ]
    if len(terms) == 4:
        terms = [terms[0] + terms[2], terms[1] + terms[3]]
    joined = jnp.where((row < docs) & (column >= place), top_row, terms[0] + terms[1])
    return jnp.where(row == docs + 1, top_lane, joined)


def batch_kernel(docs, emb, everyone, product_out, stats):
    everything = everyone[...]
    all_docs = everything.shape[0]
    own = lax.dot_general(emb[...], everything, NT, precision=HIGHEST, preferred_element_type=jnp.float32) / TAU
    product = lax.dot_general(everything, everything, NT, precision=HIGHEST, preferred_element_type=jnp.float32) / TAU
    wide = (all_docs, all_docs)
    same = lax.broadcasted_iota(jnp.int32, wide, 0) == lax.broadcasted_iota(jnp.int32, wide, 1)
    product = jnp.where(same, -1e30, product)
    top = jnp.max(product, axis=0, keepdims=True)
    total = jnp.sum(jnp.exp(product - top), axis=0, keepdims=True)
    product_out[...] = own
    stats[...] = jnp.concatenate([top, total] * 4, axis=0)


def grad_kernel(
    lengths, state, other, emb, rinv, everyone, target, product, stats, gain, normed, rstd, turned,
    send_out, d_summed, loss_out,
):
    docs, width = target.shape
    all_docs = everyone.shape[0]
    dp, _ = here()
    y, z_lo = dp & 3, dp >> 2
    own, others = emb[0:docs], everyone[...]
    now = merge(docs, width, [state[...], other[...]])
    total, top, found = (now[docs + k : docs + k + 1, 0:all_docs] for k in range(3))
    batch_top, batch_total = stats[0:1], stats[1:2]
    peak = jnp.maximum(top, batch_top)
    lse_row = peak + jnp.log(total * jnp.exp(top - peak) + batch_total * jnp.exp(batch_top - peak))
    loss_out[...] = jnp.broadcast_to(jnp.sum(lse_row - found, axis=1, keepdims=True) / all_docs, loss_out.shape)
    column = lax.broadcasted_iota(jnp.int32, (docs, all_docs), 1)
    same = column == lax.broadcasted_iota(jnp.int32, (docs, all_docs), 0) + y * 2 * docs + z_lo * docs
    lse = jnp.sum(jnp.where(same, lse_row, 0.0), axis=1, keepdims=True)
    scores = product[0:docs]
    g_batch = jnp.where(same, 0.0, jnp.exp(scores - lse) + jnp.exp(scores - lse_row)) / all_docs
    mix = now[0:docs, 0:width] * jnp.exp(now[0:docs, width + 128 : width + 129] - lse)
    from_batch = jnp.dot(g_batch, others, precision=HIGHEST, preferred_element_type=jnp.float32)
    d_emb = ((mix - target[...]) / all_docs + from_batch) / TAU
    d_pooled = (d_emb - own * jnp.sum(own * d_emb, axis=1, keepdims=True)) * rinv[0:docs, 0:1]
    tb = normed.shape[1]
    for doc in range(docs):
        dy = d_pooled[doc : doc + 1] / lengths[doc].astype(jnp.float32) * gain[...].reshape(1, width)
        level = dy - jnp.mean(dy, axis=1, keepdims=True)
        unit = normed[doc].astype(jnp.float32)
        along = jnp.mean(unit * dy, axis=1, keepdims=True)
        keep = lax.axis_index("ctx") * tb + lax.broadcasted_iota(jnp.int32, (tb, 1), 0) < lengths[doc]
        scale = jnp.where(keep, rstd[doc, :, 0:1], 0.0)
        d_summed[doc * tb : (doc + 1) * tb, :] = (scale * (level - unit * along)).astype(jnp.bfloat16)
    send_out[...] = jnp.dot(turned[width // 2 :], d_summed[...], preferred_element_type=jnp.float32)


def keep_kernel(turned, d_summed, out):
    out[...] = jnp.dot(turned[0 : out.shape[0]], d_summed[...], preferred_element_type=jnp.float32)


def sum_kernel(count, *refs):
    terms, outs = refs[:count], refs[count:]
    total = terms[0][...].astype(jnp.float32)
    for term in terms[1:]:
        total = total + term[...].astype(jnp.float32)
    rows = outs[0].shape[0]
    for index, out in enumerate(outs):
        out[...] = total[index * rows : (index + 1) * rows].astype(out.dtype)


def sum_and_split(terms, kind):
    rows, width = terms[0].shape
    piece = (rows // 4, width)
    shapes = (f32(*piece),) + (jax.ShapeDtypeStruct(piece, kind),) * 3
    return call(
        functools.partial(sum_kernel, len(terms)), shapes, [VMEM] * len(terms), (VMEM,) * 4, limit=8, name="sum_split"
    )(*terms)


def shards(tokens, w_qkv, w_out, ln_gain, cache, positive, lengths):
    docs, tb, width = tokens.shape
    n_ctx, n_dp = lax.axis_size("ctx"), lax.axis_size("dp")
    all_docs = n_dp * docs
    def halo(part):
        left = lax.ppermute(part, "ctx", [(i, (i + 1) % n_ctx) for i in range(n_ctx)])
        return left, lax.ppermute(part, "ctx", [((i + 1) % n_ctx, i) for i in range(n_ctx)])

    halos = [halo(tokens[0:CHUNK])]
    swapped = swap(cache, "dp", 4)
    gain = ln_gain
    qk, v_turned, w_v_turned, late = prepare(in_hbm(tokens), in_hbm(w_qkv))
    swapped, late = lax.optimization_barrier((swapped, late))
    halos.append(halo(late))
    rows = cache.shape[0]
    table = call(stack_kernel, bf16(2 * rows, width), [VMEM, VMEM], VMEM, limit=4, name="stack")(cache, swapped)
    tables = around(table, from_y)
    done = None
    for index, (left, right) in enumerate(halos):
        if index == 1:
            *done, pool = done
            pool, after = lax.optimization_barrier((pool, positive))
            done = [*done, pool]
            target = call(
                functools.partial(target_kernel, docs), f32(docs, width), [SMEM] + [VMEM] * 4, VMEM, name="target"
            )(after, *tables)
        done = attend(
            index * CHUNK, done, lengths, tokens, left, right, qk, v_turned, w_qkv, w_v_turned, w_out, gain
        )
    hidden, mixed, normed, rstd, pool = done

    turned = call(
        turn_kernel,
        bf16(width, docs * tb),
        [VMEM],
        VMEM,
        flops=2 * docs * tb * width * width,
        moved=4 * 2**20,
        name="turn",
    )(mixed)

    sums = call(stack_kernel, f32(2 * docs, width), [VMEM, VMEM], VMEM, limit=4, name="stack")(
        pool.reshape(docs, width), target
    )
    sums = add([sums, swap(sums, "ctx", 1)])
    sums = add(around(sums, from_x))
    emb, rinv, target = call(
        norm_kernel,
        (f32(2 * docs, width), f32(2 * docs, 128), f32(docs, width)),
        [VMEM] * 4,
        (VMEM,) * 3,
        limit=4,
        name="norm",
    )(*around(sums, from_z))
    embs = around(emb, from_y)
    everyone, state = call(
        functools.partial(score_kernel, docs),
        (f32(all_docs, width), f32(2 * docs, width + 256)),
        [SMEM] + [VMEM] * 8,
        (VMEM, VMEM),
        moved=2 * 2**20,
        scratch_shapes=[pltpu.VMEM((all_docs, n_dp * cache.shape[0]), jnp.float32)],
        name="score",
    )(positive, *embs, *tables)
    product, stats = call(
        functools.partial(batch_kernel, docs),
        (f32(2 * docs, all_docs), f32(8, all_docs)),
        [VMEM, VMEM],
        (VMEM, VMEM),
        limit=4,
        name="batch",
    )(emb, everyone)
    state = merged(docs, width, [state, swap(state, "ctx", 1)])
    state = merged(docs, width, around(state, from_x))
    half = width // 2
    send, d_summed, loss = call(
        grad_kernel,
        (f32(half, width), bf16(docs * tb, width), f32(8, 128)),
        [SMEM] + [VMEM] * 12,
        (VMEM,) * 3,
        flops=docs * tb * width * width,
        moved=8 * 2**20,
        name="grad",
    )(
        lengths, state, swap(state, "ctx", 2), emb, rinv, everyone, target, product, stats, gain, normed, rstd, turned,
    )
    keep = call(
        keep_kernel,
        f32(half, width),
        [VMEM, VMEM],
        VMEM,
        flops=docs * tb * width * width,
        moved=2**20,
        name="keep",
    )(turned, d_summed)
    keep, *sends = sum_and_split([keep, swap(send, "ctx", 1)], jnp.bfloat16)
    got = [from_plane(piece, -(k + 1), False) for k, piece in enumerate(sends)]
    keep, *sends = sum_and_split([keep] + got, jnp.float32)
    got = [from_plane(piece, -(k + 1), True) for k, piece in enumerate(sends)]
    keep, *sends = sum_and_split([keep] + got, jnp.float32)
    got = [from_z(piece, -(k + 1)) for k, piece in enumerate(sends)]
    return (hidden, loss[0, 0], add([keep] + got))


def solution(mesh):
    placed = (P("dp", "ctx", None), P(), P(), P(), P(("dp", "ctx"), None), P(), P("dp"))
    return jax.shard_map(
        shards,
        mesh=mesh,
        in_specs=placed,
        out_specs=(P("dp", "ctx", None), P(), P(("dp", "ctx"), None)),
        check_vma=False,
    )
```

```python
import functools
import math

import jax
import jax.numpy as jnp
from jax import lax
from jax.experimental import pallas as pl
from jax.experimental.pallas import tpu as pltpu
from jax.sharding import PartitionSpec as P

H = 12
WIN = 256
TAU = 0.02
FAR = 1e32
CHUNK = 2
NT = (((1,), (1,)), ((), ()))
TN = (((0,), (0,)), ((), ()))
HIGHEST = lax.Precision.HIGHEST
VMEM = pl.BlockSpec(memory_space=pltpu.VMEM)
SMEM = pl.BlockSpec(memory_space=pltpu.SMEM)
ANY = pl.BlockSpec(memory_space=pl.ANY)


def swap(value, axis, bits):
    return lax.ppermute(value, axis, [(i, i ^ bits) for i in range(lax.axis_size(axis))])


def from_x(value, k):
    size = lax.axis_size("ctx")
    return lax.ppermute(value, "ctx", [((c + 4 * k) % size, c) for c in range(size)])


def from_y(value, k):
    return lax.ppermute(value, "dp", [((d & 4) | ((d + k) & 3), d) for d in range(lax.axis_size("dp"))])


def from_z(value, k):
    n_dp, n_ctx = lax.axis_size("dp"), lax.axis_size("ctx")
    pairs = []
    for d in range(n_dp):
        for c in range(n_ctx):
            z = ((c & 2) + (d >> 2) + k) & 3
            pairs.append((((z & 1) * 4 + (d & 3)) * n_ctx + (c & ~2) + (z & 2), d * n_ctx + c))
    return lax.ppermute(value, ("dp", "ctx"), pairs)


def from_plane(value, k, last):
    n_dp, n_ctx = lax.axis_size("dp"), lax.axis_size("ctx")
    pairs = []
    for d in range(n_dp):
        for c in range(n_ctx):
            along_y = (c & 1 == 1) == last
            source = ((d & 4) | ((d + k) & 3), c) if along_y else (d, (c + 4 * k) % n_ctx)
            pairs.append((source[0] * n_ctx + source[1], d * n_ctx + c))
    return lax.ppermute(value, ("dp", "ctx"), pairs)


def around(value, fetch):
    return [value] + [fetch(value, k) for k in (1, 2, 3)]


def here():
    return lax.axis_index("dp"), lax.axis_index("ctx")


def in_hbm(value):
    return pltpu.with_memory_space_constraint(value, pltpu.HBM)


def call(kernel, out_shape, in_specs, out_specs, limit=16, flops=0, moved=0, **keywords):
    return pl.pallas_call(
        kernel,
        out_shape=out_shape,
        in_specs=in_specs,
        out_specs=out_specs,
        compiler_params=pltpu.CompilerParams(vmem_limit_bytes=limit * 2**20),
        cost_estimate=pl.CostEstimate(flops=flops, bytes_accessed=moved, transcendentals=0),
        **keywords,
    )


def f32(*shape):
    return jax.ShapeDtypeStruct(shape, jnp.float32)


def bf16(*shape):
    return jax.ShapeDtypeStruct(shape, jnp.bfloat16)


def slopes_of(heads):
    largest = 2 ** int(math.floor(math.log2(heads)))
    listed = [2.0 ** (-8.0 * (h + 1) / largest) for h in range(largest)]
    return listed + [2.0 ** (-4.0 * (2 * m + 1) / largest) for m in range(heads - largest)]


def thirds(value):
    high = value.astype(jnp.bfloat16)
    rest = value - high.astype(jnp.float32)
    middle = rest.astype(jnp.bfloat16)
    low = (rest - middle.astype(jnp.float32)).astype(jnp.bfloat16)
    parts = [p.astype(jnp.float32) for p in (high, middle, low)]
    return jnp.concatenate(parts, axis=0).astype(jnp.bfloat16)


def folded(products):
    rows = products.shape[0] // 3
    return products[0:rows] + products[rows : 2 * rows] + products[2 * rows :]


def attend_kernel(
    first, lengths, tok, left, right, qk, v_turned, w_k, w_v_turned, w_out, gain, *refs
):
    hidden, mixed, normed, rstd_out, pool, keys, values, dist = refs[-8:]
    tb, width = tok.shape[1:]
    ext = tb + 2 * WIN
    start, length = lax.axis_index("ctx") * tb, lengths[first + pl.program_id(0)]
    rows = jnp.concatenate([left[0], right[0]], axis=0)
    new = jnp.dot(rows, w_k[...], preferred_element_type=jnp.float32).astype(jnp.bfloat16)
    keys[0:WIN] = new[0:WIN]
    keys[WIN : WIN + tb] = qk[0, :, width:]
    keys[WIN + tb :] = new[WIN:]
    new = lax.dot_general(w_v_turned[...], rows, NT, preferred_element_type=jnp.float32).astype(jnp.bfloat16)
    values[:, 0:WIN] = new[:, 0:WIN]
    values[:, WIN : WIN + tb] = v_turned[...]
    values[:, WIN + tb :] = new[:, WIN:]
    j = lax.broadcasted_iota(jnp.int32, (ext, tb), 0) - WIN
    away = jnp.abs(lax.broadcasted_iota(jnp.int32, (ext, tb), 1) - j)
    kpos = start + j
    seen = (away <= WIN) & (((kpos >= 0) & (kpos < length)) | (away == 0))
    dist[...] = jnp.where(seen, away.astype(jnp.float32), FAR)
    half = lax.broadcasted_iota(jnp.int32, (tb, 128), 1) < 64
    slopes = slopes_of(H)
    lanes = 128
    span = lanes + 2 * WIN
    for pair in range(H // 2):
        cols = pl.ds(pair * 128, 128)
        query = qk[0, :, cols] * jnp.bfloat16(0.125)
        zero = jnp.bfloat16(0)
        both = jnp.concatenate([jnp.where(half, query, zero), jnp.where(half, zero, query)], axis=0)
        scores = lax.dot_general(keys[:, cols], both, NT, preferred_element_type=jnp.float32)
        for part in range(2):
            columns = []
            for low in range(0, tb, lanes):
                score = scores[low : low + span, part * tb + low : part * tb + low + lanes]
                score = score - slopes[2 * pair + part] * dist[pl.ds(low, span), pl.ds(low, lanes)]
                expo = jnp.exp(score - jnp.max(score, axis=0, keepdims=True))
                weights = (expo * (1.0 / jnp.sum(expo, axis=0, keepdims=True))).astype(jnp.bfloat16)
                above, below = low, ext - span - low
                pieces = [weights]
                if above:
                    pieces = [jnp.zeros((above, lanes), jnp.bfloat16)] + pieces
                if below:
                    pieces = pieces + [jnp.zeros((below, lanes), jnp.bfloat16)]
                columns.append(jnp.concatenate(pieces, axis=0))
            weights = jnp.concatenate(columns, axis=1)
            head = pl.ds(pair * 128 + part * 64, 64)
            mixed[head, :] = jnp.dot(values[head, :], weights, preferred_element_type=jnp.float32).astype(jnp.bfloat16)
    summed = tok[0].astype(jnp.float32) + lax.dot_general(mixed[...], w_out[...], TN, preferred_element_type=jnp.float32)
    centred = summed - jnp.mean(summed, axis=1, keepdims=True)
    rstd = lax.rsqrt(jnp.mean(centred * centred, axis=1, keepdims=True) + 1e-05)
    unit = centred * rstd
    hidden_f = unit * gain[...].reshape(1, width)
    hidden[0] = hidden_f.astype(jnp.bfloat16)
    normed[0] = unit.astype(jnp.bfloat16)
    rstd_out[0] = jnp.broadcast_to(rstd, rstd_out.shape[1:])
    keep = start + lax.broadcasted_iota(jnp.int32, (tb, 1), 0) < length
    pool[0] = jnp.sum(jnp.where(keep, hidden_f, 0.0), axis=0, keepdims=True) / length.astype(jnp.float32)


def attend(first, before, lengths, tokens, left, right, qk, v_turned, w_qkv, w_v_turned, w_out, gain):
    docs, tb, width = tokens.shape
    ext = tb + 2 * WIN
    at = lambda *s: pl.BlockSpec((1,) + s, lambda i: (first + i, 0, 0))
    chunk = lambda *s: pl.BlockSpec((1,) + s, lambda i: (i, 0, 0))
    column = pl.BlockSpec((width, tb), lambda i: (0, first + i))
    fixed = lambda s, place=(0, 0): pl.BlockSpec(s, lambda i: place, pipeline_mode=pl.Buffered(1))
    out_shape = (bf16(docs, tb, width), bf16(width, docs * tb), bf16(docs, tb, width), f32(docs, tb, 128), f32(docs, 1, width))
    in_specs = [
        SMEM, at(tb, width), chunk(WIN, width), chunk(WIN, width), at(tb, 2 * width), column,
        fixed((width, width), (0, 1)), fixed((width, width)), fixed((width, width)), VMEM,
    ]
    operands = [lengths, tokens, left, right, qk, v_turned, w_qkv, w_v_turned, w_out, gain]
    aliases = {}
    if before is not None:
        aliases = {len(operands) + k: k for k in range(len(out_shape))}
        operands = operands + list(before)
        in_specs = in_specs + [ANY] * len(out_shape)
    return call(
        functools.partial(attend_kernel, first),
        out_shape,
        in_specs,
        (at(tb, width), column, at(tb, width), at(tb, 128), at(1, width)),
        limit=30,
        flops=CHUNK * 5 * 2 * tb * ext * width,
        moved=8 * 2**20,
        grid=(CHUNK,),
        scratch_shapes=[
            pltpu.VMEM((ext, width), jnp.bfloat16),
            pltpu.VMEM((width, ext), jnp.bfloat16),
            pltpu.VMEM((ext, tb), jnp.float32),
        ],
        input_output_aliases=aliases,
        name="attend",
    )(*operands)


def prepare_kernel(tok, w, qk, v_turned, w_v_turned, late):
    width = tok.shape[2]
    late[...] = tok[...]

    @pl.when(pl.program_id(0) == 0)
    def _():
        w_v_turned[...] = w[:, 2 * width :].T

    rows = tok[0]
    qk[0] = jnp.dot(rows, w[:, 0 : 2 * width], preferred_element_type=jnp.float32).astype(jnp.bfloat16)
    v_turned[...] = lax.dot_general(w_v_turned[...], rows, NT, preferred_element_type=jnp.float32).astype(jnp.bfloat16)


def prepare(tokens, w_qkv):
    docs, tb, width = tokens.shape
    return call(
        prepare_kernel,
        (bf16(docs, tb, 2 * width), bf16(width, docs * tb), bf16(width, width), bf16(docs - CHUNK, tb, width)),
        [
            pl.BlockSpec((1, tb, width), lambda i: (i, 0, 0)),
            pl.BlockSpec(w_qkv.shape, lambda i: (0, 0), pipeline_mode=pl.Buffered(1)),
        ],
        (
            pl.BlockSpec((1, tb, 2 * width), lambda i: (i, 0, 0)),
            pl.BlockSpec((width, tb), lambda i: (0, i)),
            pl.BlockSpec((width, width), lambda i: (0, 0)),
            pl.BlockSpec((1, tb, width), lambda i: (jnp.maximum(i - CHUNK, 0), 0, 0)),
        ),
        flops=2 * docs * tb * width * 3 * width,
        moved=11 * 2**20,
        grid=(docs,),
        name="prepare",
    )(tokens, w_qkv)


def row_ids(k, shape, dim):
    dp, ctx = here()
    place = lax.broadcasted_iota(jnp.int32, shape, dim)
    return (((dp & 4) | ((dp + k) & 3)) * 16 + ctx) * shape[dim] + place


def stack_kernel(pool, target, out):
    docs = pool.shape[0]
    for doc in range(docs):
        out[doc : doc + 1, :] = pool[doc]
    out[docs:, :] = target[...]


def add_kernel(*refs):
    terms = [ref[...] for ref in refs[:-1]]
    if len(terms) == 4:
        terms = [terms[0] + terms[2], terms[1] + terms[3]]
    refs[-1][...] = terms[0] + terms[1]


def add(terms):
    return call(add_kernel, f32(*terms[0].shape), [VMEM] * len(terms), VMEM, limit=4, name="add")(*terms)


def merge_kernel(docs, width, *refs):
    refs[-1][...] = merge(docs, width, [ref[...] for ref in refs[:-1]])


def merged(docs, width, states):
    kernel = functools.partial(merge_kernel, docs, width)
    return call(kernel, f32(*states[0].shape), [VMEM] * len(states), VMEM, limit=4, name="merge")(*states)


def target_kernel(docs, positive, *refs):
    pieces, out = refs[:4], refs[4]
    dp, _ = here()
    total = jnp.zeros(out.shape, jnp.float32)
    for k, piece in enumerate(pieces):
        shape = (out.shape[0], piece.shape[0])
        doc = lax.broadcasted_iota(jnp.int32, shape, 0)
        wanted = jnp.zeros(shape, jnp.int32)
        for d in range(2 * docs):
            wanted = jnp.where(doc == d, positive[(d // docs * 4 + (dp & 3)) * docs + d % docs], wanted)
        hit = (row_ids(k, shape, 1) == wanted).astype(jnp.float32).astype(jnp.bfloat16)
        total = total + jnp.dot(hit, piece[...], preferred_element_type=jnp.float32)
    out[...] = total


def turn_kernel(mixed, out):
    width = out.shape[0]
    place = lax.broadcasted_iota(jnp.int32, (width, 1), 0)
    dp, ctx = here()
    each = width // 128
    core = (ctx & 1) ^ (place // (64 * each))
    first, second = place // (16 * each) % 4, place // (4 * each) % 4
    y = ((dp & 3) + jnp.where(core == 0, first, second)) & 3
    x = ((ctx >> 2) + jnp.where(core == 0, second, first)) & 3
    z = ((ctx & 2) + (dp >> 2) + place // each % 4) & 3
    block = ((z & 1) * 4 + y) * 16 + x * 4 + (z >> 1) * 2 + core
    chosen = block * each + place % each == lax.broadcasted_iota(jnp.int32, (width, width), 1)
    chosen = jnp.where(chosen, 1.0, 0.0).astype(jnp.bfloat16)
    out[...] = jnp.dot(chosen, mixed[...], preferred_element_type=jnp.float32).astype(jnp.bfloat16)


def norm_kernel(s0, s1, s2, s3, emb_out, rinv_out, target_out):
    docs = s0.shape[0] // 3
    dp, _ = here()
    own, other = s0[0:docs] + s2[0:docs], s1[0:docs] + s3[0:docs]
    second = dp >= 4
    pooled = jnp.concatenate([jnp.where(second, other, own), jnp.where(second, own, other)], axis=0)
    rinv = lax.rsqrt(jnp.sum(pooled * pooled, axis=1, keepdims=True) + 1e-06)
    emb_out[...] = pooled * rinv
    rinv_out[...] = jnp.broadcast_to(rinv, rinv_out.shape)
    target_out[...] = (s0[docs:] + s2[docs:]) + (s1[docs:] + s3[docs:])


def as_row(column):
    size = column.shape[0]
    same = lax.broadcasted_iota(jnp.int32, (size, size), 0) == lax.broadcasted_iota(jnp.int32, (size, size), 1)
    return jnp.sum(jnp.where(same, column, 0.0), axis=0, keepdims=True)


def score_kernel(docs, positive, e0, e1, e2, e3, t0, t1, t2, t3, everyone, state, expos):
    all_docs, width = everyone.shape
    dp, _ = here()
    y = dp & 3
    group = e0.shape[0]
    for k, piece in enumerate((e0, e1, e2, e3)):
        everyone[pl.ds(pl.multiple_of(((y + k) & 3) * group, group), group), :] = piece[...]
    tables = (t0, t1, t2, t3)
    rows = t0.shape[0]
    emb = thirds(everyone[...])
    scores = [folded(lax.dot_general(emb, t[...], NT, preferred_element_type=jnp.float32)) / TAU for t in tables]
    tops = [jnp.max(s, axis=1, keepdims=True) for s in scores]
    top = jnp.maximum(jnp.maximum(tops[0], tops[2]), jnp.maximum(tops[1], tops[3]))
    row = lax.broadcasted_iota(jnp.int32, (all_docs, rows), 0)
    wanted = jnp.zeros((all_docs, rows), jnp.int32)
    for doc in range(all_docs):
        z, rest = divmod(doc, all_docs // 2)
        wanted = jnp.where(row == rest // docs * group + z * docs + rest % docs, positive[doc], wanted)
    totals, found = [], jnp.zeros((all_docs, 1), jnp.float32)
    for k, s in enumerate(scores):
        expo = jnp.exp(s - top)
        expos[:, k * rows : (k + 1) * rows] = expo
        totals.append(jnp.sum(expo, axis=1, keepdims=True))
        hit = row_ids(k, (all_docs, rows), 1) == wanted
        found = found + jnp.sum(jnp.where(hit, s, 0.0), axis=1, keepdims=True)
    total = (totals[0] + totals[2]) + (totals[1] + totals[3])
    mine = thirds(expos[pl.ds(pl.multiple_of(y * group, group), group), :])
    mix = jnp.zeros((group, width), jnp.float32)
    for k, t in enumerate(tables):
        mix = mix + folded(jnp.dot(mine[:, k * rows : (k + 1) * rows], t[...], preferred_element_type=jnp.float32))
    column = lax.broadcasted_iota(jnp.int32, (group, all_docs), 1)
    own = column == lax.broadcasted_iota(jnp.int32, (group, all_docs), 0) + y * group
    total_row, top_row, found_row = as_row(total), as_row(top), as_row(found)
    state[...] = jnp.zeros_like(state)
    state[0:group, 0:width] = mix
    for place, values in ((width, total_row), (width + 128, top_row)):
        value = jnp.sum(jnp.where(own, values, 0.0), axis=1, keepdims=True)
        state[0:group, place : place + 128] = jnp.broadcast_to(value, (group, 128))
    for index, values in enumerate((total_row, top_row, found_row)):
        state[group + index : group + index + 1, 0:all_docs] = values


def merge(docs, width, states):
    row = lax.broadcasted_iota(jnp.int32, states[0].shape, 0)
    column = lax.broadcasted_iota(jnp.int32, states[0].shape, 1)
    place = width + 128
    by_row = [s[:, place : place + 1] for s in states]
    by_lane = [s[docs + 1 : docs + 2, :] for s in states]
    top_row = functools.reduce(jnp.maximum, by_row)
    top_lane = functools.reduce(jnp.maximum, by_lane)
    terms = [
        s * jnp.exp(jnp.where(row == docs, b - top_lane, a - top_row)) for s, a, b in zip(states, by_row, by_lane)
    ]
    if len(terms) == 4:
        terms = [terms[0] + terms[2], terms[1] + terms[3]]
    joined = jnp.where((row < docs) & (column >= place), top_row, terms[0] + terms[1])
    return jnp.where(row == docs + 1, top_lane, joined)


def batch_kernel(emb, everyone, product_out, stats):
    everything = everyone[...]
    all_docs = everything.shape[0]
    own = lax.dot_general(emb[...], everything, NT, precision=HIGHEST, preferred_element_type=jnp.float32) / TAU
    product = lax.dot_general(everything, everything, NT, precision=HIGHEST, preferred_element_type=jnp.float32) / TAU
    wide = (all_docs, all_docs)
    same = lax.broadcasted_iota(jnp.int32, wide, 0) == lax.broadcasted_iota(jnp.int32, wide, 1)
    product = jnp.where(same, -1e30, product)
    top = jnp.max(product, axis=0, keepdims=True)
    total = jnp.sum(jnp.exp(product - top), axis=0, keepdims=True)
    product_out[...] = own
    stats[...] = jnp.concatenate([top, total] * 4, axis=0)


def grad_kernel(
    lengths, s0, s1, s2, s3, emb, rinv, everyone, target, product, stats, gain, normed, rstd, turned,
    send_out, d_summed, loss_out,
):
    docs, tb, width = normed.shape
    all_docs, group = everyone.shape[0], emb.shape[0]
    dp, _ = here()
    mine = lambda a: jnp.where(dp >= 4, a[docs:group], a[0:docs])
    own, others = mine(emb), everyone[...]
    now = merge(group, width, [s[...] for s in (s0, s1, s2, s3)])
    total, top, found = (now[group + k : group + k + 1, 0:all_docs] for k in range(3))
    batch_top, batch_total = stats[0:1], stats[1:2]
    peak = jnp.maximum(top, batch_top)
    lse_row = peak + jnp.log(total * jnp.exp(top - peak) + batch_total * jnp.exp(batch_top - peak))
    loss_out[...] = jnp.broadcast_to(jnp.sum(lse_row - found, axis=1, keepdims=True) / all_docs, loss_out.shape)
    column = lax.broadcasted_iota(jnp.int32, (docs, all_docs), 1)
    first = (dp & 3) * group + (dp >> 2) * docs
    same = column == lax.broadcasted_iota(jnp.int32, (docs, all_docs), 0) + first
    lse = jnp.sum(jnp.where(same, lse_row, 0.0), axis=1, keepdims=True)
    scores = mine(product)
    g_batch = jnp.where(same, 0.0, jnp.exp(scores - lse) + jnp.exp(scores - lse_row)) / all_docs
    shares = mine(now)
    mix = shares[:, 0:width] * jnp.exp(shares[:, width + 128 : width + 129] - lse)
    from_batch = jnp.dot(g_batch, others, precision=HIGHEST, preferred_element_type=jnp.float32)
    d_emb = ((mix - mine(target)) / all_docs + from_batch) / TAU
    d_pooled = (d_emb - own * jnp.sum(own * d_emb, axis=1, keepdims=True)) * mine(rinv)[:, 0:1]
    for doc in range(docs):
        dy = d_pooled[doc : doc + 1] / lengths[doc].astype(jnp.float32) * gain[...].reshape(1, width)
        level = dy - jnp.mean(dy, axis=1, keepdims=True)
        unit = normed[doc].astype(jnp.float32)
        along = jnp.mean(unit * dy, axis=1, keepdims=True)
        keep = lax.axis_index("ctx") * tb + lax.broadcasted_iota(jnp.int32, (tb, 1), 0) < lengths[doc]
        scale = jnp.where(keep, rstd[doc, :, 0:1], 0.0)
        d_summed[doc * tb : (doc + 1) * tb, :] = (scale * (level - unit * along)).astype(jnp.bfloat16)
    send_out[...] = jnp.dot(turned[width // 2 :], d_summed[...], preferred_element_type=jnp.float32)


def keep_kernel(turned, d_summed, out):
    out[...] = jnp.dot(turned[0 : out.shape[0]], d_summed[...], preferred_element_type=jnp.float32)


def sum_kernel(count, *refs):
    terms, outs = refs[:count], refs[count:]
    total = terms[0][...].astype(jnp.float32)
    for term in terms[1:]:
        total = total + term[...].astype(jnp.float32)
    rows = outs[0].shape[0]
    for index, out in enumerate(outs):
        out[...] = total[index * rows : (index + 1) * rows].astype(out.dtype)


def sum_and_split(terms, kind):
    rows, width = terms[0].shape
    piece = (rows // 4, width)
    shapes = (f32(*piece),) + (jax.ShapeDtypeStruct(piece, kind),) * 3
    return call(
        functools.partial(sum_kernel, len(terms)), shapes, [VMEM] * len(terms), (VMEM,) * 4, limit=8, name="sum_split"
    )(*terms)


def shards(tokens, w_qkv, w_out, ln_gain, cache, positive, lengths):
    docs, tb, width = tokens.shape
    n_ctx, n_dp = lax.axis_size("ctx"), lax.axis_size("dp")
    all_docs = n_dp * docs
    def halo(part):
        left = lax.ppermute(part, "ctx", [(i, (i + 1) % n_ctx) for i in range(n_ctx)])
        return left, lax.ppermute(part, "ctx", [((i + 1) % n_ctx, i) for i in range(n_ctx)])

    halos = [halo(tokens[0:CHUNK])]
    tables = around(cache, from_y)
    gain = ln_gain
    qk, v_turned, w_v_turned, late = prepare(in_hbm(tokens), in_hbm(w_qkv))
    halos.append(halo(late))
    done = None
    for index, (left, right) in enumerate(halos):
        if index == 1:
            *done, pool = done
            pool, after = lax.optimization_barrier((pool, positive))
            done = [*done, pool]
            target = call(
                functools.partial(target_kernel, docs), f32(2 * docs, width), [SMEM] + [VMEM] * 4, VMEM, name="target"
            )(after, *tables)
            left, target = lax.optimization_barrier((left, target))
        done = attend(
            index * CHUNK, done, lengths, tokens, left, right, qk, v_turned, w_qkv, w_v_turned, w_out, gain
        )
    hidden, mixed, normed, rstd, pool = done

    turned = call(
        turn_kernel,
        bf16(width, docs * tb),
        [VMEM],
        VMEM,
        flops=2 * docs * tb * width * width,
        moved=4 * 2**20,
        name="turn",
    )(mixed)

    group = 2 * docs
    sums = call(stack_kernel, f32(docs + group, width), [VMEM, VMEM], VMEM, limit=4, name="stack")(
        pool, target
    )
    sums = add([sums, swap(sums, "ctx", 1)])
    sums = add(around(sums, from_x))
    emb, rinv, target = call(
        norm_kernel,
        (f32(group, width), f32(group, 128), f32(group, width)),
        [VMEM] * 4,
        (VMEM,) * 3,
        limit=4,
        name="norm",
    )(*around(sums, from_z))
    embs = around(emb, from_y)
    everyone, state = call(
        functools.partial(score_kernel, docs),
        (f32(all_docs, width), f32(2 * group, width + 256)),
        [SMEM] + [VMEM] * 8,
        (VMEM, VMEM),
        moved=2 * 2**20,
        scratch_shapes=[pltpu.VMEM((all_docs, n_dp * cache.shape[0]), jnp.float32)],
        name="score",
    )(positive, *embs, *tables)
    product, stats = call(
        batch_kernel,
        (f32(group, all_docs), f32(8, all_docs)),
        [VMEM, VMEM],
        (VMEM, VMEM),
        limit=4,
        name="batch",
    )(emb, everyone)
    state = merged(group, width, [state, swap(state, "ctx", 1)])
    state = merged(group, width, around(state, from_x))
    half = width // 2
    send, d_summed, loss = call(
        grad_kernel,
        (f32(half, width), bf16(docs * tb, width), f32(8, 128)),
        [SMEM] + [VMEM] * 14,
        (VMEM,) * 3,
        flops=docs * tb * width * width,
        moved=8 * 2**20,
        name="grad",
    )(
        lengths, *around(state, from_z), emb, rinv, everyone, target, product, stats, gain, normed, rstd, turned,
    )
    keep = call(
        keep_kernel,
        f32(half, width),
        [VMEM, VMEM],
        VMEM,
        flops=docs * tb * width * width,
        moved=2**20,
        name="keep",
    )(turned, d_summed)
    keep, *sends = sum_and_split([keep, swap(send, "ctx", 1)], jnp.bfloat16)
    got = [from_plane(piece, -(k + 1), False) for k, piece in enumerate(sends)]
    keep, *sends = sum_and_split([keep] + got, jnp.float32)
    got = [from_plane(piece, -(k + 1), True) for k, piece in enumerate(sends)]
    keep, *sends = sum_and_split([keep] + got, jnp.float32)
    got = [from_z(piece, -(k + 1)) for k, piece in enumerate(sends)]
    return (hidden, loss[0, 0], add([keep] + got))


def solution(mesh):
    placed = (P("dp", "ctx", None), P(), P(), P(), P(("dp", "ctx"), None), P(), P("dp"))
    return jax.shard_map(
        shards,
        mesh=mesh,
        in_specs=placed,
        out_specs=(P("dp", "ctx", None), P(), P(("dp", "ctx"), None)),
        check_vma=False,
    )
```

```python
import functools
import math

import jax
import jax.numpy as jnp
from jax import lax
from jax.experimental import pallas as pl
from jax.experimental.pallas import tpu as pltpu
from jax.sharding import PartitionSpec as P

H = 12
WIN = 256
TAU = 0.02
FAR = 1e32
NT = (((1,), (1,)), ((), ()))
TN = (((0,), (0,)), ((), ()))
HIGHEST = lax.Precision.HIGHEST
VMEM = pl.BlockSpec(memory_space=pltpu.VMEM)
SMEM = pl.BlockSpec(memory_space=pltpu.SMEM)
ANY = pl.BlockSpec(memory_space=pl.ANY)


def swap(value, axis, bits):
    return lax.ppermute(value, axis, [(i, i ^ bits) for i in range(lax.axis_size(axis))])


def from_x(value, k):
    size = lax.axis_size("ctx")
    return lax.ppermute(value, "ctx", [((c + 4 * k) % size, c) for c in range(size)])


def from_y(value, k):
    return lax.ppermute(value, "dp", [((d & 4) | ((d + k) & 3), d) for d in range(lax.axis_size("dp"))])


def from_z(value, k):
    n_dp, n_ctx = lax.axis_size("dp"), lax.axis_size("ctx")
    pairs = []
    for d in range(n_dp):
        for c in range(n_ctx):
            z = ((c & 2) + (d >> 2) + k) & 3
            pairs.append((((z & 1) * 4 + (d & 3)) * n_ctx + (c & ~2) + (z & 2), d * n_ctx + c))
    return lax.ppermute(value, ("dp", "ctx"), pairs)


def from_plane(value, k, last):
    n_dp, n_ctx = lax.axis_size("dp"), lax.axis_size("ctx")
    pairs = []
    for d in range(n_dp):
        for c in range(n_ctx):
            along_y = (c & 1 == 1) == last
            source = ((d & 4) | ((d + k) & 3), c) if along_y else (d, (c + 4 * k) % n_ctx)
            pairs.append((source[0] * n_ctx + source[1], d * n_ctx + c))
    return lax.ppermute(value, ("dp", "ctx"), pairs)


def around(value, fetch):
    return [value] + [fetch(value, k) for k in (1, 2, 3)]


def here():
    return lax.axis_index("dp"), lax.axis_index("ctx")


def in_hbm(value):
    return pltpu.with_memory_space_constraint(value, pltpu.HBM)


def call(kernel, out_shape, in_specs, out_specs, limit=16, flops=0, moved=0, **keywords):
    return pl.pallas_call(
        kernel,
        out_shape=out_shape,
        in_specs=in_specs,
        out_specs=out_specs,
        compiler_params=pltpu.CompilerParams(vmem_limit_bytes=limit * 2**20),
        cost_estimate=pl.CostEstimate(flops=flops, bytes_accessed=moved, transcendentals=0),
        **keywords,
    )


def f32(*shape):
    return jax.ShapeDtypeStruct(shape, jnp.float32)


def bf16(*shape):
    return jax.ShapeDtypeStruct(shape, jnp.bfloat16)


def slopes_of(heads):
    largest = 2 ** int(math.floor(math.log2(heads)))
    listed = [2.0 ** (-8.0 * (h + 1) / largest) for h in range(largest)]
    return listed + [2.0 ** (-4.0 * (2 * m + 1) / largest) for m in range(heads - largest)]


def thirds(value):
    high = value.astype(jnp.bfloat16)
    rest = value - high.astype(jnp.float32)
    middle = rest.astype(jnp.bfloat16)
    low = (rest - middle.astype(jnp.float32)).astype(jnp.bfloat16)
    parts = [p.astype(jnp.float32) for p in (high, middle, low)]
    return jnp.concatenate(parts, axis=0).astype(jnp.bfloat16)


def folded(products):
    rows = products.shape[0] // 3
    return products[0:rows] + products[rows : 2 * rows] + products[2 * rows :]


def attend_kernel(
    doc, lengths, tok, near, far, qk, v_turned, w, w_v_turned, w_out, gain, *refs
):
    hidden, mixed_all, normed, rstd_out, pool, keys, values, dist, hidden_here, sem = refs[-10:]
    docs, tb, width = tok.shape
    ext = tb + 2 * WIN
    own = pl.ds(doc * tb, tb)
    mixed = mixed_all.at[:, own]
    ctx = lax.axis_index("ctx")
    start, length = ctx * tb, lengths[doc]
    right = lax.rem(ctx, 2) == 0
    rows = jnp.concatenate([jnp.where(right, far[...], near[doc]), jnp.where(right, near[doc], far[...])], axis=0)
    new = jnp.dot(rows, w[:, width : 2 * width], preferred_element_type=jnp.float32).astype(jnp.bfloat16)
    keys[0:WIN] = new[0:WIN]
    keys[WIN : WIN + tb] = qk[doc, :, width:]
    keys[WIN + tb :] = new[WIN:]
    new = lax.dot_general(w_v_turned[...], rows, NT, preferred_element_type=jnp.float32).astype(jnp.bfloat16)
    values[:, 0:WIN] = new[:, 0:WIN]
    values[:, WIN : WIN + tb] = v_turned[:, own]
    values[:, WIN + tb :] = new[:, WIN:]
    j = lax.broadcasted_iota(jnp.int32, (ext, tb), 0) - WIN
    away = jnp.abs(lax.broadcasted_iota(jnp.int32, (ext, tb), 1) - j)
    kpos = start + j
    seen = (away <= WIN) & (((kpos >= 0) & (kpos < length)) | (away == 0))
    dist[...] = jnp.where(seen, away.astype(jnp.float32), FAR)
    half = lax.broadcasted_iota(jnp.int32, (tb, 128), 1) < 64
    slopes = slopes_of(H)
    lanes = 128
    span = lanes + 2 * WIN
    for pair in range(H // 2):
        cols = pl.ds(pair * 128, 128)
        query = qk[doc, :, cols] * jnp.bfloat16(0.125)
        zero = jnp.bfloat16(0)
        both = jnp.concatenate([jnp.where(half, query, zero), jnp.where(half, zero, query)], axis=0)
        scores = lax.dot_general(keys[:, cols], both, NT, preferred_element_type=jnp.float32)
        for part in range(2):
            columns = []
            for low in range(0, tb, lanes):
                score = scores[low : low + span, part * tb + low : part * tb + low + lanes]
                score = score - slopes[2 * pair + part] * dist[pl.ds(low, span), pl.ds(low, lanes)]
                expo = jnp.exp(score - jnp.max(score, axis=0, keepdims=True))
                weights = (expo * (1.0 / jnp.sum(expo, axis=0, keepdims=True))).astype(jnp.bfloat16)
                above, below = low, ext - span - low
                pieces = [weights]
                if above:
                    pieces = [jnp.zeros((above, lanes), jnp.bfloat16)] + pieces
                if below:
                    pieces = pieces + [jnp.zeros((below, lanes), jnp.bfloat16)]
                columns.append(jnp.concatenate(pieces, axis=0))
            weights = jnp.concatenate(columns, axis=1)
            head = pl.ds(pair * 128 + part * 64, 64)
            mixed[head, :] = jnp.dot(values[head, :], weights, preferred_element_type=jnp.float32).astype(jnp.bfloat16)
    summed = tok[doc].astype(jnp.float32) + lax.dot_general(
        mixed[...], w_out[...], TN, preferred_element_type=jnp.float32
    )
    centred = summed - jnp.mean(summed, axis=1, keepdims=True)
    rstd = lax.rsqrt(jnp.mean(centred * centred, axis=1, keepdims=True) + 1e-05)
    unit = centred * rstd
    hidden_f = unit * gain[...].reshape(1, width)
    hidden_here[...] = hidden_f.astype(jnp.bfloat16)
    leaving = pltpu.make_async_copy(hidden_here, hidden.at[doc], sem)
    leaving.start()
    normed[doc] = unit.astype(jnp.bfloat16)
    rstd_out[doc] = jnp.broadcast_to(rstd, rstd_out.shape[1:])
    keep = start + lax.broadcasted_iota(jnp.int32, (tb, 1), 0) < length
    pool[doc] = jnp.sum(jnp.where(keep, hidden_f, 0.0), axis=0, keepdims=True) / length.astype(jnp.float32)
    leaving.wait()


def attend(doc, before, lengths, tokens, near, far, qk, v_turned, w_qkv, w_v_turned, w_out, gain):
    docs, tb, width = tokens.shape
    ext = tb + 2 * WIN
    out_shape = (bf16(docs, tb, width), bf16(width, docs * tb), bf16(docs, tb, width), f32(docs, tb, 128), f32(docs, 1, width))
    out_specs = (ANY,) + (VMEM,) * 4
    operands = [lengths, tokens, near, far, qk, v_turned, w_qkv, w_v_turned, w_out, gain]
    in_specs = [SMEM] + [VMEM] * 9
    aliases = {}
    if before is not None:
        aliases = {len(operands) + k: k for k in range(len(out_shape))}
        operands = operands + list(before)
        in_specs = in_specs + list(out_specs)
    return call(
        functools.partial(attend_kernel, doc),
        out_shape,
        in_specs,
        out_specs,
        limit=24,
        flops=5 * 2 * tb * ext * width,
        moved=4 * 2**20,
        scratch_shapes=[
            pltpu.VMEM((ext, width), jnp.bfloat16),
            pltpu.VMEM((width, ext), jnp.bfloat16),
            pltpu.VMEM((ext, tb), jnp.float32),
            pltpu.VMEM((tb, width), jnp.bfloat16),
            pltpu.SemaphoreType.DMA,
        ],
        input_output_aliases=aliases,
        name="attend",
    )(*operands)


def prepare_kernel(tok, w, qk, v_turned, w_v_turned, *later):
    width = tok.shape[2]
    for index, late in enumerate(later):

        @pl.when(pl.program_id(0) == index + 1)
        def _():
            late[...] = tok[0]

    @pl.when(pl.program_id(0) == 0)
    def _():
        w_v_turned[...] = w[:, 2 * width :].T

    rows = tok[0]
    qk[0] = jnp.dot(rows, w[:, 0 : 2 * width], preferred_element_type=jnp.float32).astype(jnp.bfloat16)
    v_turned[...] = lax.dot_general(w_v_turned[...], rows, NT, preferred_element_type=jnp.float32).astype(jnp.bfloat16)


def prepare(tokens, w_qkv):
    docs, tb, width = tokens.shape
    return call(
        prepare_kernel,
        (bf16(docs, tb, 2 * width), bf16(width, docs * tb), bf16(width, width)) + (bf16(tb, width),) * (docs - 1),
        [
            pl.BlockSpec((1, tb, width), lambda i: (i, 0, 0)),
            pl.BlockSpec(w_qkv.shape, lambda i: (0, 0), pipeline_mode=pl.Buffered(1)),
        ],
        (
            pl.BlockSpec((1, tb, 2 * width), lambda i: (i, 0, 0)),
            pl.BlockSpec((width, tb), lambda i: (0, i)),
            pl.BlockSpec((width, width), lambda i: (0, 0)),
        )
        + (pl.BlockSpec((tb, width), lambda i: (0, 0)),) * (docs - 1),
        flops=2 * docs * tb * width * 3 * width,
        moved=11 * 2**20,
        grid=(docs,),
        name="prepare",
    )(tokens, w_qkv)


def row_ids(k, shape, dim):
    dp, ctx = here()
    place = lax.broadcasted_iota(jnp.int32, shape, dim)
    return (((dp & 4) | ((dp + k) & 3)) * 16 + ctx) * shape[dim] + place


def stack_kernel(pool, target, out):
    docs = pool.shape[0]
    for doc in range(docs):
        out[doc : doc + 1, :] = pool[doc]
    out[docs:, :] = target[...]


def add_kernel(*refs):
    terms = [ref[...] for ref in refs[:-1]]
    if len(terms) == 4:
        terms = [terms[0] + terms[2], terms[1] + terms[3]]
    refs[-1][...] = terms[0] + terms[1]


def add(terms):
    return call(add_kernel, f32(*terms[0].shape), [VMEM] * len(terms), VMEM, limit=4, name="add")(*terms)


def merge_kernel(docs, width, *refs):
    refs[-1][...] = merge(docs, width, [ref[...] for ref in refs[:-1]])


def merged(docs, width, states):
    kernel = functools.partial(merge_kernel, docs, width)
    return call(kernel, f32(*states[0].shape), [VMEM] * len(states), VMEM, limit=4, name="merge")(*states)


def target_kernel(docs, positive, *refs):
    pieces, out = refs[:4], refs[4]
    dp, _ = here()
    total = jnp.zeros(out.shape, jnp.float32)
    for k, piece in enumerate(pieces):
        shape = (out.shape[0], piece.shape[0])
        doc = lax.broadcasted_iota(jnp.int32, shape, 0)
        wanted = jnp.zeros(shape, jnp.int32)
        for d in range(2 * docs):
            wanted = jnp.where(doc == d, positive[(d // docs * 4 + (dp & 3)) * docs + d % docs], wanted)
        hit = (row_ids(k, shape, 1) == wanted).astype(jnp.float32).astype(jnp.bfloat16)
        total = total + jnp.dot(hit, piece[...], preferred_element_type=jnp.float32)
    out[...] = total


def turn_kernel(mixed, out):
    width = out.shape[0]
    place = lax.broadcasted_iota(jnp.int32, (width, 1), 0)
    dp, ctx = here()
    each = width // 128
    core = (ctx & 1) ^ (place // (64 * each))
    first, second = place // (16 * each) % 4, place // (4 * each) % 4
    y = ((dp & 3) + jnp.where(core == 0, first, second)) & 3
    x = ((ctx >> 2) + jnp.where(core == 0, second, first)) & 3
    z = ((ctx & 2) + (dp >> 2) + place // each % 4) & 3
    block = ((z & 1) * 4 + y) * 16 + x * 4 + (z >> 1) * 2 + core
    chosen = block * each + place % each == lax.broadcasted_iota(jnp.int32, (width, width), 1)
    chosen = jnp.where(chosen, 1.0, 0.0).astype(jnp.bfloat16)
    out[...] = jnp.dot(chosen, mixed[...], preferred_element_type=jnp.float32).astype(jnp.bfloat16)


def norm_kernel(s0, s1, s2, s3, emb_out, rinv_out, target_out):
    docs = s0.shape[0] // 3
    dp, _ = here()
    own, other = s0[0:docs] + s2[0:docs], s1[0:docs] + s3[0:docs]
    second = dp >= 4
    pooled = jnp.concatenate([jnp.where(second, other, own), jnp.where(second, own, other)], axis=0)
    rinv = lax.rsqrt(jnp.sum(pooled * pooled, axis=1, keepdims=True) + 1e-06)
    emb_out[...] = pooled * rinv
    rinv_out[...] = jnp.broadcast_to(rinv, rinv_out.shape)
    target_out[...] = (s0[docs:] + s2[docs:]) + (s1[docs:] + s3[docs:])


def as_row(column):
    size = column.shape[0]
    same = lax.broadcasted_iota(jnp.int32, (size, size), 0) == lax.broadcasted_iota(jnp.int32, (size, size), 1)
    return jnp.sum(jnp.where(same, column, 0.0), axis=0, keepdims=True)


def score_kernel(docs, positive, e0, e1, e2, e3, t0, t1, t2, t3, everyone, state, expos):
    all_docs, width = everyone.shape
    dp, _ = here()
    y = dp & 3
    group = e0.shape[0]
    for k, piece in enumerate((e0, e1, e2, e3)):
        everyone[pl.ds(pl.multiple_of(((y + k) & 3) * group, group), group), :] = piece[...]
    tables = (t0, t1, t2, t3)
    rows = t0.shape[0]
    emb = thirds(everyone[...])
    scores = [folded(lax.dot_general(emb, t[...], NT, preferred_element_type=jnp.float32)) / TAU for t in tables]
    tops = [jnp.max(s, axis=1, keepdims=True) for s in scores]
    top = jnp.maximum(jnp.maximum(tops[0], tops[2]), jnp.maximum(tops[1], tops[3]))
    row = lax.broadcasted_iota(jnp.int32, (all_docs, rows), 0)
    wanted = jnp.zeros((all_docs, rows), jnp.int32)
    for doc in range(all_docs):
        z, rest = divmod(doc, all_docs // 2)
        wanted = jnp.where(row == rest // docs * group + z * docs + rest % docs, positive[doc], wanted)
    totals, found = [], jnp.zeros((all_docs, 1), jnp.float32)
    for k, s in enumerate(scores):
        expo = jnp.exp(s - top)
        expos[:, k * rows : (k + 1) * rows] = expo
        totals.append(jnp.sum(expo, axis=1, keepdims=True))
        hit = row_ids(k, (all_docs, rows), 1) == wanted
        found = found + jnp.sum(jnp.where(hit, s, 0.0), axis=1, keepdims=True)
    total = (totals[0] + totals[2]) + (totals[1] + totals[3])
    mine = thirds(expos[pl.ds(pl.multiple_of(y * group, group), group), :])
    mix = jnp.zeros((group, width), jnp.float32)
    for k, t in enumerate(tables):
        mix = mix + folded(jnp.dot(mine[:, k * rows : (k + 1) * rows], t[...], preferred_element_type=jnp.float32))
    column = lax.broadcasted_iota(jnp.int32, (group, all_docs), 1)
    own = column == lax.broadcasted_iota(jnp.int32, (group, all_docs), 0) + y * group
    total_row, top_row, found_row = as_row(total), as_row(top), as_row(found)
    state[...] = jnp.zeros_like(state)
    state[0:group, 0:width] = mix
    for place, values in ((width, total_row), (width + 128, top_row)):
        value = jnp.sum(jnp.where(own, values, 0.0), axis=1, keepdims=True)
        state[0:group, place : place + 128] = jnp.broadcast_to(value, (group, 128))
    for index, values in enumerate((total_row, top_row, found_row)):
        state[group + index : group + index + 1, 0:all_docs] = values


def merge(docs, width, states):
    row = lax.broadcasted_iota(jnp.int32, states[0].shape, 0)
    column = lax.broadcasted_iota(jnp.int32, states[0].shape, 1)
    place = width + 128
    by_row = [s[:, place : place + 1] for s in states]
    by_lane = [s[docs + 1 : docs + 2, :] for s in states]
    top_row = functools.reduce(jnp.maximum, by_row)
    top_lane = functools.reduce(jnp.maximum, by_lane)
    terms = [
        s * jnp.exp(jnp.where(row == docs, b - top_lane, a - top_row)) for s, a, b in zip(states, by_row, by_lane)
    ]
    if len(terms) == 4:
        terms = [terms[0] + terms[2], terms[1] + terms[3]]
    joined = jnp.where((row < docs) & (column >= place), top_row, terms[0] + terms[1])
    return jnp.where(row == docs + 1, top_lane, joined)


def batch_kernel(emb, everyone, product_out, stats):
    everything = everyone[...]
    all_docs = everything.shape[0]
    own = lax.dot_general(emb[...], everything, NT, precision=HIGHEST, preferred_element_type=jnp.float32) / TAU
    product = lax.dot_general(everything, everything, NT, precision=HIGHEST, preferred_element_type=jnp.float32) / TAU
    wide = (all_docs, all_docs)
    same = lax.broadcasted_iota(jnp.int32, wide, 0) == lax.broadcasted_iota(jnp.int32, wide, 1)
    product = jnp.where(same, -1e30, product)
    top = jnp.max(product, axis=0, keepdims=True)
    total = jnp.sum(jnp.exp(product - top), axis=0, keepdims=True)
    product_out[...] = own
    stats[...] = jnp.concatenate([top, total] * 4, axis=0)


def grad_kernel(
    lengths, s0, s1, s2, s3, emb, rinv, everyone, target, product, stats, gain, normed, rstd, turned,
    send_out, d_summed, loss_out,
):
    docs, tb, width = normed.shape
    all_docs, group = everyone.shape[0], emb.shape[0]
    dp, _ = here()
    mine = lambda a: jnp.where(dp >= 4, a[docs:group], a[0:docs])
    own, others = mine(emb), everyone[...]
    now = merge(group, width, [s[...] for s in (s0, s1, s2, s3)])
    total, top, found = (now[group + k : group + k + 1, 0:all_docs] for k in range(3))
    batch_top, batch_total = stats[0:1], stats[1:2]
    peak = jnp.maximum(top, batch_top)
    lse_row = peak + jnp.log(total * jnp.exp(top - peak) + batch_total * jnp.exp(batch_top - peak))
    loss_out[...] = jnp.broadcast_to(jnp.sum(lse_row - found, axis=1, keepdims=True) / all_docs, loss_out.shape)
    column = lax.broadcasted_iota(jnp.int32, (docs, all_docs), 1)
    first = (dp & 3) * group + (dp >> 2) * docs
    same = column == lax.broadcasted_iota(jnp.int32, (docs, all_docs), 0) + first
    lse = jnp.sum(jnp.where(same, lse_row, 0.0), axis=1, keepdims=True)
    scores = mine(product)
    g_batch = jnp.where(same, 0.0, jnp.exp(scores - lse) + jnp.exp(scores - lse_row)) / all_docs
    shares = mine(now)
    mix = shares[:, 0:width] * jnp.exp(shares[:, width + 128 : width + 129] - lse)
    from_batch = jnp.dot(g_batch, others, precision=HIGHEST, preferred_element_type=jnp.float32)
    d_emb = ((mix - mine(target)) / all_docs + from_batch) / TAU
    d_pooled = (d_emb - own * jnp.sum(own * d_emb, axis=1, keepdims=True)) * mine(rinv)[:, 0:1]
    for doc in range(docs):
        dy = d_pooled[doc : doc + 1] / lengths[doc].astype(jnp.float32) * gain[...].reshape(1, width)
        level = dy - jnp.mean(dy, axis=1, keepdims=True)
        unit = normed[doc].astype(jnp.float32)
        along = jnp.mean(unit * dy, axis=1, keepdims=True)
        keep = lax.axis_index("ctx") * tb + lax.broadcasted_iota(jnp.int32, (tb, 1), 0) < lengths[doc]
        scale = jnp.where(keep, rstd[doc, :, 0:1], 0.0)
        d_summed[doc * tb : (doc + 1) * tb, :] = (scale * (level - unit * along)).astype(jnp.bfloat16)
    send_out[...] = jnp.dot(turned[width // 2 :], d_summed[...], preferred_element_type=jnp.float32)


def keep_kernel(turned, d_summed, out):
    out[...] = jnp.dot(turned[0 : out.shape[0]], d_summed[...], preferred_element_type=jnp.float32)


def sum_kernel(count, *refs):
    terms, outs = refs[:count], refs[count:]
    total = terms[0][...].astype(jnp.float32)
    for term in terms[1:]:
        total = total + term[...].astype(jnp.float32)
    rows = outs[0].shape[0]
    for index, out in enumerate(outs):
        out[...] = total[index * rows : (index + 1) * rows].astype(out.dtype)


def sum_and_split(terms, kind):
    rows, width = terms[0].shape
    piece = (rows // 4, width)
    shapes = (f32(*piece),) + (jax.ShapeDtypeStruct(piece, kind),) * 3
    return call(
        functools.partial(sum_kernel, len(terms)), shapes, [VMEM] * len(terms), (VMEM,) * 4, limit=8, name="sum_split"
    )(*terms)


def shards(tokens, w_qkv, w_out, ln_gain, cache, positive, lengths):
    docs, tb, width = tokens.shape
    n_ctx, n_dp = lax.axis_size("ctx"), lax.axis_size("dp")
    all_docs = n_dp * docs
    fetch = lambda part: lax.ppermute(part, "ctx", [(i, (i + 2 * (i % 2) - 1) % n_ctx) for i in range(n_ctx)])
    far = [fetch(tokens[0])]
    near = swap(tokens, "ctx", 1)
    tables = around(cache, from_y)
    qk, v_turned, w_v_turned, *later = prepare(in_hbm(tokens), in_hbm(w_qkv))
    done, gain = None, ln_gain
    for doc in range(docs):
        if doc == 0:
            far.append(fetch(later[0]))
            far[0], late = lax.optimization_barrier((far[0], later[1]))
            far.append(fetch(late))
        elif doc + 2 < docs:
            *done, pool = done
            far[doc], late, pool = lax.optimization_barrier((far[doc], later[doc + 1], pool))
            done = [*done, pool]
            far.append(fetch(late))
        if doc == 2:
            *done, pool = done
            pool, after = lax.optimization_barrier((pool, positive))
            done = [*done, pool]
            target = call(
                functools.partial(target_kernel, docs), f32(2 * docs, width), [SMEM] + [VMEM] * 4, VMEM, name="target"
            )(after, *tables)
            far[doc], target = lax.optimization_barrier((far[doc], target))
        done = attend(doc, done, lengths, tokens, near, far[doc], qk, v_turned, w_qkv, w_v_turned, w_out, gain)
    hidden, mixed, normed, rstd, pool = done

    turned = call(
        turn_kernel,
        bf16(width, docs * tb),
        [VMEM],
        VMEM,
        flops=2 * docs * tb * width * width,
        moved=4 * 2**20,
        name="turn",
    )(mixed)

    group = 2 * docs
    sums = call(stack_kernel, f32(docs + group, width), [VMEM, VMEM], VMEM, limit=4, name="stack")(
        pool, target
    )
    sums = add([sums, swap(sums, "ctx", 1)])
    sums = add(around(sums, from_x))
    emb, rinv, target = call(
        norm_kernel,
        (f32(group, width), f32(group, 128), f32(group, width)),
        [VMEM] * 4,
        (VMEM,) * 3,
        limit=4,
        name="norm",
    )(*around(sums, from_z))
    embs = around(emb, from_y)
    everyone, state = call(
        functools.partial(score_kernel, docs),
        (f32(all_docs, width), f32(2 * group, width + 256)),
        [SMEM] + [VMEM] * 8,
        (VMEM, VMEM),
        moved=2 * 2**20,
        scratch_shapes=[pltpu.VMEM((all_docs, n_dp * cache.shape[0]), jnp.float32)],
        name="score",
    )(positive, *embs, *tables)
    product, stats = call(
        batch_kernel,
        (f32(group, all_docs), f32(8, all_docs)),
        [VMEM, VMEM],
        (VMEM, VMEM),
        limit=4,
        name="batch",
    )(emb, everyone)
    state = merged(group, width, [state, swap(state, "ctx", 1)])
    state = merged(group, width, around(state, from_x))
    half = width // 2
    send, d_summed, loss = call(
        grad_kernel,
        (f32(half, width), bf16(docs * tb, width), f32(8, 128)),
        [SMEM] + [VMEM] * 14,
        (VMEM,) * 3,
        flops=docs * tb * width * width,
        moved=8 * 2**20,
        name="grad",
    )(
        lengths, *around(state, from_z), emb, rinv, everyone, target, product, stats, gain, normed, rstd, turned,
    )
    keep = call(
        keep_kernel,
        f32(half, width),
        [VMEM, VMEM],
        VMEM,
        flops=docs * tb * width * width,
        moved=2**20,
        name="keep",
    )(turned, d_summed)
    keep, *sends = sum_and_split([keep, swap(send, "ctx", 1)], jnp.bfloat16)
    got = [from_plane(piece, -(k + 1), False) for k, piece in enumerate(sends)]
    keep, *sends = sum_and_split([keep] + got, jnp.float32)
    got = [from_plane(piece, -(k + 1), True) for k, piece in enumerate(sends)]
    keep, *sends = sum_and_split([keep] + got, jnp.float32)
    got = [from_z(piece, -(k + 1)) for k, piece in enumerate(sends)]
    return (hidden, loss[0, 0], add([keep] + got))


def solution(mesh):
    placed = (P("dp", "ctx", None), P(), P(), P(), P(("dp", "ctx"), None), P(), P("dp"))
    return jax.shard_map(
        shards,
        mesh=mesh,
        in_specs=placed,
        out_specs=(P("dp", "ctx", None), P(), P(("dp", "ctx"), None)),
        check_vma=False,
    )
```

```python
import functools
import math

import jax
import jax.numpy as jnp
from jax import lax
from jax.experimental import pallas as pl
from jax.experimental.pallas import tpu as pltpu
from jax.sharding import PartitionSpec as P

H = 12
WIN = 256
TAU = 0.02
FAR = 1e32
NT = (((1,), (1,)), ((), ()))
TN = (((0,), (0,)), ((), ()))
HIGHEST = lax.Precision.HIGHEST
VMEM = pl.BlockSpec(memory_space=pltpu.VMEM)
SMEM = pl.BlockSpec(memory_space=pltpu.SMEM)
ANY = pl.BlockSpec(memory_space=pl.ANY)


def swap(value, axis, bits):
    return lax.ppermute(value, axis, [(i, i ^ bits) for i in range(lax.axis_size(axis))])


def from_x(value, k):
    size = lax.axis_size("ctx")
    return lax.ppermute(value, "ctx", [((c + 4 * k) % size, c) for c in range(size)])


def from_y(value, k):
    return lax.ppermute(value, "dp", [((d & 4) | ((d + k) & 3), d) for d in range(lax.axis_size("dp"))])


def from_z(value, k):
    n_dp, n_ctx = lax.axis_size("dp"), lax.axis_size("ctx")
    pairs = []
    for d in range(n_dp):
        for c in range(n_ctx):
            z = ((c & 2) + (d >> 2) + k) & 3
            pairs.append((((z & 1) * 4 + (d & 3)) * n_ctx + (c & ~2) + (z & 2), d * n_ctx + c))
    return lax.ppermute(value, ("dp", "ctx"), pairs)


def from_plane(value, k, last):
    n_dp, n_ctx = lax.axis_size("dp"), lax.axis_size("ctx")
    pairs = []
    for d in range(n_dp):
        for c in range(n_ctx):
            along_y = (c & 1 == 1) == last
            source = ((d & 4) | ((d + k) & 3), c) if along_y else (d, (c + 4 * k) % n_ctx)
            pairs.append((source[0] * n_ctx + source[1], d * n_ctx + c))
    return lax.ppermute(value, ("dp", "ctx"), pairs)


def around(value, fetch):
    return [value] + [fetch(value, k) for k in (1, 2, 3)]


def here():
    return lax.axis_index("dp"), lax.axis_index("ctx")


def in_hbm(value):
    return pltpu.with_memory_space_constraint(value, pltpu.HBM)


def call(kernel, out_shape, in_specs, out_specs, limit=16, flops=0, moved=0, **keywords):
    return pl.pallas_call(
        kernel,
        out_shape=out_shape,
        in_specs=in_specs,
        out_specs=out_specs,
        compiler_params=pltpu.CompilerParams(vmem_limit_bytes=limit * 2**20),
        cost_estimate=pl.CostEstimate(flops=flops, bytes_accessed=moved, transcendentals=0),
        **keywords,
    )


def f32(*shape):
    return jax.ShapeDtypeStruct(shape, jnp.float32)


def bf16(*shape):
    return jax.ShapeDtypeStruct(shape, jnp.bfloat16)


def slopes_of(heads):
    largest = 2 ** int(math.floor(math.log2(heads)))
    listed = [2.0 ** (-8.0 * (h + 1) / largest) for h in range(largest)]
    return listed + [2.0 ** (-4.0 * (2 * m + 1) / largest) for m in range(heads - largest)]


def thirds(value):
    high = value.astype(jnp.bfloat16)
    rest = value - high.astype(jnp.float32)
    middle = rest.astype(jnp.bfloat16)
    low = (rest - middle.astype(jnp.float32)).astype(jnp.bfloat16)
    parts = [p.astype(jnp.float32) for p in (high, middle, low)]
    return jnp.concatenate(parts, axis=0).astype(jnp.bfloat16)


def folded(products):
    rows = products.shape[0] // 3
    return products[0:rows] + products[rows : 2 * rows] + products[2 * rows :]


def attend_kernel(first, *refs):
    far = refs[3]
    lax.fori_loop(0, far.shape[0], lambda index, _: attend_doc(first + index, index, *refs), None)


def attend_doc(
    doc, index, lengths, tok, near, far, qk, v_turned, w, w_v_turned, w_out, gain, *refs
):
    hidden, mixed_all, normed, rstd_out, pool, keys, values, dist, hidden_here, sem = refs[-10:]
    docs, tb, width = tok.shape
    ext = tb + 2 * WIN
    own = pl.ds(pl.multiple_of(doc * tb, tb), tb)
    mixed = mixed_all.at[:, own]
    ctx = lax.axis_index("ctx")
    start, length = ctx * tb, lengths[doc]
    right = lax.rem(ctx, 2) == 0
    ends = far[index], near[doc]
    rows = jnp.concatenate([jnp.where(right, *ends), jnp.where(right, *ends[::-1])], axis=0)
    new = jnp.dot(rows, w[:, width : 2 * width], preferred_element_type=jnp.float32).astype(jnp.bfloat16)
    keys[0:WIN] = new[0:WIN]
    keys[WIN : WIN + tb] = qk[doc, :, width:]
    keys[WIN + tb :] = new[WIN:]
    new = lax.dot_general(w_v_turned[...], rows, NT, preferred_element_type=jnp.float32).astype(jnp.bfloat16)
    values[:, 0:WIN] = new[:, 0:WIN]
    values[:, WIN : WIN + tb] = v_turned[:, own]
    values[:, WIN + tb :] = new[:, WIN:]
    j = lax.broadcasted_iota(jnp.int32, (ext, tb), 0) - WIN
    away = jnp.abs(lax.broadcasted_iota(jnp.int32, (ext, tb), 1) - j)
    kpos = start + j
    seen = (away <= WIN) & (((kpos >= 0) & (kpos < length)) | (away == 0))
    dist[...] = jnp.where(seen, away.astype(jnp.float32), FAR)
    half = lax.broadcasted_iota(jnp.int32, (tb, 128), 1) < 64
    slopes = slopes_of(H)
    lanes = 128
    span = lanes + 2 * WIN

    def scores_of(pair):
        cols = pl.ds(pair * 128, 128)
        query, zero = qk[doc, :, cols] * jnp.bfloat16(0.125), jnp.bfloat16(0)
        both = jnp.concatenate([jnp.where(half, query, zero), jnp.where(half, zero, query)], axis=0)
        return lax.dot_general(keys[:, cols], both, NT, preferred_element_type=jnp.float32)

    upcoming = scores_of(0)
    for pair in range(H // 2):
        scores = upcoming
        if pair + 1 < H // 2:
            upcoming = scores_of(pair + 1)
        for part in range(2):
            columns = []
            for low in range(0, tb, lanes):
                score = scores[low : low + span, part * tb + low : part * tb + low + lanes]
                score = score - slopes[2 * pair + part] * dist[pl.ds(low, span), pl.ds(low, lanes)]
                expo = jnp.exp(score - jnp.max(score, axis=0, keepdims=True))
                weights = (expo * (1.0 / jnp.sum(expo, axis=0, keepdims=True))).astype(jnp.bfloat16)
                above, below = low, ext - span - low
                pieces = [weights]
                if above:
                    pieces = [jnp.zeros((above, lanes), jnp.bfloat16)] + pieces
                if below:
                    pieces = pieces + [jnp.zeros((below, lanes), jnp.bfloat16)]
                columns.append(jnp.concatenate(pieces, axis=0))
            weights = jnp.concatenate(columns, axis=1)
            head = pl.ds(pair * 128 + part * 64, 64)
            mixed[head, :] = jnp.dot(values[head, :], weights, preferred_element_type=jnp.float32).astype(jnp.bfloat16)
    summed = tok[doc].astype(jnp.float32) + lax.dot_general(
        mixed[...], w_out[...], TN, preferred_element_type=jnp.float32
    )
    centred = summed - jnp.mean(summed, axis=1, keepdims=True)
    rstd = lax.rsqrt(jnp.mean(centred * centred, axis=1, keepdims=True) + 1e-05)
    unit = centred * rstd
    hidden_f = unit * gain[...].reshape(1, width)
    hidden_here[...] = hidden_f.astype(jnp.bfloat16)
    leaving = pltpu.make_async_copy(hidden_here, hidden.at[doc], sem)
    leaving.start()
    normed[doc] = unit.astype(jnp.bfloat16)
    rstd_out[doc] = jnp.broadcast_to(rstd, rstd_out.shape[1:])
    keep = start + lax.broadcasted_iota(jnp.int32, (tb, 1), 0) < length
    pool[doc] = jnp.sum(jnp.where(keep, hidden_f, 0.0), axis=0, keepdims=True) / length.astype(jnp.float32)
    leaving.wait()


def attend(first, before, lengths, tokens, near, far, qk, v_turned, w_qkv, w_v_turned, w_out, gain):
    docs, tb, width = tokens.shape
    ext = tb + 2 * WIN
    out_shape = (bf16(docs, tb, width), bf16(width, docs * tb), bf16(docs, tb, width), f32(docs, tb, 128), f32(docs, 1, width))
    out_specs = (ANY,) + (VMEM,) * 4
    operands = [lengths, tokens, near, far, qk, v_turned, w_qkv, w_v_turned, w_out, gain]
    in_specs = [SMEM] + [VMEM] * 9
    aliases = {}
    if before is not None:
        aliases = {len(operands) + k: k for k in range(len(out_shape))}
        operands = operands + list(before)
        in_specs = in_specs + list(out_specs)
    return call(
        functools.partial(attend_kernel, first),
        out_shape,
        in_specs,
        out_specs,
        limit=24,
        flops=5 * 2 * far.shape[0] * tb * ext * width,
        moved=4 * 2**20,
        scratch_shapes=[
            pltpu.VMEM((ext, width), jnp.bfloat16),
            pltpu.VMEM((width, ext), jnp.bfloat16),
            pltpu.VMEM((ext, tb), jnp.float32),
            pltpu.VMEM((tb, width), jnp.bfloat16),
            pltpu.SemaphoreType.DMA,
        ],
        input_output_aliases=aliases,
        name="attend",
    )(*operands)


def prepare_kernel(tok, w, qk, v_turned, w_v_turned, *later):
    width = tok.shape[2]
    for index, late in enumerate(later):

        @pl.when(pl.program_id(0) == index + 2)
        def _():
            late[...] = tok[...]

    @pl.when(pl.program_id(0) == 0)
    def _():
        w_v_turned[...] = w[:, 2 * width :].T

    rows = tok[0]
    qk[0] = jnp.dot(rows, w[:, 0 : 2 * width], preferred_element_type=jnp.float32).astype(jnp.bfloat16)
    v_turned[...] = lax.dot_general(w_v_turned[...], rows, NT, preferred_element_type=jnp.float32).astype(jnp.bfloat16)


def prepare(tokens, w_qkv):
    docs, tb, width = tokens.shape
    return call(
        prepare_kernel,
        (bf16(docs, tb, 2 * width), bf16(width, docs * tb), bf16(width, width)) + (bf16(1, tb, width),) * (docs - 2),
        [
            pl.BlockSpec((1, tb, width), lambda i: (i, 0, 0)),
            pl.BlockSpec(w_qkv.shape, lambda i: (0, 0), pipeline_mode=pl.Buffered(1)),
        ],
        (
            pl.BlockSpec((1, tb, 2 * width), lambda i: (i, 0, 0)),
            pl.BlockSpec((width, tb), lambda i: (0, i)),
            pl.BlockSpec((width, width), lambda i: (0, 0)),
        )
        + (pl.BlockSpec((1, tb, width), lambda i: (0, 0, 0)),) * (docs - 2),
        flops=2 * docs * tb * width * 3 * width,
        moved=11 * 2**20,
        grid=(docs,),
        name="prepare",
    )(tokens, w_qkv)


def row_ids(k, shape, dim):
    dp, ctx = here()
    place = lax.broadcasted_iota(jnp.int32, shape, dim)
    return (((dp & 4) | ((dp + k) & 3)) * 16 + ctx) * shape[dim] + place


def stack_kernel(pool, target, out):
    docs = pool.shape[0]
    for doc in range(docs):
        out[doc : doc + 1, :] = pool[doc]
    out[docs:, :] = target[...]


def add_kernel(*refs):
    terms = [ref[...] for ref in refs[:-1]]
    if len(terms) == 4:
        terms = [terms[0] + terms[2], terms[1] + terms[3]]
    refs[-1][...] = terms[0] + terms[1]


def add(terms):
    return call(add_kernel, f32(*terms[0].shape), [VMEM] * len(terms), VMEM, limit=4, name="add")(*terms)


def merge_kernel(docs, width, *refs):
    refs[-1][...] = merge(docs, width, [ref[...] for ref in refs[:-1]])


def merged(docs, width, states):
    kernel = functools.partial(merge_kernel, docs, width)
    return call(kernel, f32(*states[0].shape), [VMEM] * len(states), VMEM, limit=4, name="merge")(*states)


def target_kernel(docs, positive, *refs):
    pieces, out = refs[:4], refs[4]
    dp, _ = here()
    total = jnp.zeros(out.shape, jnp.float32)
    for k, piece in enumerate(pieces):
        shape = (out.shape[0], piece.shape[0])
        doc = lax.broadcasted_iota(jnp.int32, shape, 0)
        wanted = jnp.zeros(shape, jnp.int32)
        for d in range(2 * docs):
            wanted = jnp.where(doc == d, positive[(d // docs * 4 + (dp & 3)) * docs + d % docs], wanted)
        hit = (row_ids(k, shape, 1) == wanted).astype(jnp.float32).astype(jnp.bfloat16)
        total = total + jnp.dot(hit, piece[...], preferred_element_type=jnp.float32)
    out[...] = total


def turn_kernel(mixed, out):
    width = out.shape[0]
    rows = 128
    lax.fori_loop(0, width // rows, lambda index, _: turn_rows(index * rows, rows, mixed, out), None)


def turn_rows(low, rows, mixed, out):
    width = out.shape[0]
    place = low + lax.broadcasted_iota(jnp.int32, (rows, 1), 0)
    dp, ctx = here()
    each = width // 128
    core = (ctx & 1) ^ (place // (64 * each))
    first, second = place // (16 * each) % 4, place // (4 * each) % 4
    y = ((dp & 3) + jnp.where(core == 0, first, second)) & 3
    x = ((ctx >> 2) + jnp.where(core == 0, second, first)) & 3
    z = ((ctx & 2) + (dp >> 2) + place // each % 4) & 3
    block = ((z & 1) * 4 + y) * 16 + x * 4 + (z >> 1) * 2 + core
    chosen = block * each + place % each == lax.broadcasted_iota(jnp.int32, (rows, width), 1)
    chosen = jnp.where(chosen, 1.0, 0.0).astype(jnp.bfloat16)
    here_rows = pl.ds(pl.multiple_of(low, rows), rows)
    out[here_rows, :] = jnp.dot(chosen, mixed[...], preferred_element_type=jnp.float32).astype(jnp.bfloat16)


def norm_kernel(s0, s1, s2, s3, emb_out, rinv_out, target_out):
    docs = s0.shape[0] // 3
    dp, _ = here()
    own, other = s0[0:docs] + s2[0:docs], s1[0:docs] + s3[0:docs]
    second = dp >= 4
    pooled = jnp.concatenate([jnp.where(second, other, own), jnp.where(second, own, other)], axis=0)
    rinv = lax.rsqrt(jnp.sum(pooled * pooled, axis=1, keepdims=True) + 1e-06)
    emb_out[...] = pooled * rinv
    rinv_out[...] = jnp.broadcast_to(rinv, rinv_out.shape)
    target_out[...] = (s0[docs:] + s2[docs:]) + (s1[docs:] + s3[docs:])


def as_row(column):
    size = column.shape[0]
    same = lax.broadcasted_iota(jnp.int32, (size, size), 0) == lax.broadcasted_iota(jnp.int32, (size, size), 1)
    return jnp.sum(jnp.where(same, column, 0.0), axis=0, keepdims=True)


def score_kernel(docs, positive, e0, e1, e2, e3, t0, t1, t2, t3, everyone, state, expos):
    all_docs, width = everyone.shape
    dp, _ = here()
    y = dp & 3
    group = e0.shape[0]
    for k, piece in enumerate((e0, e1, e2, e3)):
        everyone[pl.ds(pl.multiple_of(((y + k) & 3) * group, group), group), :] = piece[...]
    tables = (t0, t1, t2, t3)
    rows = t0.shape[0]
    emb = thirds(everyone[...])
    scores = [folded(lax.dot_general(emb, t[...], NT, preferred_element_type=jnp.float32)) / TAU for t in tables]
    tops = [jnp.max(s, axis=1, keepdims=True) for s in scores]
    top = jnp.maximum(jnp.maximum(tops[0], tops[2]), jnp.maximum(tops[1], tops[3]))
    row = lax.broadcasted_iota(jnp.int32, (all_docs, rows), 0)
    wanted = jnp.zeros((all_docs, rows), jnp.int32)
    for doc in range(all_docs):
        z, rest = divmod(doc, all_docs // 2)
        wanted = jnp.where(row == rest // docs * group + z * docs + rest % docs, positive[doc], wanted)
    totals, found = [], jnp.zeros((all_docs, 1), jnp.float32)
    for k, s in enumerate(scores):
        expo = jnp.exp(s - top)
        expos[:, k * rows : (k + 1) * rows] = expo
        totals.append(jnp.sum(expo, axis=1, keepdims=True))
        hit = row_ids(k, (all_docs, rows), 1) == wanted
        found = found + jnp.sum(jnp.where(hit, s, 0.0), axis=1, keepdims=True)
    total = (totals[0] + totals[2]) + (totals[1] + totals[3])
    mine = thirds(expos[pl.ds(pl.multiple_of(y * group, group), group), :])
    mix = jnp.zeros((group, width), jnp.float32)
    for k, t in enumerate(tables):
        mix = mix + folded(jnp.dot(mine[:, k * rows : (k + 1) * rows], t[...], preferred_element_type=jnp.float32))
    column = lax.broadcasted_iota(jnp.int32, (group, all_docs), 1)
    own = column == lax.broadcasted_iota(jnp.int32, (group, all_docs), 0) + y * group
    total_row, top_row, found_row = as_row(total), as_row(top), as_row(found)
    state[...] = jnp.zeros_like(state)
    state[0:group, 0:width] = mix
    for place, values in ((width, total_row), (width + 128, top_row)):
        value = jnp.sum(jnp.where(own, values, 0.0), axis=1, keepdims=True)
        state[0:group, place : place + 128] = jnp.broadcast_to(value, (group, 128))
    for index, values in enumerate((total_row, top_row, found_row)):
        state[group + index : group + index + 1, 0:all_docs] = values


def merge(docs, width, states):
    row = lax.broadcasted_iota(jnp.int32, states[0].shape, 0)
    column = lax.broadcasted_iota(jnp.int32, states[0].shape, 1)
    place = width + 128
    by_row = [s[:, place : place + 1] for s in states]
    by_lane = [s[docs + 1 : docs + 2, :] for s in states]
    top_row = functools.reduce(jnp.maximum, by_row)
    top_lane = functools.reduce(jnp.maximum, by_lane)
    terms = [
        s * jnp.exp(jnp.where(row == docs, b - top_lane, a - top_row)) for s, a, b in zip(states, by_row, by_lane)
    ]
    if len(terms) == 4:
        terms = [terms[0] + terms[2], terms[1] + terms[3]]
    joined = jnp.where((row < docs) & (column >= place), top_row, terms[0] + terms[1])
    return jnp.where(row == docs + 1, top_lane, joined)


def batch_kernel(emb, everyone, product_out, stats):
    everything = everyone[...]
    all_docs = everything.shape[0]
    own = lax.dot_general(emb[...], everything, NT, precision=HIGHEST, preferred_element_type=jnp.float32) / TAU
    product = lax.dot_general(everything, everything, NT, precision=HIGHEST, preferred_element_type=jnp.float32) / TAU
    wide = (all_docs, all_docs)
    same = lax.broadcasted_iota(jnp.int32, wide, 0) == lax.broadcasted_iota(jnp.int32, wide, 1)
    product = jnp.where(same, -1e30, product)
    top = jnp.max(product, axis=0, keepdims=True)
    total = jnp.sum(jnp.exp(product - top), axis=0, keepdims=True)
    product_out[...] = own
    stats[...] = jnp.concatenate([top, total] * 4, axis=0)


def grad_kernel(
    lengths, s0, s1, s2, s3, emb, rinv, everyone, target, product, stats, gain, normed, rstd, turned,
    send_out, d_summed, loss_out,
):
    docs, tb, width = normed.shape
    all_docs, group = everyone.shape[0], emb.shape[0]
    dp, _ = here()
    mine = lambda a: jnp.where(dp >= 4, a[docs:group], a[0:docs])
    own, others = mine(emb), everyone[...]
    now = merge(group, width, [s[...] for s in (s0, s1, s2, s3)])
    total, top, found = (now[group + k : group + k + 1, 0:all_docs] for k in range(3))
    batch_top, batch_total = stats[0:1], stats[1:2]
    peak = jnp.maximum(top, batch_top)
    lse_row = peak + jnp.log(total * jnp.exp(top - peak) + batch_total * jnp.exp(batch_top - peak))
    loss_out[...] = jnp.broadcast_to(jnp.sum(lse_row - found, axis=1, keepdims=True) / all_docs, loss_out.shape)
    column = lax.broadcasted_iota(jnp.int32, (docs, all_docs), 1)
    first = (dp & 3) * group + (dp >> 2) * docs
    same = column == lax.broadcasted_iota(jnp.int32, (docs, all_docs), 0) + first
    lse = jnp.sum(jnp.where(same, lse_row, 0.0), axis=1, keepdims=True)
    scores = mine(product)
    g_batch = jnp.where(same, 0.0, jnp.exp(scores - lse) + jnp.exp(scores - lse_row)) / all_docs
    shares = mine(now)
    mix = shares[:, 0:width] * jnp.exp(shares[:, width + 128 : width + 129] - lse)
    from_batch = jnp.dot(g_batch, others, precision=HIGHEST, preferred_element_type=jnp.float32)
    d_emb = ((mix - mine(target)) / all_docs + from_batch) / TAU
    d_pooled = (d_emb - own * jnp.sum(own * d_emb, axis=1, keepdims=True)) * mine(rinv)[:, 0:1]
    for doc in range(docs):
        dy = d_pooled[doc : doc + 1] / lengths[doc].astype(jnp.float32) * gain[...].reshape(1, width)
        level = dy - jnp.mean(dy, axis=1, keepdims=True)
        unit = normed[doc].astype(jnp.float32)
        along = jnp.mean(unit * dy, axis=1, keepdims=True)
        keep = lax.axis_index("ctx") * tb + lax.broadcasted_iota(jnp.int32, (tb, 1), 0) < lengths[doc]
        scale = jnp.where(keep, rstd[doc, :, 0:1], 0.0)
        d_summed[doc * tb : (doc + 1) * tb, :] = (scale * (level - unit * along)).astype(jnp.bfloat16)
    product_rows(turned, width // 2, d_summed, send_out)


def product_rows(turned, low, d_summed, out):
    rows = 128

    def some(index, _):
        source = pl.ds(pl.multiple_of(low + index * rows, rows), rows)
        here_rows = pl.ds(pl.multiple_of(index * rows, rows), rows)
        out[here_rows, :] = jnp.dot(turned[source, :], d_summed[...], preferred_element_type=jnp.float32)

    lax.fori_loop(0, out.shape[0] // rows, some, None)


def keep_kernel(turned, d_summed, out):
    product_rows(turned, 0, d_summed, out)


def sum_kernel(count, *refs):
    terms, outs = refs[:count], refs[count:]
    total = terms[0][...].astype(jnp.float32)
    for term in terms[1:]:
        total = total + term[...].astype(jnp.float32)
    rows = outs[0].shape[0]
    for index, out in enumerate(outs):
        out[...] = total[index * rows : (index + 1) * rows].astype(out.dtype)


def sum_and_split(terms, kind):
    rows, width = terms[0].shape
    piece = (rows // 4, width)
    shapes = (f32(*piece),) + (jax.ShapeDtypeStruct(piece, kind),) * 3
    return call(
        functools.partial(sum_kernel, len(terms)), shapes, [VMEM] * len(terms), (VMEM,) * 4, limit=8, name="sum_split"
    )(*terms)


def shards(tokens, w_qkv, w_out, ln_gain, cache, positive, lengths):
    docs, tb, width = tokens.shape
    n_ctx, n_dp = lax.axis_size("ctx"), lax.axis_size("dp")
    all_docs = n_dp * docs
    ring = [(i, (i + 2 * (i % 2) - 1) % n_ctx) for i in range(n_ctx)]
    fetch = lambda part: lax.ppermute(part, "ctx", ring)
    early = fetch(tokens[0:2])
    near = swap(tokens, "ctx", 1)
    tables = around(cache, from_y)
    qk, v_turned, w_v_turned, third, fourth = prepare(in_hbm(tokens), in_hbm(w_qkv))
    target = call(
        functools.partial(target_kernel, docs), f32(2 * docs, width), [SMEM] + [VMEM] * 4, VMEM, name="target"
    )(positive, *tables)
    early, third = lax.optimization_barrier((early, third))
    third = fetch(third)
    early, target = lax.optimization_barrier((early, target))
    gain = ln_gain
    fixed = (lengths, tokens, near), (qk, v_turned, w_qkv, w_v_turned, w_out, gain)
    *done, pool = attend(0, None, *fixed[0], early, *fixed[1])
    pool, fourth = lax.optimization_barrier((pool, fourth))
    fourth = fetch(fourth)
    done = attend(2, [*done, pool], *fixed[0], third, *fixed[1])
    done = attend(3, done, *fixed[0], fourth, *fixed[1])
    hidden, mixed, normed, rstd, pool = done

    turned = call(
        turn_kernel,
        bf16(width, docs * tb),
        [VMEM],
        VMEM,
        flops=2 * docs * tb * width * width,
        moved=4 * 2**20,
        name="turn",
    )(mixed)

    group = 2 * docs
    sums = call(stack_kernel, f32(docs + group, width), [VMEM, VMEM], VMEM, limit=4, name="stack")(
        pool, target
    )
    sums = add([sums, swap(sums, "ctx", 1)])
    sums = add(around(sums, from_x))
    emb, rinv, target = call(
        norm_kernel,
        (f32(group, width), f32(group, 128), f32(group, width)),
        [VMEM] * 4,
        (VMEM,) * 3,
        limit=4,
        name="norm",
    )(*around(sums, from_z))
    embs = around(emb, from_y)
    everyone, state = call(
        functools.partial(score_kernel, docs),
        (f32(all_docs, width), f32(2 * group, width + 256)),
        [SMEM] + [VMEM] * 8,
        (VMEM, VMEM),
        moved=2 * 2**20,
        scratch_shapes=[pltpu.VMEM((all_docs, n_dp * cache.shape[0]), jnp.float32)],
        name="score",
    )(positive, *embs, *tables)
    product, stats = call(
        batch_kernel,
        (f32(group, all_docs), f32(8, all_docs)),
        [VMEM, VMEM],
        (VMEM, VMEM),
        limit=4,
        name="batch",
    )(emb, everyone)
    state = merged(group, width, [state, swap(state, "ctx", 1)])
    state = merged(group, width, around(state, from_x))
    half = width // 2
    send, d_summed, loss = call(
        grad_kernel,
        (f32(half, width), bf16(docs * tb, width), f32(8, 128)),
        [SMEM] + [VMEM] * 14,
        (VMEM,) * 3,
        flops=docs * tb * width * width,
        moved=8 * 2**20,
        name="grad",
    )(
        lengths, *around(state, from_z), emb, rinv, everyone, target, product, stats, gain, normed, rstd, turned,
    )
    keep = call(
        keep_kernel,
        f32(half, width),
        [VMEM, VMEM],
        VMEM,
        flops=docs * tb * width * width,
        moved=2**20,
        name="keep",
    )(turned, d_summed)
    keep, *sends = sum_and_split([keep, swap(send, "ctx", 1)], jnp.bfloat16)
    got = [from_plane(piece, -(k + 1), False) for k, piece in enumerate(sends)]
    keep, *sends = sum_and_split([keep] + got, jnp.float32)
    got = [from_plane(piece, -(k + 1), True) for k, piece in enumerate(sends)]
    keep, *sends = sum_and_split([keep] + got, jnp.float32)
    got = [from_z(piece, -(k + 1)) for k, piece in enumerate(sends)]
    return (hidden, loss[0, 0], add([keep] + got))


def solution(mesh):
    placed = (P("dp", "ctx", None), P(), P(), P(), P(("dp", "ctx"), None), P(), P("dp"))
    return jax.shard_map(
        shards,
        mesh=mesh,
        in_specs=placed,
        out_specs=(P("dp", "ctx", None), P(), P(("dp", "ctx"), None)),
        check_vma=False,
    )
```

```python
import functools
import math

import jax
import jax.numpy as jnp
from jax import lax
from jax.experimental import pallas as pl
from jax.experimental.pallas import tpu as pltpu
from jax.sharding import PartitionSpec as P

H = 12
WIN = 256
TAU = 0.02
FAR = 1e32
NT = (((1,), (1,)), ((), ()))
TN = (((0,), (0,)), ((), ()))
HIGHEST = lax.Precision.HIGHEST
VMEM = pl.BlockSpec(memory_space=pltpu.VMEM)
SMEM = pl.BlockSpec(memory_space=pltpu.SMEM)
ANY = pl.BlockSpec(memory_space=pl.ANY)


def swap(value, axis, bits):
    return lax.ppermute(value, axis, [(i, i ^ bits) for i in range(lax.axis_size(axis))])


def from_x(value, k):
    size = lax.axis_size("ctx")
    return lax.ppermute(value, "ctx", [((c + 4 * k) % size, c) for c in range(size)])


def from_y(value, k):
    return lax.ppermute(value, "dp", [((d & 4) | ((d + k) & 3), d) for d in range(lax.axis_size("dp"))])


def from_z(value, k):
    n_dp, n_ctx = lax.axis_size("dp"), lax.axis_size("ctx")
    pairs = []
    for d in range(n_dp):
        for c in range(n_ctx):
            z = ((c & 2) + (d >> 2) + k) & 3
            pairs.append((((z & 1) * 4 + (d & 3)) * n_ctx + (c & ~2) + (z & 2), d * n_ctx + c))
    return lax.ppermute(value, ("dp", "ctx"), pairs)


def from_plane(value, k, last):
    n_dp, n_ctx = lax.axis_size("dp"), lax.axis_size("ctx")
    pairs = []
    for d in range(n_dp):
        for c in range(n_ctx):
            along_y = (c & 1 == 1) == last
            source = ((d & 4) | ((d + k) & 3), c) if along_y else (d, (c + 4 * k) % n_ctx)
            pairs.append((source[0] * n_ctx + source[1], d * n_ctx + c))
    return lax.ppermute(value, ("dp", "ctx"), pairs)


def around(value, fetch):
    return [value] + [fetch(value, k) for k in (1, 2, 3)]


def here():
    return lax.axis_index("dp"), lax.axis_index("ctx")


def in_hbm(value):
    return pltpu.with_memory_space_constraint(value, pltpu.HBM)


def call(kernel, out_shape, in_specs, out_specs, limit=16, flops=0, moved=0, **keywords):
    return pl.pallas_call(
        kernel,
        out_shape=out_shape,
        in_specs=in_specs,
        out_specs=out_specs,
        compiler_params=pltpu.CompilerParams(vmem_limit_bytes=limit * 2**20),
        cost_estimate=pl.CostEstimate(flops=flops, bytes_accessed=moved, transcendentals=0),
        **keywords,
    )


def f32(*shape):
    return jax.ShapeDtypeStruct(shape, jnp.float32)


def bf16(*shape):
    return jax.ShapeDtypeStruct(shape, jnp.bfloat16)


def slopes_of(heads):
    largest = 2 ** int(math.floor(math.log2(heads)))
    listed = [2.0 ** (-8.0 * (h + 1) / largest) for h in range(largest)]
    return listed + [2.0 ** (-4.0 * (2 * m + 1) / largest) for m in range(heads - largest)]


def thirds(value):
    high = value.astype(jnp.bfloat16)
    rest = value - high.astype(jnp.float32)
    middle = rest.astype(jnp.bfloat16)
    low = (rest - middle.astype(jnp.float32)).astype(jnp.bfloat16)
    parts = [p.astype(jnp.float32) for p in (high, middle, low)]
    return jnp.concatenate(parts, axis=0).astype(jnp.bfloat16)


def folded(products):
    rows = products.shape[0] // 3
    return products[0:rows] + products[rows : 2 * rows] + products[2 * rows :]


def attend_kernel(first, *refs):
    far = refs[3]
    lax.fori_loop(0, far.shape[0], lambda index, _: attend_doc(first + index, index, *refs), None)


def attend_doc(
    doc, index, lengths, tok, near_k, far, near_v, qk, v_turned, w, w_v_turned, w_out, gain, *refs
):
    hidden, mixed_all, normed, rstd_out, pool, keys, values, dist, hidden_here, sem = refs[-10:]
    docs, tb, width = tok.shape
    ext = tb + 2 * WIN
    own = pl.ds(pl.multiple_of(doc * tb, tb), tb)
    mixed = mixed_all.at[:, own]
    ctx = lax.axis_index("ctx")
    start, length = ctx * tb, lengths[doc]
    odd = lax.rem(ctx, 2)
    near_at = pl.ds(pl.multiple_of((1 - odd) * (WIN + tb), 128), WIN)
    far_at = pl.ds(pl.multiple_of(odd * (WIN + tb), 128), WIN)
    rows = far[index]
    keys[far_at, :] = jnp.dot(
        rows, w[:, width : 2 * width], preferred_element_type=jnp.float32
    ).astype(jnp.bfloat16)
    keys[near_at, :] = near_k[doc]
    keys[WIN : WIN + tb] = qk[doc, :, width:]
    values[:, far_at] = lax.dot_general(
        w_v_turned[...], rows, NT, preferred_element_type=jnp.float32
    ).astype(jnp.bfloat16)
    values[:, near_at] = near_v[:, own]
    values[:, WIN : WIN + tb] = v_turned[:, own]
    j = lax.broadcasted_iota(jnp.int32, (ext, tb), 0) - WIN
    away = jnp.abs(lax.broadcasted_iota(jnp.int32, (ext, tb), 1) - j)
    kpos = start + j
    seen = (away <= WIN) & (((kpos >= 0) & (kpos < length)) | (away == 0))
    dist[...] = jnp.where(seen, away.astype(jnp.float32), FAR)
    half = lax.broadcasted_iota(jnp.int32, (tb, 128), 1) < 64
    slopes = slopes_of(H)
    lanes = 128
    span = lanes + 2 * WIN

    def scores_of(pair):
        cols = pl.ds(pair * 128, 128)
        query, zero = qk[doc, :, cols] * jnp.bfloat16(0.125), jnp.bfloat16(0)
        both = jnp.concatenate([jnp.where(half, query, zero), jnp.where(half, zero, query)], axis=0)
        return lax.dot_general(keys[:, cols], both, NT, preferred_element_type=jnp.float32)

    upcoming = scores_of(0)
    for pair in range(H // 2):
        scores = upcoming
        if pair + 1 < H // 2:
            upcoming = scores_of(pair + 1)
        for part in range(2):
            columns = []
            for low in range(0, tb, lanes):
                score = scores[low : low + span, part * tb + low : part * tb + low + lanes]
                score = score - slopes[2 * pair + part] * dist[pl.ds(low, span), pl.ds(low, lanes)]
                expo = jnp.exp(score - jnp.max(score, axis=0, keepdims=True))
                weights = (expo * (1.0 / jnp.sum(expo, axis=0, keepdims=True))).astype(jnp.bfloat16)
                above, below = low, ext - span - low
                pieces = [weights]
                if above:
                    pieces = [jnp.zeros((above, lanes), jnp.bfloat16)] + pieces
                if below:
                    pieces = pieces + [jnp.zeros((below, lanes), jnp.bfloat16)]
                columns.append(jnp.concatenate(pieces, axis=0))
            weights = jnp.concatenate(columns, axis=1)
            head = pl.ds(pair * 128 + part * 64, 64)
            mixed[head, :] = jnp.dot(values[head, :], weights, preferred_element_type=jnp.float32).astype(jnp.bfloat16)
    summed = tok[doc].astype(jnp.float32) + lax.dot_general(
        mixed[...], w_out[...], TN, preferred_element_type=jnp.float32
    )
    centred = summed - jnp.mean(summed, axis=1, keepdims=True)
    rstd = lax.rsqrt(jnp.mean(centred * centred, axis=1, keepdims=True) + 1e-05)
    unit = centred * rstd
    hidden_f = unit * gain[...].reshape(1, width)
    hidden_here[...] = hidden_f.astype(jnp.bfloat16)
    leaving = pltpu.make_async_copy(hidden_here, hidden.at[doc], sem)
    leaving.start()
    normed[doc] = unit.astype(jnp.bfloat16)
    rstd_out[doc] = jnp.broadcast_to(rstd, rstd_out.shape[1:])
    keep = start + lax.broadcasted_iota(jnp.int32, (tb, 1), 0) < length
    pool[doc] = jnp.sum(jnp.where(keep, hidden_f, 0.0), axis=0, keepdims=True) / length.astype(jnp.float32)
    leaving.wait()


def attend(first, before, lengths, tokens, near_k, far, near_v, qk, v_turned, w_qkv, w_v_turned, w_out, gain):
    docs, tb, width = tokens.shape
    ext = tb + 2 * WIN
    out_shape = (bf16(docs, tb, width), bf16(width, docs * tb), bf16(docs, tb, width), f32(docs, tb, 128), f32(docs, 1, width))
    out_specs = (ANY,) + (VMEM,) * 4
    operands = [lengths, tokens, near_k, far, near_v, qk, v_turned, w_qkv, w_v_turned, w_out, gain]
    in_specs = [SMEM] + [VMEM] * 10
    aliases = {}
    if before is not None:
        aliases = {len(operands) + k: k for k in range(len(out_shape))}
        operands = operands + list(before)
        in_specs = in_specs + list(out_specs)
    return call(
        functools.partial(attend_kernel, first),
        out_shape,
        in_specs,
        out_specs,
        limit=24,
        flops=5 * 2 * far.shape[0] * tb * ext * width,
        moved=4 * 2**20,
        scratch_shapes=[
            pltpu.VMEM((ext, width), jnp.bfloat16),
            pltpu.VMEM((width, ext), jnp.bfloat16),
            pltpu.VMEM((ext, tb), jnp.float32),
            pltpu.VMEM((tb, width), jnp.bfloat16),
            pltpu.SemaphoreType.DMA,
        ],
        input_output_aliases=aliases,
        name="attend",
    )(*operands)


def near_kernel(near, w, w_v_turned, near_k, near_v):
    docs, tb, width = near.shape

    def some(doc, _):
        rows = near[doc]
        own = pl.ds(pl.multiple_of(doc * tb, tb), tb)
        near_k[doc] = jnp.dot(rows, w[:, width : 2 * width], preferred_element_type=jnp.float32).astype(jnp.bfloat16)
        near_v[:, own] = lax.dot_general(
            w_v_turned[...], rows, NT, preferred_element_type=jnp.float32
        ).astype(jnp.bfloat16)

    lax.fori_loop(0, docs, some, None)


def prepare_kernel(tok, w, qk, v_turned, w_v_turned):
    width = tok.shape[2]

    @pl.when(pl.program_id(0) == 0)
    def _():
        w_v_turned[...] = w[:, 2 * width :].T

    rows = tok[0]
    qk[0] = jnp.dot(rows, w[:, 0 : 2 * width], preferred_element_type=jnp.float32).astype(jnp.bfloat16)
    v_turned[...] = lax.dot_general(w_v_turned[...], rows, NT, preferred_element_type=jnp.float32).astype(jnp.bfloat16)


def prepare(tokens, w_qkv):
    docs, tb, width = tokens.shape
    return call(
        prepare_kernel,
        (bf16(docs, tb, 2 * width), bf16(width, docs * tb), bf16(width, width)),
        [
            pl.BlockSpec((1, tb, width), lambda i: (i, 0, 0)),
            pl.BlockSpec(w_qkv.shape, lambda i: (0, 0), pipeline_mode=pl.Buffered(1)),
        ],
        (
            pl.BlockSpec((1, tb, 2 * width), lambda i: (i, 0, 0)),
            pl.BlockSpec((width, tb), lambda i: (0, i)),
            pl.BlockSpec((width, width), lambda i: (0, 0)),
        ),
        flops=2 * docs * tb * width * 3 * width,
        moved=11 * 2**20,
        grid=(docs,),
        name="prepare",
    )(tokens, w_qkv)


def row_ids(k, shape, dim):
    dp, ctx = here()
    place = lax.broadcasted_iota(jnp.int32, shape, dim)
    return (((dp & 4) | ((dp + k) & 3)) * 16 + (ctx ^ (k // 4))) * shape[dim] + place


def stack_kernel(pool, target, out):
    docs = pool.shape[0]
    for doc in range(docs):
        out[doc : doc + 1, :] = pool[doc]
    out[docs:, :] = target[...]


def add_kernel(*refs):
    terms = [ref[...] for ref in refs[:-1]]
    if len(terms) == 4:
        terms = [terms[0] + terms[2], terms[1] + terms[3]]
    refs[-1][...] = terms[0] + terms[1]


def add(terms):
    return call(add_kernel, f32(*terms[0].shape), [VMEM] * len(terms), VMEM, limit=4, name="add")(*terms)


def merge_kernel(docs, width, *refs):
    refs[-1][...] = merge(docs, width, [ref[...] for ref in refs[:-1]])


def merged(docs, width, states):
    kernel = functools.partial(merge_kernel, docs, width)
    return call(kernel, f32(*states[0].shape), [VMEM] * len(states), VMEM, limit=4, name="merge")(*states)


def target_kernel(docs, positive, *refs):
    pieces, out = refs[:4], refs[4]
    dp, _ = here()
    total = jnp.zeros(out.shape, jnp.float32)
    for k, piece in enumerate(pieces):
        shape = (out.shape[0], piece.shape[0])
        doc = lax.broadcasted_iota(jnp.int32, shape, 0)
        wanted = jnp.zeros(shape, jnp.int32)
        for d in range(2 * docs):
            wanted = jnp.where(doc == d, positive[(d // docs * 4 + (dp & 3)) * docs + d % docs], wanted)
        hit = (row_ids(k, shape, 1) == wanted).astype(jnp.float32).astype(jnp.bfloat16)
        total = total + jnp.dot(hit, piece[...], preferred_element_type=jnp.float32)
    out[...] = total


def turn_kernel(mixed, out):
    width = out.shape[0]
    rows = 128
    lax.fori_loop(0, width // rows, lambda index, _: turn_rows(index * rows, rows, mixed, out), None)


def turn_rows(low, rows, mixed, out):
    width = out.shape[0]
    place = low + lax.broadcasted_iota(jnp.int32, (rows, 1), 0)
    dp, ctx = here()
    each = width // 128
    core = (ctx & 1) ^ (place // (64 * each))
    first, second = place // (16 * each) % 4, place // (4 * each) % 4
    y = ((dp & 3) + jnp.where(core == 0, first, second)) & 3
    x = ((ctx >> 2) + jnp.where(core == 0, second, first)) & 3
    z = ((ctx & 2) + (dp >> 2) + place // each % 4) & 3
    block = ((z & 1) * 4 + y) * 16 + x * 4 + (z >> 1) * 2 + core
    chosen = block * each + place % each == lax.broadcasted_iota(jnp.int32, (rows, width), 1)
    chosen = jnp.where(chosen, 1.0, 0.0).astype(jnp.bfloat16)
    here_rows = pl.ds(pl.multiple_of(low, rows), rows)
    out[here_rows, :] = jnp.dot(chosen, mixed[...], preferred_element_type=jnp.float32).astype(jnp.bfloat16)


def norm_kernel(s0, s1, s2, s3, emb_out, rinv_out, target_out):
    docs = s0.shape[0] // 3
    dp, _ = here()
    own, other = s0[0:docs] + s2[0:docs], s1[0:docs] + s3[0:docs]
    second = dp >= 4
    pooled = jnp.concatenate([jnp.where(second, other, own), jnp.where(second, own, other)], axis=0)
    rinv = lax.rsqrt(jnp.sum(pooled * pooled, axis=1, keepdims=True) + 1e-06)
    emb_out[...] = pooled * rinv
    rinv_out[...] = jnp.broadcast_to(rinv, rinv_out.shape)
    target_out[...] = (s0[docs:] + s2[docs:]) + (s1[docs:] + s3[docs:])


def as_row(column):
    size = column.shape[0]
    same = lax.broadcasted_iota(jnp.int32, (size, size), 0) == lax.broadcasted_iota(jnp.int32, (size, size), 1)
    return jnp.sum(jnp.where(same, column, 0.0), axis=0, keepdims=True)


def score_kernel(docs, positive, e0, e1, e2, e3, *refs):
    tables, (everyone, state, expos) = refs[:8], refs[8:]
    all_docs, width = everyone.shape
    dp, _ = here()
    y = dp & 3
    group = e0.shape[0]
    for k, piece in enumerate((e0, e1, e2, e3)):
        everyone[pl.ds(pl.multiple_of(((y + k) & 3) * group, group), group), :] = piece[...]
    rows = tables[0].shape[0]
    emb = thirds(everyone[...])
    scores = [folded(lax.dot_general(emb, t[...], NT, preferred_element_type=jnp.float32)) / TAU for t in tables]
    top = functools.reduce(jnp.maximum, [jnp.max(s, axis=1, keepdims=True) for s in scores])
    row = lax.broadcasted_iota(jnp.int32, (all_docs, rows), 0)
    wanted = jnp.zeros((all_docs, rows), jnp.int32)
    for doc in range(all_docs):
        z, rest = divmod(doc, all_docs // 2)
        wanted = jnp.where(row == rest // docs * group + z * docs + rest % docs, positive[doc], wanted)
    totals, found = [], jnp.zeros((all_docs, 1), jnp.float32)
    for k, s in enumerate(scores):
        expo = jnp.exp(s - top)
        expos[:, k * rows : (k + 1) * rows] = expo
        totals.append(jnp.sum(expo, axis=1, keepdims=True))
        hit = row_ids(k, (all_docs, rows), 1) == wanted
        found = found + jnp.sum(jnp.where(hit, s, 0.0), axis=1, keepdims=True)
    totals = [totals[k] + totals[k + 4] for k in range(4)]
    total = (totals[0] + totals[2]) + (totals[1] + totals[3])
    mine = thirds(expos[pl.ds(pl.multiple_of(y * group, group), group), :])
    mix = jnp.zeros((group, width), jnp.float32)
    for k, t in enumerate(tables):
        mix = mix + folded(jnp.dot(mine[:, k * rows : (k + 1) * rows], t[...], preferred_element_type=jnp.float32))
    column = lax.broadcasted_iota(jnp.int32, (group, all_docs), 1)
    own = column == lax.broadcasted_iota(jnp.int32, (group, all_docs), 0) + y * group
    total_row, top_row, found_row = as_row(total), as_row(top), as_row(found)
    state[...] = jnp.zeros_like(state)
    state[0:group, 0:width] = mix
    for place, values in ((width, total_row), (width + 128, top_row)):
        value = jnp.sum(jnp.where(own, values, 0.0), axis=1, keepdims=True)
        state[0:group, place : place + 128] = jnp.broadcast_to(value, (group, 128))
    for index, values in enumerate((total_row, top_row, found_row)):
        state[group + index : group + index + 1, 0:all_docs] = values


def merge(docs, width, states):
    row = lax.broadcasted_iota(jnp.int32, states[0].shape, 0)
    column = lax.broadcasted_iota(jnp.int32, states[0].shape, 1)
    place = width + 128
    by_row = [s[:, place : place + 1] for s in states]
    by_lane = [s[docs + 1 : docs + 2, :] for s in states]
    top_row = functools.reduce(jnp.maximum, by_row)
    top_lane = functools.reduce(jnp.maximum, by_lane)
    terms = [
        s * jnp.exp(jnp.where(row == docs, b - top_lane, a - top_row)) for s, a, b in zip(states, by_row, by_lane)
    ]
    if len(terms) == 4:
        terms = [terms[0] + terms[2], terms[1] + terms[3]]
    joined = jnp.where((row < docs) & (column >= place), top_row, terms[0] + terms[1])
    return jnp.where(row == docs + 1, top_lane, joined)


def batch_kernel(emb, everyone, product_out, stats):
    everything = everyone[...]
    all_docs = everything.shape[0]
    own = lax.dot_general(emb[...], everything, NT, precision=HIGHEST, preferred_element_type=jnp.float32) / TAU
    product = lax.dot_general(everything, everything, NT, precision=HIGHEST, preferred_element_type=jnp.float32) / TAU
    wide = (all_docs, all_docs)
    same = lax.broadcasted_iota(jnp.int32, wide, 0) == lax.broadcasted_iota(jnp.int32, wide, 1)
    product = jnp.where(same, -1e30, product)
    top = jnp.max(product, axis=0, keepdims=True)
    total = jnp.sum(jnp.exp(product - top), axis=0, keepdims=True)
    product_out[...] = own
    stats[...] = jnp.concatenate([top, total] * 4, axis=0)


def grad_kernel(
    lengths, s0, s1, s2, s3, emb, rinv, everyone, target, product, stats, gain, normed, rstd, turned,
    send_out, d_summed, loss_out,
):
    docs, tb, width = normed.shape
    all_docs, group = everyone.shape[0], emb.shape[0]
    dp, _ = here()
    mine = lambda a: jnp.where(dp >= 4, a[docs:group], a[0:docs])
    own, others = mine(emb), everyone[...]
    now = merge(group, width, [s[...] for s in (s0, s1, s2, s3)])
    total, top, found = (now[group + k : group + k + 1, 0:all_docs] for k in range(3))
    batch_top, batch_total = stats[0:1], stats[1:2]
    peak = jnp.maximum(top, batch_top)
    lse_row = peak + jnp.log(total * jnp.exp(top - peak) + batch_total * jnp.exp(batch_top - peak))
    loss_out[...] = jnp.broadcast_to(jnp.sum(lse_row - found, axis=1, keepdims=True) / all_docs, loss_out.shape)
    column = lax.broadcasted_iota(jnp.int32, (docs, all_docs), 1)
    first = (dp & 3) * group + (dp >> 2) * docs
    same = column == lax.broadcasted_iota(jnp.int32, (docs, all_docs), 0) + first
    lse = jnp.sum(jnp.where(same, lse_row, 0.0), axis=1, keepdims=True)
    scores = mine(product)
    g_batch = jnp.where(same, 0.0, jnp.exp(scores - lse) + jnp.exp(scores - lse_row)) / all_docs
    shares = mine(now)
    mix = shares[:, 0:width] * jnp.exp(shares[:, width + 128 : width + 129] - lse)
    from_batch = jnp.dot(g_batch, others, precision=HIGHEST, preferred_element_type=jnp.float32)
    d_emb = ((mix - mine(target)) / all_docs + from_batch) / TAU
    d_pooled = (d_emb - own * jnp.sum(own * d_emb, axis=1, keepdims=True)) * mine(rinv)[:, 0:1]
    for doc in range(docs):
        dy = d_pooled[doc : doc + 1] / lengths[doc].astype(jnp.float32) * gain[...].reshape(1, width)
        level = dy - jnp.mean(dy, axis=1, keepdims=True)
        unit = normed[doc].astype(jnp.float32)
        along = jnp.mean(unit * dy, axis=1, keepdims=True)
        keep = lax.axis_index("ctx") * tb + lax.broadcasted_iota(jnp.int32, (tb, 1), 0) < lengths[doc]
        scale = jnp.where(keep, rstd[doc, :, 0:1], 0.0)
        d_summed[doc * tb : (doc + 1) * tb, :] = (scale * (level - unit * along)).astype(jnp.bfloat16)
    product_rows(turned, width // 2, d_summed, send_out)


def product_rows(turned, low, d_summed, out):
    rows = 128

    def some(index, _):
        source = pl.ds(pl.multiple_of(low + index * rows, rows), rows)
        here_rows = pl.ds(pl.multiple_of(index * rows, rows), rows)
        out[here_rows, :] = jnp.dot(turned[source, :], d_summed[...], preferred_element_type=jnp.float32)

    lax.fori_loop(0, out.shape[0] // rows, some, None)


def keep_kernel(turned, d_summed, out):
    product_rows(turned, 0, d_summed, out)


def sum_kernel(count, *refs):
    terms, outs = refs[:count], refs[count:]
    total = terms[0][...].astype(jnp.float32)
    for term in terms[1:]:
        total = total + term[...].astype(jnp.float32)
    rows = outs[0].shape[0]
    for index, out in enumerate(outs):
        out[...] = total[index * rows : (index + 1) * rows].astype(out.dtype)


def sum_and_split(terms, kind):
    rows, width = terms[0].shape
    piece = (rows // 4, width)
    shapes = (f32(*piece),) + (jax.ShapeDtypeStruct(piece, kind),) * 3
    return call(
        functools.partial(sum_kernel, len(terms)), shapes, [VMEM] * len(terms), (VMEM,) * 4, limit=8, name="sum_split"
    )(*terms)


def shards(tokens, w_qkv, w_out, ln_gain, cache, positive, lengths):
    docs, tb, width = tokens.shape
    n_ctx, n_dp = lax.axis_size("ctx"), lax.axis_size("dp")
    all_docs = n_dp * docs
    ring = [(i, (i + 2 * (i % 2) - 1) % n_ctx) for i in range(n_ctx)]
    fetch = lambda part: lax.ppermute(part, "ctx", ring)
    early, middle, late = fetch(tokens[0:1]), fetch(tokens[1:3]), tokens[3:]
    near = swap(tokens, "ctx", 1)
    tables = around(cache, from_y)
    qk, v_turned, w_v_turned = prepare(in_hbm(tokens), in_hbm(w_qkv))
    near_k, near_v = call(
        near_kernel,
        (bf16(docs, tb, width), bf16(width, docs * tb)),
        [VMEM] * 3,
        (VMEM,) * 2,
        flops=4 * docs * tb * width * width,
        moved=4 * 2**20,
        name="near",
    )(near, w_qkv, w_v_turned)
    gain = ln_gain
    fixed = (lengths, tokens, near_k), (near_v, qk, v_turned, w_qkv, w_v_turned, w_out, gain)
    *done, pool = attend(0, None, *fixed[0], early, *fixed[1])
    pool, after, *tables = lax.optimization_barrier((pool, positive, *tables))
    others = [swap(table, "ctx", 1) for table in tables]
    target = call(
        functools.partial(target_kernel, docs), f32(2 * docs, width), [SMEM] + [VMEM] * 4, VMEM, name="target"
    )(after, *tables)
    middle, late, target, *others = lax.optimization_barrier((middle, late, target, *others))
    late = fetch(late)
    done = attend(1, [*done, pool], *fixed[0], middle, *fixed[1])
    done = attend(3, done, *fixed[0], late, *fixed[1])
    hidden, mixed, normed, rstd, pool = done

    turned = call(
        turn_kernel,
        bf16(width, docs * tb),
        [VMEM],
        VMEM,
        flops=2 * docs * tb * width * width,
        moved=4 * 2**20,
        name="turn",
    )(mixed)

    group = 2 * docs
    sums = call(stack_kernel, f32(docs + group, width), [VMEM, VMEM], VMEM, limit=4, name="stack")(
        pool, target
    )
    sums = add([sums, swap(sums, "ctx", 1)])
    sums = add(around(sums, from_x))
    emb, rinv, target = call(
        norm_kernel,
        (f32(group, width), f32(group, 128), f32(group, width)),
        [VMEM] * 4,
        (VMEM,) * 3,
        limit=4,
        name="norm",
    )(*around(sums, from_z))
    embs = around(emb, from_y)
    everyone, state = call(
        functools.partial(score_kernel, docs),
        (f32(all_docs, width), f32(2 * group, width + 256)),
        [SMEM] + [VMEM] * 12,
        (VMEM, VMEM),
        moved=2 * 2**20,
        scratch_shapes=[pltpu.VMEM((all_docs, 8 * cache.shape[0]), jnp.float32)],
        name="score",
    )(positive, *embs, *tables, *others)
    product, stats = call(
        batch_kernel,
        (f32(group, all_docs), f32(8, all_docs)),
        [VMEM, VMEM],
        (VMEM, VMEM),
        limit=4,
        name="batch",
    )(emb, everyone)
    state = merged(group, width, around(state, from_x))
    half = width // 2
    send, d_summed, loss = call(
        grad_kernel,
        (f32(half, width), bf16(docs * tb, width), f32(8, 128)),
        [SMEM] + [VMEM] * 14,
        (VMEM,) * 3,
        flops=docs * tb * width * width,
        moved=8 * 2**20,
        name="grad",
    )(
        lengths, *around(state, from_z), emb, rinv, everyone, target, product, stats, gain, normed, rstd, turned,
    )
    keep = call(
        keep_kernel,
        f32(half, width),
        [VMEM, VMEM],
        VMEM,
        flops=docs * tb * width * width,
        moved=2**20,
        name="keep",
    )(turned, d_summed)
    keep, *sends = sum_and_split([keep, swap(send, "ctx", 1)], jnp.bfloat16)
    got = [from_plane(piece, -(k + 1), False) for k, piece in enumerate(sends)]
    keep, *sends = sum_and_split([keep] + got, jnp.float32)
    got = [from_plane(piece, -(k + 1), True) for k, piece in enumerate(sends)]
    keep, *sends = sum_and_split([keep] + got, jnp.float32)
    got = [from_z(piece, -(k + 1)) for k, piece in enumerate(sends)]
    return (hidden, loss[0, 0], add([keep] + got))


def solution(mesh):
    placed = (P("dp", "ctx", None), P(), P(), P(), P(("dp", "ctx"), None), P(), P("dp"))
    return jax.shard_map(
        shards,
        mesh=mesh,
        in_specs=placed,
        out_specs=(P("dp", "ctx", None), P(), P(("dp", "ctx"), None)),
        check_vma=False,
    )
```

```python
import functools
import math

import jax
import jax.numpy as jnp
from jax import lax
from jax.experimental import pallas as pl
from jax.experimental.pallas import tpu as pltpu
from jax.sharding import PartitionSpec as P

H = 12
WIN = 256
TAU = 0.02
FAR = 1e32
NT = (((1,), (1,)), ((), ()))
TN = (((0,), (0,)), ((), ()))
HIGHEST = lax.Precision.HIGHEST
VMEM = pl.BlockSpec(memory_space=pltpu.VMEM)
SMEM = pl.BlockSpec(memory_space=pltpu.SMEM)
ANY = pl.BlockSpec(memory_space=pl.ANY)


def swap(value, axis, bits):
    return lax.ppermute(value, axis, [(i, i ^ bits) for i in range(lax.axis_size(axis))])


def from_x(value, k):
    size = lax.axis_size("ctx")
    return lax.ppermute(value, "ctx", [((c + 4 * k) % size, c) for c in range(size)])


def from_y(value, k):
    return lax.ppermute(value, "dp", [((d & 4) | ((d + k) & 3), d) for d in range(lax.axis_size("dp"))])


def from_z(value, k):
    n_dp, n_ctx = lax.axis_size("dp"), lax.axis_size("ctx")
    pairs = []
    for d in range(n_dp):
        for c in range(n_ctx):
            z = ((c & 2) + (d >> 2) + k) & 3
            pairs.append((((z & 1) * 4 + (d & 3)) * n_ctx + (c & ~2) + (z & 2), d * n_ctx + c))
    return lax.ppermute(value, ("dp", "ctx"), pairs)


def from_plane(value, k, last):
    n_dp, n_ctx = lax.axis_size("dp"), lax.axis_size("ctx")
    pairs = []
    for d in range(n_dp):
        for c in range(n_ctx):
            along_y = (c & 1 == 1) == last
            source = ((d & 4) | ((d + k) & 3), c) if along_y else (d, (c + 4 * k) % n_ctx)
            pairs.append((source[0] * n_ctx + source[1], d * n_ctx + c))
    return lax.ppermute(value, ("dp", "ctx"), pairs)


def around(value, fetch):
    return [value] + [fetch(value, k) for k in (1, 2, 3)]


def here():
    return lax.axis_index("dp"), lax.axis_index("ctx")


def in_hbm(value):
    return pltpu.with_memory_space_constraint(value, pltpu.HBM)


def call(kernel, out_shape, in_specs, out_specs, limit=16, flops=0, moved=0, **keywords):
    return pl.pallas_call(
        kernel,
        out_shape=out_shape,
        in_specs=in_specs,
        out_specs=out_specs,
        compiler_params=pltpu.CompilerParams(vmem_limit_bytes=limit * 2**20),
        cost_estimate=pl.CostEstimate(flops=flops, bytes_accessed=moved, transcendentals=0),
        **keywords,
    )


def f32(*shape):
    return jax.ShapeDtypeStruct(shape, jnp.float32)


def bf16(*shape):
    return jax.ShapeDtypeStruct(shape, jnp.bfloat16)


def slopes_of(heads):
    largest = 2 ** int(math.floor(math.log2(heads)))
    listed = [2.0 ** (-8.0 * (h + 1) / largest) for h in range(largest)]
    return listed + [2.0 ** (-4.0 * (2 * m + 1) / largest) for m in range(heads - largest)]


def thirds(value):
    high = value.astype(jnp.bfloat16)
    rest = value - high.astype(jnp.float32)
    middle = rest.astype(jnp.bfloat16)
    low = (rest - middle.astype(jnp.float32)).astype(jnp.bfloat16)
    parts = [p.astype(jnp.float32) for p in (high, middle, low)]
    return jnp.concatenate(parts, axis=0).astype(jnp.bfloat16)


def folded(products):
    rows = products.shape[0] // 3
    return products[0:rows] + products[rows : 2 * rows] + products[2 * rows :]


def attend_kernel(first, *refs):
    far = refs[3]
    lax.fori_loop(0, far.shape[0], lambda index, _: attend_doc(first + index, index, *refs), None)


def attend_doc(
    doc, index, lengths, tok, near_k, far, near_v, qk, v_turned, w, w_v_turned, w_out, gain, *refs
):
    hidden, mixed_all, normed, rstd_out, pool, keys, values, dist, hidden_here, sem = refs[-10:]
    docs, tb, width = tok.shape
    ext = tb + 2 * WIN
    own = pl.ds(pl.multiple_of(doc * tb, tb), tb)
    mixed = mixed_all.at[:, own]
    ctx = lax.axis_index("ctx")
    start, length = ctx * tb, lengths[doc]
    odd = lax.rem(ctx, 2)
    near_at = pl.ds(pl.multiple_of((1 - odd) * (WIN + tb), 128), WIN)
    far_at = pl.ds(pl.multiple_of(odd * (WIN + tb), 128), WIN)
    rows = far[index]
    keys[far_at, :] = jnp.dot(
        rows, w[:, width : 2 * width], preferred_element_type=jnp.float32
    ).astype(jnp.bfloat16)
    keys[near_at, :] = near_k[doc]
    keys[WIN : WIN + tb] = qk[doc, :, width:]
    values[:, far_at] = lax.dot_general(
        w_v_turned[...], rows, NT, preferred_element_type=jnp.float32
    ).astype(jnp.bfloat16)
    values[:, near_at] = near_v[:, own]
    values[:, WIN : WIN + tb] = v_turned[:, own]
    j = lax.broadcasted_iota(jnp.int32, (ext, tb), 0) - WIN
    away = jnp.abs(lax.broadcasted_iota(jnp.int32, (ext, tb), 1) - j)
    kpos = start + j
    seen = (away <= WIN) & (((kpos >= 0) & (kpos < length)) | (away == 0))
    dist[...] = jnp.where(seen, away.astype(jnp.float32), FAR)
    half = lax.broadcasted_iota(jnp.int32, (tb, 128), 1) < 64
    slopes = slopes_of(H)
    lanes = 128
    span = lanes + 2 * WIN

    def scores_of(pair):
        cols = pl.ds(pair * 128, 128)
        query, zero = qk[doc, :, cols] * jnp.bfloat16(0.125), jnp.bfloat16(0)
        both = jnp.concatenate([jnp.where(half, query, zero), jnp.where(half, zero, query)], axis=0)
        return lax.dot_general(keys[:, cols], both, NT, preferred_element_type=jnp.float32)

    upcoming = scores_of(0)
    for pair in range(H // 2):
        scores = upcoming
        if pair + 1 < H // 2:
            upcoming = scores_of(pair + 1)
        for part in range(2):
            columns = []
            for low in range(0, tb, lanes):
                score = scores[low : low + span, part * tb + low : part * tb + low + lanes]
                score = score - slopes[2 * pair + part] * dist[pl.ds(low, span), pl.ds(low, lanes)]
                expo = jnp.exp(score - jnp.max(score, axis=0, keepdims=True))
                weights = (expo * (1.0 / jnp.sum(expo, axis=0, keepdims=True))).astype(jnp.bfloat16)
                above, below = low, ext - span - low
                pieces = [weights]
                if above:
                    pieces = [jnp.zeros((above, lanes), jnp.bfloat16)] + pieces
                if below:
                    pieces = pieces + [jnp.zeros((below, lanes), jnp.bfloat16)]
                columns.append(jnp.concatenate(pieces, axis=0))
            weights = jnp.concatenate(columns, axis=1)
            head = pl.ds(pair * 128 + part * 64, 64)
            mixed[head, :] = jnp.dot(values[head, :], weights, preferred_element_type=jnp.float32).astype(jnp.bfloat16)
    summed = tok[doc].astype(jnp.float32) + lax.dot_general(
        mixed[...], w_out[...], TN, preferred_element_type=jnp.float32
    )
    centred = summed - jnp.mean(summed, axis=1, keepdims=True)
    rstd = lax.rsqrt(jnp.mean(centred * centred, axis=1, keepdims=True) + 1e-05)
    unit = centred * rstd
    hidden_f = unit * gain[...].reshape(1, width)
    hidden_here[...] = hidden_f.astype(jnp.bfloat16)
    leaving = pltpu.make_async_copy(hidden_here, hidden.at[doc], sem)
    leaving.start()
    normed[doc] = unit.astype(jnp.bfloat16)
    rstd_out[doc] = jnp.broadcast_to(rstd, rstd_out.shape[1:])
    keep = start + lax.broadcasted_iota(jnp.int32, (tb, 1), 0) < length
    pool[doc] = jnp.sum(jnp.where(keep, hidden_f, 0.0), axis=0, keepdims=True) / length.astype(jnp.float32)
    leaving.wait()


def attend(first, before, lengths, tokens, near_k, far, near_v, qk, v_turned, w_qkv, w_v_turned, w_out, gain):
    docs, tb, width = tokens.shape
    ext = tb + 2 * WIN
    out_shape = (bf16(docs, tb, width), bf16(width, docs * tb), bf16(docs, tb, width), f32(docs, tb, 128), f32(docs, 1, width))
    out_specs = (ANY,) + (VMEM,) * 4
    operands = [lengths, tokens, near_k, far, near_v, qk, v_turned, w_qkv, w_v_turned, w_out, gain]
    in_specs = [SMEM] + [VMEM] * 10
    aliases = {}
    if before is not None:
        aliases = {len(operands) + k: k for k in range(len(out_shape))}
        operands = operands + list(before)
        in_specs = in_specs + list(out_specs)
    return call(
        functools.partial(attend_kernel, first),
        out_shape,
        in_specs,
        out_specs,
        limit=24,
        flops=5 * 2 * far.shape[0] * tb * ext * width,
        moved=4 * 2**20,
        scratch_shapes=[
            pltpu.VMEM((ext, width), jnp.bfloat16),
            pltpu.VMEM((width, ext), jnp.bfloat16),
            pltpu.VMEM((ext, tb), jnp.float32),
            pltpu.VMEM((tb, width), jnp.bfloat16),
            pltpu.SemaphoreType.DMA,
        ],
        input_output_aliases=aliases,
        name="attend",
    )(*operands)


def near_kernel(near, w, w_v_turned, near_k, near_v):
    docs, tb, width = near.shape

    def some(doc, _):
        rows = near[doc]
        own = pl.ds(pl.multiple_of(doc * tb, tb), tb)
        near_k[doc] = jnp.dot(rows, w[:, width : 2 * width], preferred_element_type=jnp.float32).astype(jnp.bfloat16)
        near_v[:, own] = lax.dot_general(
            w_v_turned[...], rows, NT, preferred_element_type=jnp.float32
        ).astype(jnp.bfloat16)

    lax.fori_loop(0, docs, some, None)


def prepare_kernel(tok, w, qk, v_turned, w_v_turned):
    width = tok.shape[2]

    @pl.when(pl.program_id(0) == 0)
    def _():
        w_v_turned[...] = w[:, 2 * width :].T

    rows = tok[0]
    qk[0] = jnp.dot(rows, w[:, 0 : 2 * width], preferred_element_type=jnp.float32).astype(jnp.bfloat16)
    v_turned[...] = lax.dot_general(w_v_turned[...], rows, NT, preferred_element_type=jnp.float32).astype(jnp.bfloat16)


def prepare(tokens, w_qkv):
    docs, tb, width = tokens.shape
    return call(
        prepare_kernel,
        (bf16(docs, tb, 2 * width), bf16(width, docs * tb), bf16(width, width)),
        [
            pl.BlockSpec((1, tb, width), lambda i: (i, 0, 0)),
            pl.BlockSpec(w_qkv.shape, lambda i: (0, 0), pipeline_mode=pl.Buffered(1)),
        ],
        (
            pl.BlockSpec((1, tb, 2 * width), lambda i: (i, 0, 0)),
            pl.BlockSpec((width, tb), lambda i: (0, i)),
            pl.BlockSpec((width, width), lambda i: (0, 0)),
        ),
        flops=2 * docs * tb * width * 3 * width,
        moved=11 * 2**20,
        grid=(docs,),
        name="prepare",
    )(tokens, w_qkv)


def row_ids(k, shape, dim):
    dp, ctx = here()
    place = lax.broadcasted_iota(jnp.int32, shape, dim)
    return (((dp & 4) | ((dp + k) & 3)) * 16 + (ctx ^ (k // 4))) * shape[dim] + place


def stack_kernel(pool, target, out):
    docs = pool.shape[0]
    for doc in range(docs):
        out[doc : doc + 1, :] = pool[doc]
    out[docs:, :] = target[...]


def add_kernel(*refs):
    terms = [ref[...] for ref in refs[:-1]]
    if len(terms) == 4:
        terms = [terms[0] + terms[2], terms[1] + terms[3]]
    refs[-1][...] = terms[0] + terms[1]


def add(terms):
    return call(add_kernel, f32(*terms[0].shape), [VMEM] * len(terms), VMEM, limit=4, name="add")(*terms)


def merge_kernel(docs, width, *refs):
    refs[-1][...] = merge(docs, width, [ref[...] for ref in refs[:-1]])


def merged(docs, width, states):
    kernel = functools.partial(merge_kernel, docs, width)
    return call(kernel, f32(*states[0].shape), [VMEM] * len(states), VMEM, limit=4, name="merge")(*states)


def target_kernel(docs, positive, *refs):
    pieces, out = refs[:4], refs[4]
    dp, _ = here()
    total = jnp.zeros(out.shape, jnp.float32)
    for k, piece in enumerate(pieces):
        shape = (out.shape[0], piece.shape[0])
        doc = lax.broadcasted_iota(jnp.int32, shape, 0)
        wanted = jnp.zeros(shape, jnp.int32)
        for d in range(2 * docs):
            wanted = jnp.where(doc == d, positive[(d // docs * 4 + (dp & 3)) * docs + d % docs], wanted)
        hit = (row_ids(k, shape, 1) == wanted).astype(jnp.float32).astype(jnp.bfloat16)
        total = total + jnp.dot(hit, piece[...], preferred_element_type=jnp.float32)
    out[...] = total


def choose_kernel(out):
    lax.fori_loop(0, out.shape[0] // 128, lambda index, _: choose_rows(index * 128, 128, out), None)


def choose_rows(low, rows, out):
    width = out.shape[0]
    place = low + lax.broadcasted_iota(jnp.int32, (rows, 1), 0)
    dp, ctx = here()
    each = width // 128
    core = (ctx & 1) ^ (place // (64 * each))
    first, second = place // (16 * each) % 4, place // (4 * each) % 4
    y = ((dp & 3) + jnp.where(core == 0, first, second)) & 3
    x = ((ctx >> 2) + jnp.where(core == 0, second, first)) & 3
    z = ((ctx & 2) + (dp >> 2) + place // each % 4) & 3
    block = ((z & 1) * 4 + y) * 16 + x * 4 + (z >> 1) * 2 + core
    chosen = block * each + place % each == lax.broadcasted_iota(jnp.int32, (rows, width), 1)
    out[pl.ds(pl.multiple_of(low, rows), rows), :] = jnp.where(chosen, 1.0, 0.0).astype(jnp.bfloat16)


def turn_kernel(chosen, mixed, own, other):
    half, rows = own.shape[0], 192

    def some(index, _):
        for out, low in ((own, 0), (other, half)):
            source = chosen[pl.ds(pl.multiple_of(low + index * rows, 64), rows), :]
            product = jnp.dot(source, mixed[...], preferred_element_type=jnp.float32)
            out[pl.ds(pl.multiple_of(index * rows, 64), rows), :] = product.astype(jnp.bfloat16)

    lax.fori_loop(0, half // rows, some, None)


def norm_kernel(s0, s1, s2, s3, emb_out, rinv_out, target_out):
    docs = s0.shape[0] // 3
    dp, _ = here()
    own, other = s0[0:docs] + s2[0:docs], s1[0:docs] + s3[0:docs]
    second = dp >= 4
    pooled = jnp.concatenate([jnp.where(second, other, own), jnp.where(second, own, other)], axis=0)
    rinv = lax.rsqrt(jnp.sum(pooled * pooled, axis=1, keepdims=True) + 1e-06)
    emb_out[...] = pooled * rinv
    rinv_out[...] = jnp.broadcast_to(rinv, rinv_out.shape)
    target_out[...] = (s0[docs:] + s2[docs:]) + (s1[docs:] + s3[docs:])


def as_row(column):
    size = column.shape[0]
    same = lax.broadcasted_iota(jnp.int32, (size, size), 0) == lax.broadcasted_iota(jnp.int32, (size, size), 1)
    return jnp.sum(jnp.where(same, column, 0.0), axis=0, keepdims=True)


def score_kernel(docs, positive, e0, e1, e2, e3, *refs):
    tables, (everyone, state, expos) = refs[:8], refs[8:]
    all_docs, width = everyone.shape
    dp, _ = here()
    y = dp & 3
    group = e0.shape[0]
    for k, piece in enumerate((e0, e1, e2, e3)):
        everyone[pl.ds(pl.multiple_of(((y + k) & 3) * group, group), group), :] = piece[...]
    rows = tables[0].shape[0]
    emb = thirds(everyone[...])
    scores = [folded(lax.dot_general(emb, t[...], NT, preferred_element_type=jnp.float32)) / TAU for t in tables]
    top = functools.reduce(jnp.maximum, [jnp.max(s, axis=1, keepdims=True) for s in scores])
    row = lax.broadcasted_iota(jnp.int32, (all_docs, rows), 0)
    wanted = jnp.zeros((all_docs, rows), jnp.int32)
    for doc in range(all_docs):
        z, rest = divmod(doc, all_docs // 2)
        wanted = jnp.where(row == rest // docs * group + z * docs + rest % docs, positive[doc], wanted)
    totals, found = [], jnp.zeros((all_docs, 1), jnp.float32)
    for k, s in enumerate(scores):
        expo = jnp.exp(s - top)
        expos[:, k * rows : (k + 1) * rows] = expo
        totals.append(jnp.sum(expo, axis=1, keepdims=True))
        hit = row_ids(k, (all_docs, rows), 1) == wanted
        found = found + jnp.sum(jnp.where(hit, s, 0.0), axis=1, keepdims=True)
    totals = [totals[k] + totals[k + 4] for k in range(4)]
    total = (totals[0] + totals[2]) + (totals[1] + totals[3])
    mine = thirds(expos[pl.ds(pl.multiple_of(y * group, group), group), :])
    mix = jnp.zeros((group, width), jnp.float32)
    for k, t in enumerate(tables):
        mix = mix + folded(jnp.dot(mine[:, k * rows : (k + 1) * rows], t[...], preferred_element_type=jnp.float32))
    column = lax.broadcasted_iota(jnp.int32, (group, all_docs), 1)
    own = column == lax.broadcasted_iota(jnp.int32, (group, all_docs), 0) + y * group
    total_row, top_row, found_row = as_row(total), as_row(top), as_row(found)
    state[...] = jnp.zeros_like(state)
    state[0:group, 0:width] = mix
    for place, values in ((width, total_row), (width + 128, top_row)):
        value = jnp.sum(jnp.where(own, values, 0.0), axis=1, keepdims=True)
        state[0:group, place : place + 128] = jnp.broadcast_to(value, (group, 128))
    for index, values in enumerate((total_row, top_row, found_row)):
        state[group + index : group + index + 1, 0:all_docs] = values


def merge(docs, width, states):
    row = lax.broadcasted_iota(jnp.int32, states[0].shape, 0)
    column = lax.broadcasted_iota(jnp.int32, states[0].shape, 1)
    place = width + 128
    by_row = [s[:, place : place + 1] for s in states]
    by_lane = [s[docs + 1 : docs + 2, :] for s in states]
    top_row = functools.reduce(jnp.maximum, by_row)
    top_lane = functools.reduce(jnp.maximum, by_lane)
    terms = [
        s * jnp.exp(jnp.where(row == docs, b - top_lane, a - top_row)) for s, a, b in zip(states, by_row, by_lane)
    ]
    if len(terms) == 4:
        terms = [terms[0] + terms[2], terms[1] + terms[3]]
    joined = jnp.where((row < docs) & (column >= place), top_row, terms[0] + terms[1])
    return jnp.where(row == docs + 1, top_lane, joined)


def batch_kernel(emb, everyone, product_out, stats):
    everything = everyone[...]
    all_docs = everything.shape[0]
    own = lax.dot_general(emb[...], everything, NT, precision=HIGHEST, preferred_element_type=jnp.float32) / TAU
    product = lax.dot_general(everything, everything, NT, precision=HIGHEST, preferred_element_type=jnp.float32) / TAU
    wide = (all_docs, all_docs)
    same = lax.broadcasted_iota(jnp.int32, wide, 0) == lax.broadcasted_iota(jnp.int32, wide, 1)
    product = jnp.where(same, -1e30, product)
    top = jnp.max(product, axis=0, keepdims=True)
    total = jnp.sum(jnp.exp(product - top), axis=0, keepdims=True)
    product_out[...] = own
    stats[...] = jnp.concatenate([top, total] * 4, axis=0)


def grad_kernel(
    lengths, s0, s1, s2, s3, emb, rinv, everyone, target, scored, stats, gain, normed, rstd, turned, *refs,
):
    normed_other, rstd_other, turned_other, loss_out, *outs, rows_dy, rows_level, d_summed, product = refs
    docs, tb, width = normed.shape
    all_docs, group = everyone.shape[0], emb.shape[0]
    dp, ctx = here()
    mine = lambda a: jnp.where(dp >= 4, a[docs:group], a[0:docs])
    own, others = mine(emb), everyone[...]
    now = merge(group, width, [s[...] for s in (s0, s1, s2, s3)])
    total, top, found = (now[group + k : group + k + 1, 0:all_docs] for k in range(3))
    batch_top, batch_total = stats[0:1], stats[1:2]
    peak = jnp.maximum(top, batch_top)
    lse_row = peak + jnp.log(total * jnp.exp(top - peak) + batch_total * jnp.exp(batch_top - peak))
    loss_out[...] = jnp.broadcast_to(jnp.sum(lse_row - found, axis=1, keepdims=True) / all_docs, loss_out.shape)
    column = lax.broadcasted_iota(jnp.int32, (docs, all_docs), 1)
    first = (dp & 3) * group + (dp >> 2) * docs
    same = column == lax.broadcasted_iota(jnp.int32, (docs, all_docs), 0) + first
    lse = jnp.sum(jnp.where(same, lse_row, 0.0), axis=1, keepdims=True)
    scores = mine(scored)
    g_batch = jnp.where(same, 0.0, jnp.exp(scores - lse) + jnp.exp(scores - lse_row)) / all_docs
    shares = mine(now)
    mix = shares[:, 0:width] * jnp.exp(shares[:, width + 128 : width + 129] - lse)
    from_batch = jnp.dot(g_batch, others, precision=HIGHEST, preferred_element_type=jnp.float32)
    d_emb = ((mix - mine(target)) / all_docs + from_batch) / TAU
    d_pooled = (d_emb - own * jnp.sum(own * d_emb, axis=1, keepdims=True)) * mine(rinv)[:, 0:1]
    row = lax.broadcasted_iota(jnp.int32, (docs, width), 0)
    count = jnp.ones((docs, width), jnp.float32)
    for doc in range(docs):
        count = jnp.where(row == doc, lengths[doc].astype(jnp.float32), count)
    dy = d_pooled / count * gain[...].reshape(1, width)
    rows_dy[0:docs, :] = dy
    rows_level[0:docs, :] = dy - jnp.mean(dy, axis=1, keepdims=True)

    def some(doc, _):
        dy, level = rows_dy[pl.ds(doc, 1), :], rows_level[pl.ds(doc, 1), :]
        for index, (units, scales) in enumerate(((normed, rstd), (normed_other, rstd_other))):
            unit = units[doc].astype(jnp.float32)
            along = jnp.mean(unit * dy, axis=1, keepdims=True)
            start = (ctx ^ index) * tb
            keep = start + lax.broadcasted_iota(jnp.int32, (tb, 1), 0) < lengths[doc]
            scale = jnp.where(keep, scales[doc, :, 0:1], 0.0)
            place = pl.ds(pl.multiple_of((index * docs + doc) * tb, tb), tb)
            d_summed[place, :] = (scale * (level - unit * along)).astype(jnp.bfloat16)

    lax.fori_loop(0, docs, some, None)
    half = docs * tb
    rows = 192

    def block(index, _):
        place = pl.ds(pl.multiple_of(index * rows, 64), rows)
        total = jnp.dot(turned[place, :], d_summed[0:half], preferred_element_type=jnp.float32)
        product[place, :] = total + jnp.dot(turned_other[place, :], d_summed[half:], preferred_element_type=jnp.float32)

    lax.fori_loop(0, turned.shape[0] // rows, block, None)
    rows = outs[0].shape[0]
    for index, out in enumerate(outs):
        out[...] = product[index * rows : (index + 1) * rows, :].astype(out.dtype)


def sum_kernel(count, *refs):
    terms, outs = refs[:count], refs[count:]
    total = terms[0][...].astype(jnp.float32)
    for term in terms[1:]:
        total = total + term[...].astype(jnp.float32)
    rows = outs[0].shape[0]
    for index, out in enumerate(outs):
        out[...] = total[index * rows : (index + 1) * rows].astype(out.dtype)


def sum_and_split(terms, kind):
    rows, width = terms[0].shape
    piece = (rows // 4, width)
    shapes = (f32(*piece),) + (jax.ShapeDtypeStruct(piece, kind),) * 3
    return call(
        functools.partial(sum_kernel, len(terms)), shapes, [VMEM] * len(terms), (VMEM,) * 4, limit=8, name="sum_split"
    )(*terms)


def shards(tokens, w_qkv, w_out, ln_gain, cache, positive, lengths):
    docs, tb, width = tokens.shape
    n_ctx, n_dp = lax.axis_size("ctx"), lax.axis_size("dp")
    all_docs = n_dp * docs
    ring = [(i, (i + 2 * (i % 2) - 1) % n_ctx) for i in range(n_ctx)]
    fetch = lambda part: lax.ppermute(part, "ctx", ring)
    early, middle, late = fetch(tokens[0:1]), fetch(tokens[1:3]), tokens[3:]
    near = swap(tokens, "ctx", 1)
    tables = around(cache, from_y)
    qk, v_turned, w_v_turned = prepare(in_hbm(tokens), in_hbm(w_qkv))
    near_k, near_v = call(
        near_kernel,
        (bf16(docs, tb, width), bf16(width, docs * tb)),
        [VMEM] * 3,
        (VMEM,) * 2,
        flops=4 * docs * tb * width * width,
        moved=4 * 2**20,
        name="near",
    )(near, w_qkv, w_v_turned)
    chosen = call(choose_kernel, bf16(width, width), [], VMEM, limit=4, name="choose")()
    early, chosen = lax.optimization_barrier((early, chosen))
    gain = ln_gain
    fixed = (lengths, tokens, near_k), (near_v, qk, v_turned, w_qkv, w_v_turned, w_out, gain)
    *done, pool = attend(0, None, *fixed[0], early, *fixed[1])
    pool, after = lax.optimization_barrier((pool, positive))
    target = call(
        functools.partial(target_kernel, docs), f32(2 * docs, width), [SMEM] + [VMEM] * 4, VMEM, name="target"
    )(after, *tables)
    middle, late, target = lax.optimization_barrier((middle, late, target))
    late = fetch(late)
    done = attend(1, [*done, pool], *fixed[0], middle, *fixed[1])
    done = attend(3, done, *fixed[0], late, *fixed[1])
    hidden, mixed, normed, rstd, pool = done

    half = width // 2
    turned, leaving = call(
        turn_kernel,
        (bf16(half, docs * tb),) * 2,
        [VMEM, VMEM],
        (VMEM,) * 2,
        flops=2 * docs * tb * width * width,
        moved=4 * 2**20,
        name="turn",
    )(chosen, mixed)

    group = 2 * docs
    sums = call(stack_kernel, f32(docs + group, width), [VMEM, VMEM], VMEM, limit=4, name="stack")(
        pool, target
    )
    sums = add([sums, swap(sums, "ctx", 1)])
    sums, *tables = lax.optimization_barrier((sums, *tables))
    others = [swap(table, "ctx", 1) for table in tables]
    sums = add(around(sums, from_x))
    sums, leaving = lax.optimization_barrier((sums, leaving))
    emb, rinv, target = call(
        norm_kernel,
        (f32(group, width), f32(group, 128), f32(group, width)),
        [VMEM] * 4,
        (VMEM,) * 3,
        limit=4,
        name="norm",
    )(*around(sums, from_z))
    emb, *others = lax.optimization_barrier((emb, *others))
    swapped = [swap(value, "ctx", 1) for value in (normed, rstd, leaving)]
    embs = around(emb, from_y)
    everyone, state = call(
        functools.partial(score_kernel, docs),
        (f32(all_docs, width), f32(2 * group, width + 256)),
        [SMEM] + [VMEM] * 12,
        (VMEM, VMEM),
        moved=2 * 2**20,
        scratch_shapes=[pltpu.VMEM((all_docs, 8 * cache.shape[0]), jnp.float32)],
        name="score",
    )(positive, *embs, *tables, *others)
    product, stats = call(
        batch_kernel,
        (f32(group, all_docs), f32(8, all_docs)),
        [VMEM, VMEM],
        (VMEM, VMEM),
        limit=4,
        name="batch",
    )(emb, everyone)
    state, *swapped = lax.optimization_barrier((state, *swapped))
    state = merged(group, width, around(state, from_x))
    piece = (half // 4, width)
    loss, keep, *sends = call(
        grad_kernel,
        (f32(8, 128), f32(*piece)) + (bf16(*piece),) * 3,
        [SMEM] + [VMEM] * 17,
        (VMEM,) * 5,
        flops=2 * docs * tb * width * width,
        moved=8 * 2**20,
        scratch_shapes=[
            pltpu.VMEM((8, width), jnp.float32),
            pltpu.VMEM((8, width), jnp.float32),
            pltpu.VMEM((2 * docs * tb, width), jnp.bfloat16),
            pltpu.VMEM((half, width), jnp.float32),
        ],
        name="grad",
    )(
        lengths, *around(state, from_z), emb, rinv, everyone, target, product, stats, gain,
        normed, rstd, turned, *swapped,
    )
    got = [from_plane(piece, -(k + 1), False) for k, piece in enumerate(sends)]
    keep, *sends = sum_and_split([keep] + got, jnp.float32)
    got = [from_plane(piece, -(k + 1), True) for k, piece in enumerate(sends)]
    keep, *sends = sum_and_split([keep] + got, jnp.float32)
    got = [from_z(piece, -(k + 1)) for k, piece in enumerate(sends)]
    return (hidden, loss[0, 0], add([keep] + got))


def solution(mesh):
    placed = (P("dp", "ctx", None), P(), P(), P(), P(("dp", "ctx"), None), P(), P("dp"))
    return jax.shard_map(
        shards,
        mesh=mesh,
        in_specs=placed,
        out_specs=(P("dp", "ctx", None), P(), P(("dp", "ctx"), None)),
        check_vma=False,
    )
```

```python
import functools
import math

import jax
import jax.numpy as jnp
from jax import lax
from jax.experimental import pallas as pl
from jax.experimental.pallas import tpu as pltpu
from jax.sharding import PartitionSpec as P

H = 12
WIN = 256
TAU = 0.02
FAR = 1e32
NT = (((1,), (1,)), ((), ()))
TN = (((0,), (0,)), ((), ()))
HIGHEST = lax.Precision.HIGHEST
VMEM = pl.BlockSpec(memory_space=pltpu.VMEM)
SMEM = pl.BlockSpec(memory_space=pltpu.SMEM)
ANY = pl.BlockSpec(memory_space=pl.ANY)

ORDER = (0, 1, 3, 2)


def swap(value, axis, bits):
    return lax.ppermute(value, axis, [(i, i ^ bits) for i in range(lax.axis_size(axis))])


def from_x(value, k):
    size = lax.axis_size("ctx")
    return lax.ppermute(value, "ctx", [((c + 4 * k) % size, c) for c in range(size)])


def from_y(value, k):
    return lax.ppermute(value, "dp", [((d & 4) | ((d + k) & 3), d) for d in range(lax.axis_size("dp"))])


def from_z(value, k):
    n_dp, n_ctx = lax.axis_size("dp"), lax.axis_size("ctx")
    pairs = []
    for d in range(n_dp):
        for c in range(n_ctx):
            z = ((c & 2) + (d >> 2) + k) & 3
            pairs.append((((z & 1) * 4 + (d & 3)) * n_ctx + (c & ~2) + (z & 2), d * n_ctx + c))
    return lax.ppermute(value, ("dp", "ctx"), pairs)


def from_plane(value, k, last):
    n_dp, n_ctx = lax.axis_size("dp"), lax.axis_size("ctx")
    pairs = []
    for d in range(n_dp):
        for c in range(n_ctx):
            along_y = (c & 1 == 1) == last
            source = ((d & 4) | ((d + k) & 3), c) if along_y else (d, (c + 4 * k) % n_ctx)
            pairs.append((source[0] * n_ctx + source[1], d * n_ctx + c))
    return lax.ppermute(value, ("dp", "ctx"), pairs)


def around(value, fetch):
    return [value] + [fetch(value, k) for k in ORDER[1:]]


def here():
    return lax.axis_index("dp"), lax.axis_index("ctx")


def in_hbm(value):
    return pltpu.with_memory_space_constraint(value, pltpu.HBM)


def dealt(pieces, fetch):
    return [fetch(pieces[k - 1], -k) for k in (2, 1, 3)]


def call(kernel, out_shape, in_specs, out_specs, limit=16, flops=0, moved=0, **keywords):
    return pl.pallas_call(
        kernel,
        out_shape=out_shape,
        in_specs=in_specs,
        out_specs=out_specs,
        compiler_params=pltpu.CompilerParams(vmem_limit_bytes=limit * 2**20),
        cost_estimate=pl.CostEstimate(flops=flops, bytes_accessed=moved, transcendentals=0),
        **keywords,
    )


def f32(*shape):
    return jax.ShapeDtypeStruct(shape, jnp.float32)


def bf16(*shape):
    return jax.ShapeDtypeStruct(shape, jnp.bfloat16)


def slopes_of(heads):
    largest = 2 ** int(math.floor(math.log2(heads)))
    listed = [2.0 ** (-8.0 * (h + 1) / largest) for h in range(largest)]
    return listed + [2.0 ** (-4.0 * (2 * m + 1) / largest) for m in range(heads - largest)]


def thirds(value):
    high = value.astype(jnp.bfloat16)
    rest = value - high.astype(jnp.float32)
    middle = rest.astype(jnp.bfloat16)
    low = (rest - middle.astype(jnp.float32)).astype(jnp.bfloat16)
    parts = [p.astype(jnp.float32) for p in (high, middle, low)]
    return jnp.concatenate(parts, axis=0).astype(jnp.bfloat16)


def folded(products):
    rows = products.shape[0] // 3
    return products[0:rows] + products[rows : 2 * rows] + products[2 * rows :]


def attend_kernel(first, *refs):
    far = refs[3]
    lax.fori_loop(0, far.shape[0], lambda index, _: attend_doc(first + index, index, *refs), None)


def attend_doc(
    doc, index, lengths, tok, near_k, far, near_v, qk, v_turned, w, w_v_turned, w_out, gain, *refs
):
    hidden, mixed_all, normed, rstd_out, pool, keys, values, dist, hidden_here, sem = refs[-10:]
    docs, tb, width = tok.shape
    ext = tb + 2 * WIN
    own = pl.ds(pl.multiple_of(doc * tb, tb), tb)
    mixed = mixed_all.at[:, own]
    ctx = lax.axis_index("ctx")
    start, length = ctx * tb, lengths[doc]
    odd = lax.rem(ctx, 2)
    near_at = pl.ds(pl.multiple_of((1 - odd) * (WIN + tb), 128), WIN)
    far_at = pl.ds(pl.multiple_of(odd * (WIN + tb), 128), WIN)
    rows = far[index]
    keys[far_at, :] = jnp.dot(
        rows, w[:, width : 2 * width], preferred_element_type=jnp.float32
    ).astype(jnp.bfloat16)
    keys[near_at, :] = near_k[doc]
    keys[WIN : WIN + tb] = qk[doc, :, width:]
    values[:, far_at] = lax.dot_general(
        w_v_turned[...], rows, NT, preferred_element_type=jnp.float32
    ).astype(jnp.bfloat16)
    values[:, near_at] = near_v[:, own]
    values[:, WIN : WIN + tb] = v_turned[:, own]
    j = lax.broadcasted_iota(jnp.int32, (ext, tb), 0) - WIN
    away = jnp.abs(lax.broadcasted_iota(jnp.int32, (ext, tb), 1) - j)
    kpos = start + j
    seen = (away <= WIN) & (((kpos >= 0) & (kpos < length)) | (away == 0))
    dist[...] = jnp.where(seen, away.astype(jnp.float32), FAR)
    half = lax.broadcasted_iota(jnp.int32, (tb, 128), 1) < 64
    slopes = slopes_of(H)
    lanes = 128
    span = lanes + 2 * WIN

    def scores_of(pair):
        cols = pl.ds(pair * 128, 128)
        query, zero = qk[doc, :, cols] * jnp.bfloat16(0.125), jnp.bfloat16(0)
        both = jnp.concatenate([jnp.where(half, query, zero), jnp.where(half, zero, query)], axis=0)
        return lax.dot_general(keys[:, cols], both, NT, preferred_element_type=jnp.float32)

    upcoming = scores_of(0)
    for pair in range(H // 2):
        scores = upcoming
        if pair + 1 < H // 2:
            upcoming = scores_of(pair + 1)
        for part in range(2):
            columns = []
            for low in range(0, tb, lanes):
                score = scores[low : low + span, part * tb + low : part * tb + low + lanes]
                score = score - slopes[2 * pair + part] * dist[pl.ds(low, span), pl.ds(low, lanes)]
                expo = jnp.exp(score - jnp.max(score, axis=0, keepdims=True))
                weights = (expo * (1.0 / jnp.sum(expo, axis=0, keepdims=True))).astype(jnp.bfloat16)
                above, below = low, ext - span - low
                pieces = [weights]
                if above:
                    pieces = [jnp.zeros((above, lanes), jnp.bfloat16)] + pieces
                if below:
                    pieces = pieces + [jnp.zeros((below, lanes), jnp.bfloat16)]
                columns.append(jnp.concatenate(pieces, axis=0))
            weights = jnp.concatenate(columns, axis=1)
            head = pl.ds(pair * 128 + part * 64, 64)
            mixed[head, :] = jnp.dot(values[head, :], weights, preferred_element_type=jnp.float32).astype(jnp.bfloat16)
    summed = tok[doc].astype(jnp.float32) + lax.dot_general(
        mixed[...], w_out[...], TN, preferred_element_type=jnp.float32
    )
    centred = summed - jnp.mean(summed, axis=1, keepdims=True)
    rstd = lax.rsqrt(jnp.mean(centred * centred, axis=1, keepdims=True) + 1e-05)
    unit = centred * rstd
    hidden_f = unit * gain[...].reshape(1, width)
    hidden_here[...] = hidden_f.astype(jnp.bfloat16)
    leaving = pltpu.make_async_copy(hidden_here, hidden.at[doc], sem)
    leaving.start()
    normed[doc] = unit.astype(jnp.bfloat16)
    rstd_out[doc] = jnp.broadcast_to(rstd, rstd_out.shape[1:])
    keep = start + lax.broadcasted_iota(jnp.int32, (tb, 1), 0) < length
    pool[doc] = jnp.sum(jnp.where(keep, hidden_f, 0.0), axis=0, keepdims=True) / length.astype(jnp.float32)
    leaving.wait()


def attend(first, before, lengths, tokens, near_k, far, near_v, qk, v_turned, w_qkv, w_v_turned, w_out, gain):
    docs, tb, width = tokens.shape
    ext = tb + 2 * WIN
    out_shape = (bf16(docs, tb, width), bf16(width, docs * tb), bf16(docs, tb, width), f32(docs, tb, 128), f32(docs, 1, width))
    out_specs = (ANY,) + (VMEM,) * 4
    operands = [lengths, tokens, near_k, far, near_v, qk, v_turned, w_qkv, w_v_turned, w_out, gain]
    in_specs = [SMEM] + [VMEM] * 10
    aliases = {}
    if before is not None:
        aliases = {len(operands) + k: k for k in range(len(out_shape))}
        operands = operands + list(before)
        in_specs = in_specs + list(out_specs)
    return call(
        functools.partial(attend_kernel, first),
        out_shape,
        in_specs,
        out_specs,
        limit=24,
        flops=5 * 2 * far.shape[0] * tb * ext * width,
        moved=4 * 2**20,
        scratch_shapes=[
            pltpu.VMEM((ext, width), jnp.bfloat16),
            pltpu.VMEM((width, ext), jnp.bfloat16),
            pltpu.VMEM((ext, tb), jnp.float32),
            pltpu.VMEM((tb, width), jnp.bfloat16),
            pltpu.SemaphoreType.DMA,
        ],
        input_output_aliases=aliases,
        name="attend",
    )(*operands)


def near_kernel(near, w, w_v_turned, near_k, near_v):
    docs, tb, width = near.shape

    def some(doc, _):
        rows = near[doc]
        own = pl.ds(pl.multiple_of(doc * tb, tb), tb)
        near_k[doc] = jnp.dot(rows, w[:, width : 2 * width], preferred_element_type=jnp.float32).astype(jnp.bfloat16)
        near_v[:, own] = lax.dot_general(
            w_v_turned[...], rows, NT, preferred_element_type=jnp.float32
        ).astype(jnp.bfloat16)

    lax.fori_loop(0, docs, some, None)


def prepare_kernel(tok, w, qk, v_turned, w_v_turned):
    width = tok.shape[2]

    @pl.when(pl.program_id(0) == 0)
    def _():
        w_v_turned[...] = w[:, 2 * width :].T

    rows = tok[0]
    qk[0] = jnp.dot(rows, w[:, 0 : 2 * width], preferred_element_type=jnp.float32).astype(jnp.bfloat16)
    v_turned[...] = lax.dot_general(w_v_turned[...], rows, NT, preferred_element_type=jnp.float32).astype(jnp.bfloat16)


def prepare(tokens, w_qkv):
    docs, tb, width = tokens.shape
    return call(
        prepare_kernel,
        (bf16(docs, tb, 2 * width), bf16(width, docs * tb), bf16(width, width)),
        [
            pl.BlockSpec((1, tb, width), lambda i: (i, 0, 0)),
            pl.BlockSpec(w_qkv.shape, lambda i: (0, 0), pipeline_mode=pl.Buffered(1)),
        ],
        (
            pl.BlockSpec((1, tb, 2 * width), lambda i: (i, 0, 0)),
            pl.BlockSpec((width, tb), lambda i: (0, i)),
            pl.BlockSpec((width, width), lambda i: (0, 0)),
        ),
        flops=2 * docs * tb * width * 3 * width,
        moved=11 * 2**20,
        grid=(docs,),
        name="prepare",
    )(tokens, w_qkv)


def row_ids(k, shape, dim):
    dp, ctx = here()
    place = lax.broadcasted_iota(jnp.int32, shape, dim)
    return (((dp & 4) | ((dp + k) & 3)) * 16 + (ctx ^ (k // 4))) * shape[dim] + place


def stack_kernel(pool, target, out):
    docs = pool.shape[0]
    for doc in range(docs):
        out[doc : doc + 1, :] = pool[doc]
    out[docs:, :] = target[...]


def add_kernel(*refs):
    terms = [ref[...] for ref in refs[:-1]]
    if len(terms) == 4:
        terms = [terms[0] + terms[3], terms[1] + terms[2]]
    refs[-1][...] = terms[0] + terms[1]


def add(terms):
    return call(add_kernel, f32(*terms[0].shape), [VMEM] * len(terms), VMEM, limit=4, name="add")(*terms)


def merge_kernel(docs, width, *refs):
    refs[-1][...] = merge(docs, width, [ref[...] for ref in refs[:-1]])


def merged(docs, width, states):
    kernel = functools.partial(merge_kernel, docs, width)
    return call(kernel, f32(*states[0].shape), [VMEM] * len(states), VMEM, limit=4, name="merge")(*states)


def target_kernel(docs, positive, *refs):
    pieces, out = refs[:4], refs[4]
    dp, _ = here()
    total = jnp.zeros(out.shape, jnp.float32)
    for k, piece in zip(ORDER, pieces):
        shape = (out.shape[0], piece.shape[0])
        doc = lax.broadcasted_iota(jnp.int32, shape, 0)
        wanted = jnp.zeros(shape, jnp.int32)
        for d in range(2 * docs):
            wanted = jnp.where(doc == d, positive[(d // docs * 4 + (dp & 3)) * docs + d % docs], wanted)
        hit = (row_ids(k, shape, 1) == wanted).astype(jnp.float32).astype(jnp.bfloat16)
        total = total + jnp.dot(hit, piece[...], preferred_element_type=jnp.float32)
    out[...] = total


def turn_kernel(mixed, out):
    width = out.shape[0]
    rows = 192
    lax.fori_loop(0, width // rows, lambda index, _: turn_rows(index * rows, rows, mixed, out), None)


def turn_rows(low, rows, mixed, out):
    width = out.shape[0]
    place = low + lax.broadcasted_iota(jnp.int32, (rows, 1), 0)
    dp, ctx = here()
    each = width // 128
    core = (ctx & 1) ^ (place // (64 * each))
    first, second = place // (16 * each) % 4, place // (4 * each) % 4
    y = ((dp & 3) + jnp.where(core == 0, first, second)) & 3
    x = ((ctx >> 2) + jnp.where(core == 0, second, first)) & 3
    z = ((ctx & 2) + (dp >> 2) + place // each % 4) & 3
    block = ((z & 1) * 4 + y) * 16 + x * 4 + (z >> 1) * 2 + core
    chosen = block * each + place % each == lax.broadcasted_iota(jnp.int32, (rows, width), 1)
    chosen = jnp.where(chosen, 1.0, 0.0).astype(jnp.bfloat16)
    here_rows = pl.ds(pl.multiple_of(low, 64), rows)
    out[here_rows, :] = jnp.dot(chosen, mixed[...], preferred_element_type=jnp.float32).astype(jnp.bfloat16)


def norm_kernel(s0, s1, s3, s2, emb_out, rinv_out, target_out):
    docs = s0.shape[0] // 3
    dp, _ = here()
    own, other = s0[0:docs] + s2[0:docs], s1[0:docs] + s3[0:docs]
    second = dp >= 4
    pooled = jnp.concatenate([jnp.where(second, other, own), jnp.where(second, own, other)], axis=0)
    rinv = lax.rsqrt(jnp.sum(pooled * pooled, axis=1, keepdims=True) + 1e-06)
    emb_out[...] = pooled * rinv
    rinv_out[...] = jnp.broadcast_to(rinv, rinv_out.shape)
    target_out[...] = (s0[docs:] + s2[docs:]) + (s1[docs:] + s3[docs:])


def as_row(column):
    size = column.shape[0]
    same = lax.broadcasted_iota(jnp.int32, (size, size), 0) == lax.broadcasted_iota(jnp.int32, (size, size), 1)
    return jnp.sum(jnp.where(same, column, 0.0), axis=0, keepdims=True)


def score_kernel(docs, positive, *refs):
    embs, tables, (everyone, state, expos) = refs[:4], refs[4:12], refs[12:]
    all_docs, width = everyone.shape
    dp, _ = here()
    y = dp & 3
    group = embs[0].shape[0]
    for k, piece in zip(ORDER, embs):
        everyone[pl.ds(pl.multiple_of(((y + k) & 3) * group, group), group), :] = piece[...]
    rows = tables[0].shape[0]
    emb = thirds(everyone[...])
    scores = [folded(lax.dot_general(emb, t[...], NT, preferred_element_type=jnp.float32)) / TAU for t in tables]
    top = functools.reduce(jnp.maximum, [jnp.max(s, axis=1, keepdims=True) for s in scores])
    row = lax.broadcasted_iota(jnp.int32, (all_docs, rows), 0)
    wanted = jnp.zeros((all_docs, rows), jnp.int32)
    for doc in range(all_docs):
        z, rest = divmod(doc, all_docs // 2)
        wanted = jnp.where(row == rest // docs * group + z * docs + rest % docs, positive[doc], wanted)
    totals, found = [], jnp.zeros((all_docs, 1), jnp.float32)
    for k, s in enumerate(scores):
        expo = jnp.exp(s - top)
        expos[:, k * rows : (k + 1) * rows] = expo
        totals.append(jnp.sum(expo, axis=1, keepdims=True))
        hit = row_ids(ORDER[k % 4] + k // 4 * 4, (all_docs, rows), 1) == wanted
        found = found + jnp.sum(jnp.where(hit, s, 0.0), axis=1, keepdims=True)
    totals = [totals[k] + totals[k + 4] for k in range(4)]
    total = (totals[0] + totals[3]) + (totals[1] + totals[2])
    mine = thirds(expos[pl.ds(pl.multiple_of(y * group, group), group), :])
    mix = jnp.zeros((group, width), jnp.float32)
    for k, t in enumerate(tables):
        mix = mix + folded(jnp.dot(mine[:, k * rows : (k + 1) * rows], t[...], preferred_element_type=jnp.float32))
    column = lax.broadcasted_iota(jnp.int32, (group, all_docs), 1)
    own = column == lax.broadcasted_iota(jnp.int32, (group, all_docs), 0) + y * group
    total_row, top_row, found_row = as_row(total), as_row(top), as_row(found)
    state[...] = jnp.zeros_like(state)
    state[0:group, 0:width] = mix
    for place, values in ((width, total_row), (width + 128, top_row)):
        value = jnp.sum(jnp.where(own, values, 0.0), axis=1, keepdims=True)
        state[0:group, place : place + 128] = jnp.broadcast_to(value, (group, 128))
    for index, values in enumerate((total_row, top_row, found_row)):
        state[group + index : group + index + 1, 0:all_docs] = values


def merge(docs, width, states):
    row = lax.broadcasted_iota(jnp.int32, states[0].shape, 0)
    column = lax.broadcasted_iota(jnp.int32, states[0].shape, 1)
    place = width + 128
    by_row = [s[:, place : place + 1] for s in states]
    by_lane = [s[docs + 1 : docs + 2, :] for s in states]
    top_row = functools.reduce(jnp.maximum, by_row)
    top_lane = functools.reduce(jnp.maximum, by_lane)
    terms = [
        s * jnp.exp(jnp.where(row == docs, b - top_lane, a - top_row)) for s, a, b in zip(states, by_row, by_lane)
    ]
    if len(terms) == 4:
        terms = [terms[0] + terms[3], terms[1] + terms[2]]
    joined = jnp.where((row < docs) & (column >= place), top_row, terms[0] + terms[1])
    return jnp.where(row == docs + 1, top_lane, joined)


def batch_kernel(emb, everyone, product_out, stats):
    everything = everyone[...]
    all_docs = everything.shape[0]
    own = lax.dot_general(emb[...], everything, NT, precision=HIGHEST, preferred_element_type=jnp.float32) / TAU
    product = lax.dot_general(everything, everything, NT, precision=HIGHEST, preferred_element_type=jnp.float32) / TAU
    wide = (all_docs, all_docs)
    same = lax.broadcasted_iota(jnp.int32, wide, 0) == lax.broadcasted_iota(jnp.int32, wide, 1)
    product = jnp.where(same, -1e30, product)
    top = jnp.max(product, axis=0, keepdims=True)
    total = jnp.sum(jnp.exp(product - top), axis=0, keepdims=True)
    product_out[...] = own
    stats[...] = jnp.concatenate([top, total] * 4, axis=0)


def grad_kernel(
    lengths, s0, s1, s2, s3, emb, rinv, everyone, target, product, stats, gain, normed, rstd, turned,
    send_out, d_summed, loss_out,
):
    docs, tb, width = normed.shape
    all_docs, group = everyone.shape[0], emb.shape[0]
    dp, _ = here()
    mine = lambda a: jnp.where(dp >= 4, a[docs:group], a[0:docs])
    own, others = mine(emb), everyone[...]
    now = merge(group, width, [s[...] for s in (s0, s1, s2, s3)])
    total, top, found = (now[group + k : group + k + 1, 0:all_docs] for k in range(3))
    batch_top, batch_total = stats[0:1], stats[1:2]
    peak = jnp.maximum(top, batch_top)
    lse_row = peak + jnp.log(total * jnp.exp(top - peak) + batch_total * jnp.exp(batch_top - peak))
    loss_out[...] = jnp.broadcast_to(jnp.sum(lse_row - found, axis=1, keepdims=True) / all_docs, loss_out.shape)
    column = lax.broadcasted_iota(jnp.int32, (docs, all_docs), 1)
    first = (dp & 3) * group + (dp >> 2) * docs
    same = column == lax.broadcasted_iota(jnp.int32, (docs, all_docs), 0) + first
    lse = jnp.sum(jnp.where(same, lse_row, 0.0), axis=1, keepdims=True)
    scores = mine(product)
    g_batch = jnp.where(same, 0.0, jnp.exp(scores - lse) + jnp.exp(scores - lse_row)) / all_docs
    shares = mine(now)
    mix = shares[:, 0:width] * jnp.exp(shares[:, width + 128 : width + 129] - lse)
    from_batch = jnp.dot(g_batch, others, precision=HIGHEST, preferred_element_type=jnp.float32)
    d_emb = ((mix - mine(target)) / all_docs + from_batch) / TAU
    d_pooled = (d_emb - own * jnp.sum(own * d_emb, axis=1, keepdims=True)) * mine(rinv)[:, 0:1]
    for doc in range(docs):
        dy = d_pooled[doc : doc + 1] / lengths[doc].astype(jnp.float32) * gain[...].reshape(1, width)
        level = dy - jnp.mean(dy, axis=1, keepdims=True)
        unit = normed[doc].astype(jnp.float32)
        along = jnp.mean(unit * dy, axis=1, keepdims=True)
        keep = lax.axis_index("ctx") * tb + lax.broadcasted_iota(jnp.int32, (tb, 1), 0) < lengths[doc]
        scale = jnp.where(keep, rstd[doc, :, 0:1], 0.0)
        d_summed[doc * tb : (doc + 1) * tb, :] = (scale * (level - unit * along)).astype(jnp.bfloat16)
    product_rows(turned, width // 2, d_summed, send_out)


def product_rows(turned, low, d_summed, out):
    rows = 192

    def some(index, _):
        source = pl.ds(pl.multiple_of(low + index * rows, 64), rows)
        here_rows = pl.ds(pl.multiple_of(index * rows, 64), rows)
        out[here_rows, :] = jnp.dot(turned[source, :], d_summed[...], preferred_element_type=jnp.float32)

    lax.fori_loop(0, out.shape[0] // rows, some, None)


def keep_kernel(turned, d_summed, out):
    product_rows(turned, 0, d_summed, out)


def sum_kernel(count, *refs):
    terms, outs = refs[:count], refs[count:]
    total = terms[0][...].astype(jnp.float32)
    for term in terms[1:]:
        total = total + term[...].astype(jnp.float32)
    rows = outs[0].shape[0]
    for index, out in enumerate(outs):
        out[...] = total[index * rows : (index + 1) * rows].astype(out.dtype)


def sum_and_split(terms, kind):
    rows, width = terms[0].shape
    piece = (rows // 4, width)
    shapes = (f32(*piece),) + (jax.ShapeDtypeStruct(piece, kind),) * 3
    return call(
        functools.partial(sum_kernel, len(terms)), shapes, [VMEM] * len(terms), (VMEM,) * 4, limit=8, name="sum_split"
    )(*terms)


def shards(tokens, w_qkv, w_out, ln_gain, cache, positive, lengths):
    docs, tb, width = tokens.shape
    n_ctx, n_dp = lax.axis_size("ctx"), lax.axis_size("dp")
    all_docs = n_dp * docs
    ring = [(i, (i + 2 * (i % 2) - 1) % n_ctx) for i in range(n_ctx)]
    fetch = lambda part: lax.ppermute(part, "ctx", ring)
    early, middle, late = fetch(tokens[0:1]), fetch(tokens[1:3]), tokens[3:]
    near = swap(tokens, "ctx", 1)
    tables = around(cache, from_y)
    qk, v_turned, w_v_turned = prepare(in_hbm(tokens), in_hbm(w_qkv))
    near_k, near_v = call(
        near_kernel,
        (bf16(docs, tb, width), bf16(width, docs * tb)),
        [VMEM] * 3,
        (VMEM,) * 2,
        flops=4 * docs * tb * width * width,
        moved=4 * 2**20,
        name="near",
    )(near, w_qkv, w_v_turned)
    gain = ln_gain
    fixed = (lengths, tokens, near_k), (near_v, qk, v_turned, w_qkv, w_v_turned, w_out, gain)
    *done, pool = attend(0, None, *fixed[0], early, *fixed[1])
    pool, after, *tables = lax.optimization_barrier((pool, positive, *tables))
    others = [swap(table, "ctx", 1) for table in tables]
    target = call(
        functools.partial(target_kernel, docs), f32(2 * docs, width), [SMEM] + [VMEM] * 4, VMEM, name="target"
    )(after, *tables)
    middle, late, target, *others = lax.optimization_barrier((middle, late, target, *others))
    late = fetch(late)
    done = attend(1, [*done, pool], *fixed[0], middle, *fixed[1])
    done = attend(3, done, *fixed[0], late, *fixed[1])
    hidden, mixed, normed, rstd, pool = done

    turned = call(
        turn_kernel,
        bf16(width, docs * tb),
        [VMEM],
        VMEM,
        flops=2 * docs * tb * width * width,
        moved=4 * 2**20,
        name="turn",
    )(mixed)

    group = 2 * docs
    sums = call(stack_kernel, f32(docs + group, width), [VMEM, VMEM], VMEM, limit=4, name="stack")(
        pool, target
    )
    sums = add([sums, swap(sums, "ctx", 1)])
    sums = add(around(sums, from_x))
    sums, turned = lax.optimization_barrier((sums, turned))
    emb, rinv, target = call(
        norm_kernel,
        (f32(group, width), f32(group, 128), f32(group, width)),
        [VMEM] * 4,
        (VMEM,) * 3,
        limit=4,
        name="norm",
    )(*around(sums, from_z))
    embs = around(emb, from_y)
    everyone, state = call(
        functools.partial(score_kernel, docs),
        (f32(all_docs, width), f32(2 * group, width + 256)),
        [SMEM] + [VMEM] * 12,
        (VMEM, VMEM),
        moved=2 * 2**20,
        scratch_shapes=[pltpu.VMEM((all_docs, 8 * cache.shape[0]), jnp.float32)],
        name="score",
    )(positive, *embs, *tables, *others)
    product, stats = call(
        batch_kernel,
        (f32(group, all_docs), f32(8, all_docs)),
        [VMEM, VMEM],
        (VMEM, VMEM),
        limit=4,
        name="batch",
    )(emb, everyone)
    state = merged(group, width, around(state, from_x))
    half = width // 2
    send, d_summed, loss = call(
        grad_kernel,
        (f32(half, width), bf16(docs * tb, width), f32(8, 128)),
        [SMEM] + [VMEM] * 14,
        (VMEM,) * 3,
        flops=docs * tb * width * width,
        moved=8 * 2**20,
        name="grad",
    )(
        lengths, *around(state, from_z), emb, rinv, everyone, target, product, stats, gain, normed, rstd, turned,
    )
    keep = call(
        keep_kernel,
        f32(half, width),
        [VMEM, VMEM],
        VMEM,
        flops=docs * tb * width * width,
        moved=2**20,
        name="keep",
    )(turned, d_summed)
    keep, *sends = sum_and_split([keep, swap(send, "ctx", 1)], jnp.bfloat16)
    got = dealt(sends, lambda piece, k: from_plane(piece, k, False))
    keep, *sends = sum_and_split([keep] + got, jnp.float32)
    got = dealt(sends, lambda piece, k: from_plane(piece, k, True))
    keep, *sends = sum_and_split([keep] + got, jnp.float32)
    got = dealt(sends, from_z)
    return (hidden, loss[0, 0], add([keep] + got))


def solution(mesh):
    placed = (P("dp", "ctx", None), P(), P(), P(), P(("dp", "ctx"), None), P(), P("dp"))
    return jax.shard_map(
        shards,
        mesh=mesh,
        in_specs=placed,
        out_specs=(P("dp", "ctx", None), P(), P(("dp", "ctx"), None)),
        check_vma=False,
    )
```

```python
import functools
import math

import jax
import jax.numpy as jnp
from jax import lax
from jax.experimental import pallas as pl
from jax.experimental.pallas import tpu as pltpu
from jax.sharding import PartitionSpec as P

H = 12
WIN = 256
TAU = 0.02
FAR = 1e32
NT = (((1,), (1,)), ((), ()))
TN = (((0,), (0,)), ((), ()))
HIGHEST = lax.Precision.HIGHEST
VMEM = pl.BlockSpec(memory_space=pltpu.VMEM)
SMEM = pl.BlockSpec(memory_space=pltpu.SMEM)
ANY = pl.BlockSpec(memory_space=pl.ANY)

ORDER = (0, 1, 3, 2)


def swap(value, axis, bits):
    return lax.ppermute(value, axis, [(i, i ^ bits) for i in range(lax.axis_size(axis))])


def fetched(value, source, cores=(0, 1)):
    n_dp, n_ctx = lax.axis_size("dp"), lax.axis_size("ctx")
    pairs = []
    for d in range(n_dp):
        for c in range(n_ctx):
            where = source(d, c) if c % 2 in cores else (d, c)
            pairs.append((where[0] * n_ctx + where[1], d * n_ctx + c))
    return lax.ppermute(value, ("dp", "ctx"), pairs)


def at_x(k):
    return lambda d, c: (d, (c + 4 * k) % 16)


def at_y(k):
    return lambda d, c: ((d & 4) | ((d + k) & 3), c)


def at_z(k):
    def place(d, c):
        z = ((c & 2) + (d >> 2) + k) & 3
        return (z & 1) * 4 + (d & 3), (c & ~2) + (z & 2)

    return place


def at_plane(k, last):
    return lambda d, c: (at_y(k) if (c & 1 == 1) == last else at_x(k))(d, c)


def around(value, at, cores=(0, 1)):
    return [value] + [fetched(value, at(k), cores) for k in ORDER[1:]]


def dealt(pieces, at):
    return [fetched(pieces[k - 1], at(-k)) for k in (2, 1, 3)]


def here():
    return lax.axis_index("dp"), lax.axis_index("ctx")


def in_hbm(value):
    return pltpu.with_memory_space_constraint(value, pltpu.HBM)


def call(kernel, out_shape, in_specs, out_specs, limit=16, flops=0, moved=0, **keywords):
    return pl.pallas_call(
        kernel,
        out_shape=out_shape,
        in_specs=in_specs,
        out_specs=out_specs,
        compiler_params=pltpu.CompilerParams(vmem_limit_bytes=limit * 2**20),
        cost_estimate=pl.CostEstimate(flops=flops, bytes_accessed=moved, transcendentals=0),
        **keywords,
    )


def f32(*shape):
    return jax.ShapeDtypeStruct(shape, jnp.float32)


def bf16(*shape):
    return jax.ShapeDtypeStruct(shape, jnp.bfloat16)


def slopes_of(heads):
    largest = 2 ** int(math.floor(math.log2(heads)))
    listed = [2.0 ** (-8.0 * (h + 1) / largest) for h in range(largest)]
    return listed + [2.0 ** (-4.0 * (2 * m + 1) / largest) for m in range(heads - largest)]


def thirds(value):
    high = value.astype(jnp.bfloat16)
    rest = value - high.astype(jnp.float32)
    middle = rest.astype(jnp.bfloat16)
    low = (rest - middle.astype(jnp.float32)).astype(jnp.bfloat16)
    parts = [p.astype(jnp.float32) for p in (high, middle, low)]
    return jnp.concatenate(parts, axis=0).astype(jnp.bfloat16)


def folded(products):
    rows = products.shape[0] // 3
    return products[0:rows] + products[rows : 2 * rows] + products[2 * rows :]


def attend_kernel(first, *refs):
    far = refs[3]
    lax.fori_loop(0, far.shape[0], lambda index, _: attend_doc(first + index, index, *refs), None)


def attend_doc(
    doc, index, lengths, tok, near_k, far, near_v, qk, v_turned, w, w_v_turned, w_out, gain, *refs
):
    hidden, mixed_all, normed, rstd_out, pool, keys, values, dist, hidden_here, sem = refs[-10:]
    docs, tb, width = tok.shape
    ext = tb + 2 * WIN
    own = pl.ds(pl.multiple_of(doc * tb, tb), tb)
    mixed = mixed_all.at[:, own]
    ctx = lax.axis_index("ctx")
    start, length = ctx * tb, lengths[doc]
    odd = lax.rem(ctx, 2)
    near_at = pl.ds(pl.multiple_of((1 - odd) * (WIN + tb), 128), WIN)
    far_at = pl.ds(pl.multiple_of(odd * (WIN + tb), 128), WIN)
    rows = far[index]
    keys[far_at, :] = jnp.dot(
        rows, w[:, width : 2 * width], preferred_element_type=jnp.float32
    ).astype(jnp.bfloat16)
    keys[near_at, :] = near_k[doc]
    keys[WIN : WIN + tb] = qk[doc, :, width:]
    values[:, far_at] = lax.dot_general(
        w_v_turned[...], rows, NT, preferred_element_type=jnp.float32
    ).astype(jnp.bfloat16)
    values[:, near_at] = near_v[:, own]
    values[:, WIN : WIN + tb] = v_turned[:, own]
    j = lax.broadcasted_iota(jnp.int32, (ext, tb), 0) - WIN
    away = jnp.abs(lax.broadcasted_iota(jnp.int32, (ext, tb), 1) - j)
    kpos = start + j
    seen = (away <= WIN) & (((kpos >= 0) & (kpos < length)) | (away == 0))
    dist[...] = jnp.where(seen, away.astype(jnp.float32), FAR)
    half = lax.broadcasted_iota(jnp.int32, (tb, 128), 1) < 64
    slopes = slopes_of(H)
    lanes = 128
    span = lanes + 2 * WIN

    def scores_of(pair):
        cols = pl.ds(pair * 128, 128)
        query, zero = qk[doc, :, cols] * jnp.bfloat16(0.125), jnp.bfloat16(0)
        both = jnp.concatenate([jnp.where(half, query, zero), jnp.where(half, zero, query)], axis=0)
        return lax.dot_general(keys[:, cols], both, NT, preferred_element_type=jnp.float32)

    upcoming = scores_of(0)
    for pair in range(H // 2):
        scores = upcoming
        if pair + 1 < H // 2:
            upcoming = scores_of(pair + 1)
        for part in range(2):
            columns = []
            for low in range(0, tb, lanes):
                score = scores[low : low + span, part * tb + low : part * tb + low + lanes]
                score = score - slopes[2 * pair + part] * dist[pl.ds(low, span), pl.ds(low, lanes)]
                expo = jnp.exp(score - jnp.max(score, axis=0, keepdims=True))
                weights = (expo * (1.0 / jnp.sum(expo, axis=0, keepdims=True))).astype(jnp.bfloat16)
                above, below = low, ext - span - low
                pieces = [weights]
                if above:
                    pieces = [jnp.zeros((above, lanes), jnp.bfloat16)] + pieces
                if below:
                    pieces = pieces + [jnp.zeros((below, lanes), jnp.bfloat16)]
                columns.append(jnp.concatenate(pieces, axis=0))
            weights = jnp.concatenate(columns, axis=1)
            head = pl.ds(pair * 128 + part * 64, 64)
            mixed[head, :] = jnp.dot(values[head, :], weights, preferred_element_type=jnp.float32).astype(jnp.bfloat16)
    summed = tok[doc].astype(jnp.float32) + lax.dot_general(
        mixed[...], w_out[...], TN, preferred_element_type=jnp.float32
    )
    centred = summed - jnp.mean(summed, axis=1, keepdims=True)
    rstd = lax.rsqrt(jnp.mean(centred * centred, axis=1, keepdims=True) + 1e-05)
    unit = centred * rstd
    hidden_f = unit * gain[...].reshape(1, width)
    hidden_here[...] = hidden_f.astype(jnp.bfloat16)
    leaving = pltpu.make_async_copy(hidden_here, hidden.at[doc], sem)
    leaving.start()
    normed[doc] = unit.astype(jnp.bfloat16)
    rstd_out[doc] = jnp.broadcast_to(rstd, rstd_out.shape[1:])
    keep = start + lax.broadcasted_iota(jnp.int32, (tb, 1), 0) < length
    pool[doc] = jnp.sum(jnp.where(keep, hidden_f, 0.0), axis=0, keepdims=True) / length.astype(jnp.float32)
    leaving.wait()


def attend(first, before, lengths, tokens, near_k, far, near_v, qk, v_turned, w_qkv, w_v_turned, w_out, gain):
    docs, tb, width = tokens.shape
    ext = tb + 2 * WIN
    out_shape = (bf16(docs, tb, width), bf16(width, docs * tb), bf16(docs, tb, width), f32(docs, tb, 128), f32(docs, 1, width))
    out_specs = (ANY,) + (VMEM,) * 4
    operands = [lengths, tokens, near_k, far, near_v, qk, v_turned, w_qkv, w_v_turned, w_out, gain]
    in_specs = [SMEM] + [VMEM] * 10
    aliases = {}
    if before is not None:
        aliases = {len(operands) + k: k for k in range(len(out_shape))}
        operands = operands + list(before)
        in_specs = in_specs + list(out_specs)
    return call(
        functools.partial(attend_kernel, first),
        out_shape,
        in_specs,
        out_specs,
        limit=24,
        flops=5 * 2 * far.shape[0] * tb * ext * width,
        moved=4 * 2**20,
        scratch_shapes=[
            pltpu.VMEM((ext, width), jnp.bfloat16),
            pltpu.VMEM((width, ext), jnp.bfloat16),
            pltpu.VMEM((ext, tb), jnp.float32),
            pltpu.VMEM((tb, width), jnp.bfloat16),
            pltpu.SemaphoreType.DMA,
        ],
        input_output_aliases=aliases,
        name="attend",
    )(*operands)


def near_kernel(near, w, w_v_turned, near_k, near_v):
    docs, tb, width = near.shape

    def some(doc, _):
        rows = near[doc]
        own = pl.ds(pl.multiple_of(doc * tb, tb), tb)
        near_k[doc] = jnp.dot(rows, w[:, width : 2 * width], preferred_element_type=jnp.float32).astype(jnp.bfloat16)
        near_v[:, own] = lax.dot_general(
            w_v_turned[...], rows, NT, preferred_element_type=jnp.float32
        ).astype(jnp.bfloat16)

    lax.fori_loop(0, docs, some, None)


def prepare_kernel(tok, w, qk, v_turned, w_v_turned):
    width = tok.shape[2]

    @pl.when(pl.program_id(0) == 0)
    def _():
        w_v_turned[...] = w[:, 2 * width :].T

    rows = tok[0]
    qk[0] = jnp.dot(rows, w[:, 0 : 2 * width], preferred_element_type=jnp.float32).astype(jnp.bfloat16)
    v_turned[...] = lax.dot_general(w_v_turned[...], rows, NT, preferred_element_type=jnp.float32).astype(jnp.bfloat16)


def prepare(tokens, w_qkv):
    docs, tb, width = tokens.shape
    return call(
        prepare_kernel,
        (bf16(docs, tb, 2 * width), bf16(width, docs * tb), bf16(width, width)),
        [
            pl.BlockSpec((1, tb, width), lambda i: (i, 0, 0)),
            pl.BlockSpec(w_qkv.shape, lambda i: (0, 0), pipeline_mode=pl.Buffered(1)),
        ],
        (
            pl.BlockSpec((1, tb, 2 * width), lambda i: (i, 0, 0)),
            pl.BlockSpec((width, tb), lambda i: (0, i)),
            pl.BlockSpec((width, width), lambda i: (0, 0)),
        ),
        flops=2 * docs * tb * width * 3 * width,
        moved=11 * 2**20,
        grid=(docs,),
        name="prepare",
    )(tokens, w_qkv)


def row_ids(k, shape, dim):
    dp, ctx = here()
    place = lax.broadcasted_iota(jnp.int32, shape, dim)
    return (((dp & 4) | ((dp + k) & 3)) * 16 + (ctx ^ (k // 4))) * shape[dim] + place


def stack_kernel(pool, target, out):
    docs = pool.shape[0]
    for doc in range(docs):
        out[doc : doc + 1, :] = pool[doc]
    out[docs:, :] = target[...]


def add_kernel(*refs):
    terms = [ref[...] for ref in refs[:-1]]
    if len(terms) == 4:
        terms = [terms[0] + terms[3], terms[1] + terms[2]]
    refs[-1][...] = terms[0] + terms[1]


def add(terms):
    return call(add_kernel, f32(*terms[0].shape), [VMEM] * len(terms), VMEM, limit=4, name="add")(*terms)


def merge_kernel(docs, width, *refs):
    refs[-1][...] = merge(docs, width, [ref[...] for ref in refs[:-1]])


def merged(docs, width, states):
    kernel = functools.partial(merge_kernel, docs, width)
    return call(kernel, f32(*states[0].shape), [VMEM] * len(states), VMEM, limit=4, name="merge")(*states)


def target_kernel(docs, positive, *refs):
    pieces, out = refs[:4], refs[4]
    dp, _ = here()
    total = jnp.zeros(out.shape, jnp.float32)
    for k, piece in zip(ORDER, pieces):
        shape = (out.shape[0], piece.shape[0])
        doc = lax.broadcasted_iota(jnp.int32, shape, 0)
        wanted = jnp.zeros(shape, jnp.int32)
        for d in range(2 * docs):
            wanted = jnp.where(doc == d, positive[(d // docs * 4 + (dp & 3)) * docs + d % docs], wanted)
        hit = (row_ids(k, shape, 1) == wanted).astype(jnp.float32).astype(jnp.bfloat16)
        total = total + jnp.dot(hit, piece[...], preferred_element_type=jnp.float32)
    out[...] = total


def turn_kernel(mixed, out):
    width = out.shape[0]
    rows = 384
    lax.fori_loop(0, width // rows, lambda index, _: turn_rows(index * rows, rows, mixed, out), None)


def turn_rows(low, rows, mixed, out):
    width = out.shape[0]
    place = low + lax.broadcasted_iota(jnp.int32, (rows, 1), 0)
    dp, ctx = here()
    each = width // 128
    core = (ctx & 1) ^ (place // (64 * each))
    first, second = place // (16 * each) % 4, place // (4 * each) % 4
    y = ((dp & 3) + jnp.where(core == 0, first, second)) & 3
    x = ((ctx >> 2) + jnp.where(core == 0, second, first)) & 3
    z = ((ctx & 2) + (dp >> 2) + place // each % 4) & 3
    block = ((z & 1) * 4 + y) * 16 + x * 4 + (z >> 1) * 2 + core
    chosen = block * each + place % each == lax.broadcasted_iota(jnp.int32, (rows, width), 1)
    chosen = jnp.where(chosen, 1.0, 0.0).astype(jnp.bfloat16)
    here_rows = pl.ds(pl.multiple_of(low, 64), rows)
    out[here_rows, :] = jnp.dot(chosen, mixed[...], preferred_element_type=jnp.float32).astype(jnp.bfloat16)


def norm_kernel(s0, s1, s3, s2, emb_out, rinv_out, target_out):
    docs = s0.shape[0] // 3
    dp, _ = here()
    own, other = s0[0:docs] + s2[0:docs], s1[0:docs] + s3[0:docs]
    second = dp >= 4
    pooled = jnp.concatenate([jnp.where(second, other, own), jnp.where(second, own, other)], axis=0)
    rinv = lax.rsqrt(jnp.sum(pooled * pooled, axis=1, keepdims=True) + 1e-06)
    emb_out[...] = pooled * rinv
    rinv_out[...] = jnp.broadcast_to(rinv, rinv_out.shape)
    target_out[...] = (s0[docs:] + s2[docs:]) + (s1[docs:] + s3[docs:])


def as_row(column):
    size = column.shape[0]
    same = lax.broadcasted_iota(jnp.int32, (size, size), 0) == lax.broadcasted_iota(jnp.int32, (size, size), 1)
    return jnp.sum(jnp.where(same, column, 0.0), axis=0, keepdims=True)


def score_kernel(docs, positive, *refs):
    embs, tables, (everyone, state, expos) = refs[:4], refs[4:12], refs[12:]
    all_docs, width = everyone.shape
    dp, _ = here()
    y = dp & 3
    group = embs[0].shape[0]
    for k, piece in zip(ORDER, embs):
        everyone[pl.ds(pl.multiple_of(((y + k) & 3) * group, group), group), :] = piece[...]
    rows = tables[0].shape[0]
    emb = thirds(everyone[...])
    scores = [folded(lax.dot_general(emb, t[...], NT, preferred_element_type=jnp.float32)) / TAU for t in tables]
    top = functools.reduce(jnp.maximum, [jnp.max(s, axis=1, keepdims=True) for s in scores])
    row = lax.broadcasted_iota(jnp.int32, (all_docs, rows), 0)
    wanted = jnp.zeros((all_docs, rows), jnp.int32)
    for doc in range(all_docs):
        z, rest = divmod(doc, all_docs // 2)
        wanted = jnp.where(row == rest // docs * group + z * docs + rest % docs, positive[doc], wanted)
    totals, found = [], jnp.zeros((all_docs, 1), jnp.float32)
    for k, s in enumerate(scores):
        expo = jnp.exp(s - top)
        expos[:, k * rows : (k + 1) * rows] = expo
        totals.append(jnp.sum(expo, axis=1, keepdims=True))
        hit = row_ids(ORDER[k % 4] + k // 4 * 4, (all_docs, rows), 1) == wanted
        found = found + jnp.sum(jnp.where(hit, s, 0.0), axis=1, keepdims=True)
    totals = [totals[k] + totals[k + 4] for k in range(4)]
    total = (totals[0] + totals[3]) + (totals[1] + totals[2])
    mine = thirds(expos[pl.ds(pl.multiple_of(y * group, group), group), :])
    mix = jnp.zeros((group, width), jnp.float32)
    for k, t in enumerate(tables):
        mix = mix + folded(jnp.dot(mine[:, k * rows : (k + 1) * rows], t[...], preferred_element_type=jnp.float32))
    column = lax.broadcasted_iota(jnp.int32, (group, all_docs), 1)
    own = column == lax.broadcasted_iota(jnp.int32, (group, all_docs), 0) + y * group
    total_row, top_row, found_row = as_row(total), as_row(top), as_row(found)
    state[...] = jnp.zeros_like(state)
    state[0:group, 0:width] = mix
    for place, values in ((width, total_row), (width + 128, top_row)):
        value = jnp.sum(jnp.where(own, values, 0.0), axis=1, keepdims=True)
        state[0:group, place : place + 128] = jnp.broadcast_to(value, (group, 128))
    for index, values in enumerate((total_row, top_row, found_row)):
        state[group + index : group + index + 1, 0:all_docs] = values


def merge(docs, width, states):
    row = lax.broadcasted_iota(jnp.int32, states[0].shape, 0)
    column = lax.broadcasted_iota(jnp.int32, states[0].shape, 1)
    place = width + 128
    by_row = [s[:, place : place + 1] for s in states]
    by_lane = [s[docs + 1 : docs + 2, :] for s in states]
    top_row = functools.reduce(jnp.maximum, by_row)
    top_lane = functools.reduce(jnp.maximum, by_lane)
    terms = [
        s * jnp.exp(jnp.where(row == docs, b - top_lane, a - top_row)) for s, a, b in zip(states, by_row, by_lane)
    ]
    if len(terms) == 4:
        terms = [terms[0] + terms[3], terms[1] + terms[2]]
    joined = jnp.where((row < docs) & (column >= place), top_row, terms[0] + terms[1])
    return jnp.where(row == docs + 1, top_lane, joined)


def batch_kernel(emb, everyone, product_out, stats):
    everything = everyone[...]
    all_docs = everything.shape[0]
    own = lax.dot_general(emb[...], everything, NT, precision=HIGHEST, preferred_element_type=jnp.float32) / TAU
    product = lax.dot_general(everything, everything, NT, precision=HIGHEST, preferred_element_type=jnp.float32) / TAU
    wide = (all_docs, all_docs)
    same = lax.broadcasted_iota(jnp.int32, wide, 0) == lax.broadcasted_iota(jnp.int32, wide, 1)
    product = jnp.where(same, -1e30, product)
    top = jnp.max(product, axis=0, keepdims=True)
    total = jnp.sum(jnp.exp(product - top), axis=0, keepdims=True)
    product_out[...] = own
    stats[...] = jnp.concatenate([top, total] * 4, axis=0)


def pack_kernel(s0, s1, s2, s3, emb, rinv, everyone, target, product, stats, out):
    group, width = emb.shape
    all_docs = everyone.shape[0]
    out[0 : 2 * group, :] = merge(group, width, [s[...] for s in (s0, s1, s2, s3)])
    for low, rows in ((2 * group, emb), (3 * group, target)):
        out[low : low + group, 0:width] = rows[...]
    out[4 * group :, 0:width] = everyone[...]
    out[2 * group :, width:] = jnp.zeros((2 * group + all_docs, 256), jnp.float32)
    out[2 * group : 3 * group, width : width + 128] = rinv[...]
    out[2 * group : 3 * group, width + 128 : width + 128 + all_docs] = product[...]
    out[3 * group : 4 * group, width + 128 : width + 128 + all_docs] = stats[...]


def grad_kernel(
    lengths, packed, other, gain, normed, rstd, turned, send_out, d_summed, loss_out,
):
    docs, tb, width = normed.shape
    group = 2 * docs
    all_docs = packed.shape[0] - 4 * group
    dp, ctx = here()
    known = jnp.where(lax.rem(ctx, 2) == 1, packed[...], other[...])
    now, emb, target = known[0 : 2 * group], known[2 * group : 3 * group], known[3 * group : 4 * group]
    rinv, scored = emb[:, width : width + 128], emb[:, width + 128 : width + 128 + all_docs]
    stats = target[:, width + 128 : width + 128 + all_docs]
    emb, target, others = emb[:, 0:width], target[:, 0:width], known[4 * group :, 0:width]
    mine = lambda a: jnp.where(dp >= 4, a[docs:group], a[0:docs])
    own = mine(emb)
    total, top, found = (now[group + k : group + k + 1, 0:all_docs] for k in range(3))
    batch_top, batch_total = stats[0:1], stats[1:2]
    peak = jnp.maximum(top, batch_top)
    lse_row = peak + jnp.log(total * jnp.exp(top - peak) + batch_total * jnp.exp(batch_top - peak))
    loss_out[...] = jnp.broadcast_to(jnp.sum(lse_row - found, axis=1, keepdims=True) / all_docs, loss_out.shape)
    column = lax.broadcasted_iota(jnp.int32, (docs, all_docs), 1)
    first = (dp & 3) * group + (dp >> 2) * docs
    same = column == lax.broadcasted_iota(jnp.int32, (docs, all_docs), 0) + first
    lse = jnp.sum(jnp.where(same, lse_row, 0.0), axis=1, keepdims=True)
    scores = mine(scored)
    g_batch = jnp.where(same, 0.0, jnp.exp(scores - lse) + jnp.exp(scores - lse_row)) / all_docs
    shares = mine(now)
    mix = shares[:, 0:width] * jnp.exp(shares[:, width + 128 : width + 129] - lse)
    from_batch = jnp.dot(g_batch, others, precision=HIGHEST, preferred_element_type=jnp.float32)
    d_emb = ((mix - mine(target)) / all_docs + from_batch) / TAU
    d_pooled = (d_emb - own * jnp.sum(own * d_emb, axis=1, keepdims=True)) * mine(rinv)[:, 0:1]
    for doc in range(docs):
        dy = d_pooled[doc : doc + 1] / lengths[doc].astype(jnp.float32) * gain[...].reshape(1, width)
        level = dy - jnp.mean(dy, axis=1, keepdims=True)
        unit = normed[doc].astype(jnp.float32)
        along = jnp.mean(unit * dy, axis=1, keepdims=True)
        keep = lax.axis_index("ctx") * tb + lax.broadcasted_iota(jnp.int32, (tb, 1), 0) < lengths[doc]
        scale = jnp.where(keep, rstd[doc, :, 0:1], 0.0)
        d_summed[doc * tb : (doc + 1) * tb, :] = (scale * (level - unit * along)).astype(jnp.bfloat16)
    product_rows(turned, width // 2, d_summed, send_out)


def product_rows(turned, low, d_summed, out):
    rows = 192

    def some(index, _):
        source = pl.ds(pl.multiple_of(low + index * rows, 64), rows)
        here_rows = pl.ds(pl.multiple_of(index * rows, 64), rows)
        out[here_rows, :] = jnp.dot(turned[source, :], d_summed[...], preferred_element_type=jnp.float32)

    lax.fori_loop(0, out.shape[0] // rows, some, None)


def keep_kernel(turned, d_summed, out):
    product_rows(turned, 0, d_summed, out)


def sum_kernel(count, *refs):
    terms, outs = refs[:count], refs[count:]
    total = terms[0][...].astype(jnp.float32)
    for term in terms[1:]:
        total = total + term[...].astype(jnp.float32)
    rows = outs[0].shape[0]
    for index, out in enumerate(outs):
        out[...] = total[index * rows : (index + 1) * rows].astype(out.dtype)


def sum_and_split(terms, kind):
    rows, width = terms[0].shape
    piece = (rows // 4, width)
    shapes = (f32(*piece),) + (jax.ShapeDtypeStruct(piece, kind),) * 3
    return call(
        functools.partial(sum_kernel, len(terms)), shapes, [VMEM] * len(terms), (VMEM,) * 4, limit=8, name="sum_split"
    )(*terms)


def shards(tokens, w_qkv, w_out, ln_gain, cache, positive, lengths):
    docs, tb, width = tokens.shape
    n_ctx, n_dp = lax.axis_size("ctx"), lax.axis_size("dp")
    all_docs = n_dp * docs
    ring = [(i, (i + 2 * (i % 2) - 1) % n_ctx) for i in range(n_ctx)]
    fetch = lambda part: lax.ppermute(part, "ctx", ring)
    early, middle, late = fetch(tokens[0:1]), fetch(tokens[1:3]), tokens[3:]
    near = swap(tokens, "ctx", 1)
    tables = around(cache, at_y)
    qk, v_turned, w_v_turned = prepare(in_hbm(tokens), in_hbm(w_qkv))
    near_k, near_v = call(
        near_kernel,
        (bf16(docs, tb, width), bf16(width, docs * tb)),
        [VMEM] * 3,
        (VMEM,) * 2,
        flops=4 * docs * tb * width * width,
        moved=4 * 2**20,
        name="near",
    )(near, w_qkv, w_v_turned)
    gain = ln_gain
    fixed = (lengths, tokens, near_k), (near_v, qk, v_turned, w_qkv, w_v_turned, w_out, gain)
    *done, pool = attend(0, None, *fixed[0], early, *fixed[1])
    pool, after, *tables = lax.optimization_barrier((pool, positive, *tables))
    others = [swap(table, "ctx", 1) for table in tables]
    target = call(
        functools.partial(target_kernel, docs), f32(2 * docs, width), [SMEM] + [VMEM] * 4, VMEM, name="target"
    )(after, *tables)
    middle, late, target, *others = lax.optimization_barrier((middle, late, target, *others))
    late = fetch(late)
    done = attend(1, [*done, pool], *fixed[0], middle, *fixed[1])
    done = attend(3, done, *fixed[0], late, *fixed[1])
    hidden, mixed, normed, rstd, pool = done

    turned = call(
        turn_kernel,
        bf16(width, docs * tb),
        [VMEM],
        VMEM,
        flops=2 * docs * tb * width * width,
        moved=4 * 2**20,
        name="turn",
    )(mixed)

    group = 2 * docs
    sums = call(stack_kernel, f32(docs + group, width), [VMEM, VMEM], VMEM, limit=4, name="stack")(
        pool, target
    )
    sums = add([sums, swap(sums, "ctx", 1)])
    sums = add(around(sums, at_x, (1,)))
    sums, turned = lax.optimization_barrier((sums, turned))
    emb, rinv, target = call(
        norm_kernel,
        (f32(group, width), f32(group, 128), f32(group, width)),
        [VMEM] * 4,
        (VMEM,) * 3,
        limit=4,
        name="norm",
    )(*around(sums, at_z, (1,)))
    embs = around(emb, at_y, (1,))
    everyone, state = call(
        functools.partial(score_kernel, docs),
        (f32(all_docs, width), f32(2 * group, width + 256)),
        [SMEM] + [VMEM] * 12,
        (VMEM, VMEM),
        moved=2 * 2**20,
        scratch_shapes=[pltpu.VMEM((all_docs, 8 * cache.shape[0]), jnp.float32)],
        name="score",
    )(positive, *embs, *tables, *others)
    product, stats = call(
        batch_kernel,
        (f32(group, all_docs), f32(8, all_docs)),
        [VMEM, VMEM],
        (VMEM, VMEM),
        limit=4,
        name="batch",
    )(emb, everyone)
    state = merged(group, width, around(state, at_x, (1,)))
    packed = call(
        pack_kernel,
        f32(4 * group + all_docs, width + 256),
        [VMEM] * 10,
        VMEM,
        limit=4,
        name="pack",
    )(*around(state, at_z, (1,)), emb, rinv, everyone, target, product, stats)
    half = width // 2
    send, d_summed, loss = call(
        grad_kernel,
        (f32(half, width), bf16(docs * tb, width), f32(8, 128)),
        [SMEM] + [VMEM] * 6,
        (VMEM,) * 3,
        flops=docs * tb * width * width,
        moved=8 * 2**20,
        name="grad",
    )(
        lengths, packed, swap(packed, "ctx", 1), gain, normed, rstd, turned,
    )
    keep = call(
        keep_kernel,
        f32(half, width),
        [VMEM, VMEM],
        VMEM,
        flops=docs * tb * width * width,
        moved=2**20,
        name="keep",
    )(turned, d_summed)
    keep, *sends = sum_and_split([keep, swap(send, "ctx", 1)], jnp.bfloat16)
    got = dealt(sends, lambda k: at_plane(k, False))
    keep, *sends = sum_and_split([keep] + got, jnp.float32)
    got = dealt(sends, lambda k: at_plane(k, True))
    keep, *sends = sum_and_split([keep] + got, jnp.float32)
    got = dealt(sends, at_z)
    return (hidden, loss[0, 0], add([keep] + got))


def solution(mesh):
    placed = (P("dp", "ctx", None), P(), P(), P(), P(("dp", "ctx"), None), P(), P("dp"))
    return jax.shard_map(
        shards,
        mesh=mesh,
        in_specs=placed,
        out_specs=(P("dp", "ctx", None), P(), P(("dp", "ctx"), None)),
        check_vma=False,
    )
```

```python
import functools
import math

import jax
import jax.numpy as jnp
from jax import lax
from jax.experimental import pallas as pl
from jax.experimental.pallas import tpu as pltpu
from jax.sharding import PartitionSpec as P

H = 12
WIN = 256
TAU = 0.02
FAR = 1e32
NT = (((1,), (1,)), ((), ()))
TN = (((0,), (0,)), ((), ()))
HIGHEST = lax.Precision.HIGHEST
VMEM = pl.BlockSpec(memory_space=pltpu.VMEM)
SMEM = pl.BlockSpec(memory_space=pltpu.SMEM)
ANY = pl.BlockSpec(memory_space=pl.ANY)

ORDER = (0, 1, 3, 2)


def swap(value, axis, bits):
    return lax.ppermute(value, axis, [(i, i ^ bits) for i in range(lax.axis_size(axis))])


def from_x(value, k):
    size = lax.axis_size("ctx")
    return lax.ppermute(value, "ctx", [((c + 4 * k) % size, c) for c in range(size)])


def from_y(value, k):
    return lax.ppermute(value, "dp", [((d & 4) | ((d + k) & 3), d) for d in range(lax.axis_size("dp"))])


def from_z(value, k):
    n_dp, n_ctx = lax.axis_size("dp"), lax.axis_size("ctx")
    pairs = []
    for d in range(n_dp):
        for c in range(n_ctx):
            z = ((c & 2) + (d >> 2) + k) & 3
            pairs.append((((z & 1) * 4 + (d & 3)) * n_ctx + (c & ~2) + (z & 2), d * n_ctx + c))
    return lax.ppermute(value, ("dp", "ctx"), pairs)


def from_plane(value, k, last):
    n_dp, n_ctx = lax.axis_size("dp"), lax.axis_size("ctx")
    pairs = []
    for d in range(n_dp):
        for c in range(n_ctx):
            along_y = (c & 1 == 1) == last
            source = ((d & 4) | ((d + k) & 3), c) if along_y else (d, (c + 4 * k) % n_ctx)
            pairs.append((source[0] * n_ctx + source[1], d * n_ctx + c))
    return lax.ppermute(value, ("dp", "ctx"), pairs)


def around(value, fetch):
    return [value] + [fetch(value, k) for k in ORDER[1:]]


def here():
    return lax.axis_index("dp"), lax.axis_index("ctx")


def in_hbm(value):
    return pltpu.with_memory_space_constraint(value, pltpu.HBM)


def dealt(pieces, fetch):
    return [fetch(pieces[k - 1], -k) for k in (2, 1, 3)]


def call(kernel, out_shape, in_specs, out_specs, limit=16, flops=0, moved=0, **keywords):
    return pl.pallas_call(
        kernel,
        out_shape=out_shape,
        in_specs=in_specs,
        out_specs=out_specs,
        compiler_params=pltpu.CompilerParams(vmem_limit_bytes=limit * 2**20),
        cost_estimate=pl.CostEstimate(flops=flops, bytes_accessed=moved, transcendentals=0),
        **keywords,
    )


def f32(*shape):
    return jax.ShapeDtypeStruct(shape, jnp.float32)


def bf16(*shape):
    return jax.ShapeDtypeStruct(shape, jnp.bfloat16)


def slopes_of(heads):
    largest = 2 ** int(math.floor(math.log2(heads)))
    listed = [2.0 ** (-8.0 * (h + 1) / largest) for h in range(largest)]
    return listed + [2.0 ** (-4.0 * (2 * m + 1) / largest) for m in range(heads - largest)]


def thirds(value):
    high = value.astype(jnp.bfloat16)
    rest = value - high.astype(jnp.float32)
    middle = rest.astype(jnp.bfloat16)
    low = (rest - middle.astype(jnp.float32)).astype(jnp.bfloat16)
    parts = [p.astype(jnp.float32) for p in (high, middle, low)]
    return jnp.concatenate(parts, axis=0).astype(jnp.bfloat16)


def folded(products):
    rows = products.shape[0] // 3
    return products[0:rows] + products[rows : 2 * rows] + products[2 * rows :]


def attend_kernel(first, *refs):
    far = refs[3]
    lax.fori_loop(0, far.shape[0], lambda index, _: attend_doc(first + index, index, *refs), None)


def attend_doc(
    doc, index, lengths, tok, near_k, far, near_v, qk, v_turned, w, w_v_turned, w_out, gain, *refs
):
    hidden, mixed_all, normed, rstd_out, pool, keys, values, dist, hidden_here, sem = refs[-10:]
    docs, tb, width = tok.shape
    ext = tb + 2 * WIN
    own = pl.ds(pl.multiple_of(doc * tb, tb), tb)
    mixed = mixed_all.at[:, own]
    ctx = lax.axis_index("ctx")
    start, length = ctx * tb, lengths[doc]
    odd = lax.rem(ctx, 2)
    near_at = pl.ds(pl.multiple_of((1 - odd) * (WIN + tb), 128), WIN)
    far_at = pl.ds(pl.multiple_of(odd * (WIN + tb), 128), WIN)
    rows = far[index]
    keys[far_at, :] = jnp.dot(
        rows, w[:, width : 2 * width], preferred_element_type=jnp.float32
    ).astype(jnp.bfloat16)
    keys[near_at, :] = near_k[doc]
    keys[WIN : WIN + tb] = qk[doc, :, width:]
    values[:, far_at] = lax.dot_general(
        w_v_turned[...], rows, NT, preferred_element_type=jnp.float32
    ).astype(jnp.bfloat16)
    values[:, near_at] = near_v[:, own]
    values[:, WIN : WIN + tb] = v_turned[:, own]
    j = lax.broadcasted_iota(jnp.int32, (ext, tb), 0) - WIN
    away = jnp.abs(lax.broadcasted_iota(jnp.int32, (ext, tb), 1) - j)
    kpos = start + j
    seen = (away <= WIN) & (((kpos >= 0) & (kpos < length)) | (away == 0))
    dist[...] = jnp.where(seen, away.astype(jnp.float32), FAR)
    half = lax.broadcasted_iota(jnp.int32, (tb, 128), 1) < 64
    slopes = slopes_of(H)
    lanes = 128
    span = lanes + 2 * WIN

    def scores_of(pair):
        cols = pl.ds(pair * 128, 128)
        query, zero = qk[doc, :, cols] * jnp.bfloat16(0.125), jnp.bfloat16(0)
        both = jnp.concatenate([jnp.where(half, query, zero), jnp.where(half, zero, query)], axis=0)
        return lax.dot_general(keys[:, cols], both, NT, preferred_element_type=jnp.float32)

    upcoming = scores_of(0)
    for pair in range(H // 2):
        scores = upcoming
        if pair + 1 < H // 2:
            upcoming = scores_of(pair + 1)
        for part in range(2):
            columns = []
            for low in range(0, tb, lanes):
                score = scores[low : low + span, part * tb + low : part * tb + low + lanes]
                score = score - slopes[2 * pair + part] * dist[pl.ds(low, span), pl.ds(low, lanes)]
                expo = jnp.exp(score - jnp.max(score, axis=0, keepdims=True))
                weights = (expo * (1.0 / jnp.sum(expo, axis=0, keepdims=True))).astype(jnp.bfloat16)
                above, below = low, ext - span - low
                pieces = [weights]
                if above:
                    pieces = [jnp.zeros((above, lanes), jnp.bfloat16)] + pieces
                if below:
                    pieces = pieces + [jnp.zeros((below, lanes), jnp.bfloat16)]
                columns.append(jnp.concatenate(pieces, axis=0))
            weights = jnp.concatenate(columns, axis=1)
            head = pl.ds(pair * 128 + part * 64, 64)
            mixed[head, :] = jnp.dot(values[head, :], weights, preferred_element_type=jnp.float32).astype(jnp.bfloat16)
    summed = tok[doc].astype(jnp.float32) + lax.dot_general(
        mixed[...], w_out[...], TN, preferred_element_type=jnp.float32
    )
    centred = summed - jnp.mean(summed, axis=1, keepdims=True)
    rstd = lax.rsqrt(jnp.mean(centred * centred, axis=1, keepdims=True) + 1e-05)
    unit = centred * rstd
    hidden_f = unit * gain[...].reshape(1, width)
    hidden_here[...] = hidden_f.astype(jnp.bfloat16)
    leaving = pltpu.make_async_copy(hidden_here, hidden.at[doc], sem)
    leaving.start()
    normed[doc] = unit.astype(jnp.bfloat16)
    rstd_out[doc] = jnp.broadcast_to(rstd, rstd_out.shape[1:])
    keep = start + lax.broadcasted_iota(jnp.int32, (tb, 1), 0) < length
    pool[doc] = jnp.sum(jnp.where(keep, hidden_f, 0.0), axis=0, keepdims=True) / length.astype(jnp.float32)
    leaving.wait()


def attend(first, before, lengths, tokens, near_k, far, near_v, qk, v_turned, w_qkv, w_v_turned, w_out, gain):
    docs, tb, width = tokens.shape
    ext = tb + 2 * WIN
    out_shape = (bf16(docs, tb, width), bf16(width, docs * tb), bf16(docs, tb, width), f32(docs, tb, 128), f32(docs, 1, width))
    out_specs = (ANY,) + (VMEM,) * 4
    operands = [lengths, tokens, near_k, far, near_v, qk, v_turned, w_qkv, w_v_turned, w_out, gain]
    in_specs = [SMEM] + [VMEM] * 10
    aliases = {}
    if before is not None:
        aliases = {len(operands) + k: k for k in range(len(out_shape))}
        operands = operands + list(before)
        in_specs = in_specs + list(out_specs)
    return call(
        functools.partial(attend_kernel, first),
        out_shape,
        in_specs,
        out_specs,
        limit=24,
        flops=5 * 2 * far.shape[0] * tb * ext * width,
        moved=4 * 2**20,
        scratch_shapes=[
            pltpu.VMEM((ext, width), jnp.bfloat16),
            pltpu.VMEM((width, ext), jnp.bfloat16),
            pltpu.VMEM((ext, tb), jnp.float32),
            pltpu.VMEM((tb, width), jnp.bfloat16),
            pltpu.SemaphoreType.DMA,
        ],
        input_output_aliases=aliases,
        name="attend",
    )(*operands)


def near_kernel(near, w, w_v_turned, near_k, near_v):
    docs, tb, width = near.shape

    def some(doc, _):
        rows = near[doc]
        own = pl.ds(pl.multiple_of(doc * tb, tb), tb)
        near_k[doc] = jnp.dot(rows, w[:, width : 2 * width], preferred_element_type=jnp.float32).astype(jnp.bfloat16)
        near_v[:, own] = lax.dot_general(
            w_v_turned[...], rows, NT, preferred_element_type=jnp.float32
        ).astype(jnp.bfloat16)

    lax.fori_loop(0, docs, some, None)


def prepare_kernel(tok, w, qk, v_turned, w_v_turned):
    width = tok.shape[2]

    @pl.when(pl.program_id(0) == 0)
    def _():
        w_v_turned[...] = w[:, 2 * width :].T

    rows = tok[0]
    qk[0] = jnp.dot(rows, w[:, 0 : 2 * width], preferred_element_type=jnp.float32).astype(jnp.bfloat16)
    v_turned[...] = lax.dot_general(w_v_turned[...], rows, NT, preferred_element_type=jnp.float32).astype(jnp.bfloat16)


def prepare(tokens, w_qkv):
    docs, tb, width = tokens.shape
    return call(
        prepare_kernel,
        (bf16(docs, tb, 2 * width), bf16(width, docs * tb), bf16(width, width)),
        [
            pl.BlockSpec((1, tb, width), lambda i: (i, 0, 0)),
            pl.BlockSpec(w_qkv.shape, lambda i: (0, 0), pipeline_mode=pl.Buffered(1)),
        ],
        (
            pl.BlockSpec((1, tb, 2 * width), lambda i: (i, 0, 0)),
            pl.BlockSpec((width, tb), lambda i: (0, i)),
            pl.BlockSpec((width, width), lambda i: (0, 0)),
        ),
        flops=2 * docs * tb * width * 3 * width,
        moved=11 * 2**20,
        grid=(docs,),
        name="prepare",
    )(tokens, w_qkv)


def row_ids(k, shape, dim):
    dp, ctx = here()
    place = lax.broadcasted_iota(jnp.int32, shape, dim)
    return (((dp & 4) | ((dp + k) & 3)) * 16 + (ctx ^ (k // 4))) * shape[dim] + place


def stack_kernel(pool, target, out):
    docs = pool.shape[0]
    for doc in range(docs):
        out[doc : doc + 1, :] = pool[doc]
    out[docs:, :] = target[...]


def add_kernel(*refs):
    terms = [ref[...] for ref in refs[:-1]]
    if len(terms) == 4:
        terms = [terms[0] + terms[3], terms[1] + terms[2]]
    refs[-1][...] = terms[0] + terms[1]


def add(terms):
    return call(add_kernel, f32(*terms[0].shape), [VMEM] * len(terms), VMEM, limit=4, name="add")(*terms)


def merge_kernel(docs, width, *refs):
    refs[-1][...] = merge(docs, width, [ref[...] for ref in refs[:-1]])


def merged(docs, width, states):
    kernel = functools.partial(merge_kernel, docs, width)
    return call(kernel, f32(*states[0].shape), [VMEM] * len(states), VMEM, limit=4, name="merge")(*states)


def target_kernel(docs, positive, *refs):
    pieces, out = refs[:4], refs[4]
    dp, _ = here()
    total = jnp.zeros(out.shape, jnp.float32)
    for k, piece in zip(ORDER, pieces):
        shape = (out.shape[0], piece.shape[0])
        doc = lax.broadcasted_iota(jnp.int32, shape, 0)
        wanted = jnp.zeros(shape, jnp.int32)
        for d in range(2 * docs):
            wanted = jnp.where(doc == d, positive[(d // docs * 4 + (dp & 3)) * docs + d % docs], wanted)
        hit = (row_ids(k, shape, 1) == wanted).astype(jnp.float32).astype(jnp.bfloat16)
        total = total + jnp.dot(hit, piece[...], preferred_element_type=jnp.float32)
    out[...] = total


def turn_kernel(mixed, out):
    width = out.shape[0]
    rows = 384
    lax.fori_loop(0, width // rows, lambda index, _: turn_rows(index * rows, rows, mixed, out), None)


def turn_rows(low, rows, mixed, out):
    width = out.shape[0]
    place = low + lax.broadcasted_iota(jnp.int32, (rows, 1), 0)
    dp, ctx = here()
    each = width // 128
    core = (ctx & 1) ^ (place // (64 * each))
    first, second = place // (16 * each) % 4, place // (4 * each) % 4
    y = ((dp & 3) + jnp.where(core == 0, first, second)) & 3
    x = ((ctx >> 2) + jnp.where(core == 0, second, first)) & 3
    z = ((ctx & 2) + (dp >> 2) + place // each % 4) & 3
    block = ((z & 1) * 4 + y) * 16 + x * 4 + (z >> 1) * 2 + core
    chosen = block * each + place % each == lax.broadcasted_iota(jnp.int32, (rows, width), 1)
    chosen = jnp.where(chosen, 1.0, 0.0).astype(jnp.bfloat16)
    here_rows = pl.ds(pl.multiple_of(low, 64), rows)
    out[here_rows, :] = jnp.dot(chosen, mixed[...], preferred_element_type=jnp.float32).astype(jnp.bfloat16)


def norm_kernel(s0, s1, s3, s2, emb_out, rinv_out, target_out):
    docs = s0.shape[0] // 3
    dp, _ = here()
    own, other = s0[0:docs] + s2[0:docs], s1[0:docs] + s3[0:docs]
    second = dp >= 4
    pooled = jnp.concatenate([jnp.where(second, other, own), jnp.where(second, own, other)], axis=0)
    rinv = lax.rsqrt(jnp.sum(pooled * pooled, axis=1, keepdims=True) + 1e-06)
    emb_out[...] = pooled * rinv
    rinv_out[...] = jnp.broadcast_to(rinv, rinv_out.shape)
    target_out[...] = (s0[docs:] + s2[docs:]) + (s1[docs:] + s3[docs:])


def as_row(column):
    size = column.shape[0]
    same = lax.broadcasted_iota(jnp.int32, (size, size), 0) == lax.broadcasted_iota(jnp.int32, (size, size), 1)
    return jnp.sum(jnp.where(same, column, 0.0), axis=0, keepdims=True)


def score_kernel(docs, positive, *refs):
    embs, tables, (everyone, state, expos) = refs[:4], refs[4:12], refs[12:]
    all_docs, width = everyone.shape
    dp, _ = here()
    y = dp & 3
    group = embs[0].shape[0]
    for k, piece in zip(ORDER, embs):
        everyone[pl.ds(pl.multiple_of(((y + k) & 3) * group, group), group), :] = piece[...]
    rows = tables[0].shape[0]
    emb = thirds(everyone[...])
    scores = [folded(lax.dot_general(emb, t[...], NT, preferred_element_type=jnp.float32)) / TAU for t in tables]
    top = functools.reduce(jnp.maximum, [jnp.max(s, axis=1, keepdims=True) for s in scores])
    row = lax.broadcasted_iota(jnp.int32, (all_docs, rows), 0)
    wanted = jnp.zeros((all_docs, rows), jnp.int32)
    for doc in range(all_docs):
        z, rest = divmod(doc, all_docs // 2)
        wanted = jnp.where(row == rest // docs * group + z * docs + rest % docs, positive[doc], wanted)
    totals, found = [], jnp.zeros((all_docs, 1), jnp.float32)
    for k, s in enumerate(scores):
        expo = jnp.exp(s - top)
        expos[:, k * rows : (k + 1) * rows] = expo
        totals.append(jnp.sum(expo, axis=1, keepdims=True))
        hit = row_ids(ORDER[k % 4] + k // 4 * 4, (all_docs, rows), 1) == wanted
        found = found + jnp.sum(jnp.where(hit, s, 0.0), axis=1, keepdims=True)
    totals = [totals[k] + totals[k + 4] for k in range(4)]
    total = (totals[0] + totals[3]) + (totals[1] + totals[2])
    mine = thirds(expos[pl.ds(pl.multiple_of(y * group, group), group), :])
    mix = jnp.zeros((group, width), jnp.float32)
    for k, t in enumerate(tables):
        mix = mix + folded(jnp.dot(mine[:, k * rows : (k + 1) * rows], t[...], preferred_element_type=jnp.float32))
    column = lax.broadcasted_iota(jnp.int32, (group, all_docs), 1)
    own = column == lax.broadcasted_iota(jnp.int32, (group, all_docs), 0) + y * group
    total_row, top_row, found_row = as_row(total), as_row(top), as_row(found)
    state[...] = jnp.zeros_like(state)
    state[0:group, 0:width] = mix
    for place, values in ((width, total_row), (width + 128, top_row)):
        value = jnp.sum(jnp.where(own, values, 0.0), axis=1, keepdims=True)
        state[0:group, place : place + 128] = jnp.broadcast_to(value, (group, 128))
    for index, values in enumerate((total_row, top_row, found_row)):
        state[group + index : group + index + 1, 0:all_docs] = values


def merge(docs, width, states):
    row = lax.broadcasted_iota(jnp.int32, states[0].shape, 0)
    column = lax.broadcasted_iota(jnp.int32, states[0].shape, 1)
    place = width + 128
    by_row = [s[:, place : place + 1] for s in states]
    by_lane = [s[docs + 1 : docs + 2, :] for s in states]
    top_row = functools.reduce(jnp.maximum, by_row)
    top_lane = functools.reduce(jnp.maximum, by_lane)
    terms = [
        s * jnp.exp(jnp.where(row == docs, b - top_lane, a - top_row)) for s, a, b in zip(states, by_row, by_lane)
    ]
    if len(terms) == 4:
        terms = [terms[0] + terms[3], terms[1] + terms[2]]
    joined = jnp.where((row < docs) & (column >= place), top_row, terms[0] + terms[1])
    return jnp.where(row == docs + 1, top_lane, joined)


def batch_kernel(emb, everyone, product_out, stats):
    everything = everyone[...]
    all_docs = everything.shape[0]
    own = lax.dot_general(emb[...], everything, NT, precision=HIGHEST, preferred_element_type=jnp.float32) / TAU
    product = lax.dot_general(everything, everything, NT, precision=HIGHEST, preferred_element_type=jnp.float32) / TAU
    wide = (all_docs, all_docs)
    same = lax.broadcasted_iota(jnp.int32, wide, 0) == lax.broadcasted_iota(jnp.int32, wide, 1)
    product = jnp.where(same, -1e30, product)
    top = jnp.max(product, axis=0, keepdims=True)
    total = jnp.sum(jnp.exp(product - top), axis=0, keepdims=True)
    product_out[...] = own
    stats[...] = jnp.concatenate([top, total] * 4, axis=0)


def grad_kernel(
    lengths, s0, s1, s2, s3, emb, rinv, everyone, target, product, stats, gain, normed, rstd, turned,
    send_out, d_summed, loss_out,
):
    docs, tb, width = normed.shape
    all_docs, group = everyone.shape[0], emb.shape[0]
    dp, _ = here()
    mine = lambda a: jnp.where(dp >= 4, a[docs:group], a[0:docs])
    own, others = mine(emb), everyone[...]
    now = merge(group, width, [s[...] for s in (s0, s1, s2, s3)])
    total, top, found = (now[group + k : group + k + 1, 0:all_docs] for k in range(3))
    batch_top, batch_total = stats[0:1], stats[1:2]
    peak = jnp.maximum(top, batch_top)
    lse_row = peak + jnp.log(total * jnp.exp(top - peak) + batch_total * jnp.exp(batch_top - peak))
    loss_out[...] = jnp.broadcast_to(jnp.sum(lse_row - found, axis=1, keepdims=True) / all_docs, loss_out.shape)
    column = lax.broadcasted_iota(jnp.int32, (docs, all_docs), 1)
    first = (dp & 3) * group + (dp >> 2) * docs
    same = column == lax.broadcasted_iota(jnp.int32, (docs, all_docs), 0) + first
    lse = jnp.sum(jnp.where(same, lse_row, 0.0), axis=1, keepdims=True)
    scores = mine(product)
    g_batch = jnp.where(same, 0.0, jnp.exp(scores - lse) + jnp.exp(scores - lse_row)) / all_docs
    shares = mine(now)
    mix = shares[:, 0:width] * jnp.exp(shares[:, width + 128 : width + 129] - lse)
    from_batch = jnp.dot(g_batch, others, precision=HIGHEST, preferred_element_type=jnp.float32)
    d_emb = ((mix - mine(target)) / all_docs + from_batch) / TAU
    d_pooled = (d_emb - own * jnp.sum(own * d_emb, axis=1, keepdims=True)) * mine(rinv)[:, 0:1]
    for doc in range(docs):
        dy = d_pooled[doc : doc + 1] / lengths[doc].astype(jnp.float32) * gain[...].reshape(1, width)
        level = dy - jnp.mean(dy, axis=1, keepdims=True)
        unit = normed[doc].astype(jnp.float32)
        along = jnp.mean(unit * dy, axis=1, keepdims=True)
        keep = lax.axis_index("ctx") * tb + lax.broadcasted_iota(jnp.int32, (tb, 1), 0) < lengths[doc]
        scale = jnp.where(keep, rstd[doc, :, 0:1], 0.0)
        d_summed[doc * tb : (doc + 1) * tb, :] = (scale * (level - unit * along)).astype(jnp.bfloat16)
    product_rows(turned, width // 2, d_summed, send_out)


def product_rows(turned, low, d_summed, out):
    rows = 192

    def some(index, _):
        source = pl.ds(pl.multiple_of(low + index * rows, 64), rows)
        here_rows = pl.ds(pl.multiple_of(index * rows, 64), rows)
        out[here_rows, :] = jnp.dot(turned[source, :], d_summed[...], preferred_element_type=jnp.float32)

    lax.fori_loop(0, out.shape[0] // rows, some, None)


def keep_kernel(turned, d_summed, out):
    product_rows(turned, 0, d_summed, out)


def sum_kernel(count, *refs):
    terms, outs = refs[:count], refs[count:]
    total = terms[0][...].astype(jnp.float32)
    for term in terms[1:]:
        total = total + term[...].astype(jnp.float32)
    rows = outs[0].shape[0]
    for index, out in enumerate(outs):
        out[...] = total[index * rows : (index + 1) * rows].astype(out.dtype)


def sum_and_split(terms, kind):
    rows, width = terms[0].shape
    piece = (rows // 4, width)
    shapes = (f32(*piece),) + (jax.ShapeDtypeStruct(piece, kind),) * 3
    return call(
        functools.partial(sum_kernel, len(terms)), shapes, [VMEM] * len(terms), (VMEM,) * 4, limit=8, name="sum_split"
    )(*terms)


def shards(tokens, w_qkv, w_out, ln_gain, cache, positive, lengths):
    docs, tb, width = tokens.shape
    n_ctx, n_dp = lax.axis_size("ctx"), lax.axis_size("dp")
    all_docs = n_dp * docs
    ring = [(i, (i + 2 * (i % 2) - 1) % n_ctx) for i in range(n_ctx)]
    fetch = lambda part: lax.ppermute(part, "ctx", ring)
    early, middle, late = fetch(tokens[0:1]), fetch(tokens[1:3]), tokens[3:]
    near = swap(tokens, "ctx", 1)
    tables = around(cache, from_y)
    qk, v_turned, w_v_turned = prepare(in_hbm(tokens), in_hbm(w_qkv))
    near_k, near_v = call(
        near_kernel,
        (bf16(docs, tb, width), bf16(width, docs * tb)),
        [VMEM] * 3,
        (VMEM,) * 2,
        flops=4 * docs * tb * width * width,
        moved=4 * 2**20,
        name="near",
    )(near, w_qkv, w_v_turned)
    gain = ln_gain
    fixed = (lengths, tokens, near_k), (near_v, qk, v_turned, w_qkv, w_v_turned, w_out, gain)
    *done, pool = attend(0, None, *fixed[0], early, *fixed[1])
    pool, after, *tables = lax.optimization_barrier((pool, positive, *tables))
    others = [swap(table, "ctx", 1) for table in tables]
    target = call(
        functools.partial(target_kernel, docs), f32(2 * docs, width), [SMEM] + [VMEM] * 4, VMEM, name="target"
    )(after, *tables)
    middle, late, target, *others = lax.optimization_barrier((middle, late, target, *others))
    late = fetch(late)
    done = attend(1, [*done, pool], *fixed[0], middle, *fixed[1])
    done = attend(3, done, *fixed[0], late, *fixed[1])
    hidden, mixed, normed, rstd, pool = done

    turned = call(
        turn_kernel,
        bf16(width, docs * tb),
        [VMEM],
        VMEM,
        flops=2 * docs * tb * width * width,
        moved=4 * 2**20,
        name="turn",
    )(mixed)

    group = 2 * docs
    sums = call(stack_kernel, f32(docs + group, width), [VMEM, VMEM], VMEM, limit=4, name="stack")(
        pool, target
    )
    sums = add([sums, swap(sums, "ctx", 1)])
    sums = add(around(sums, from_x))
    emb, rinv, target = call(
        norm_kernel,
        (f32(group, width), f32(group, 128), f32(group, width)),
        [VMEM] * 4,
        (VMEM,) * 3,
        limit=4,
        name="norm",
    )(*around(sums, from_z))
    embs = around(emb, from_y)
    everyone, state = call(
        functools.partial(score_kernel, docs),
        (f32(all_docs, width), f32(2 * group, width + 256)),
        [SMEM] + [VMEM] * 12,
        (VMEM, VMEM),
        moved=2 * 2**20,
        scratch_shapes=[pltpu.VMEM((all_docs, 8 * cache.shape[0]), jnp.float32)],
        name="score",
    )(positive, *embs, *tables, *others)
    product, stats = call(
        batch_kernel,
        (f32(group, all_docs), f32(8, all_docs)),
        [VMEM, VMEM],
        (VMEM, VMEM),
        limit=4,
        name="batch",
    )(emb, everyone)
    state = merged(group, width, around(state, from_x))
    half = width // 2
    send, d_summed, loss = call(
        grad_kernel,
        (f32(half, width), bf16(docs * tb, width), f32(8, 128)),
        [SMEM] + [VMEM] * 14,
        (VMEM,) * 3,
        flops=docs * tb * width * width,
        moved=8 * 2**20,
        name="grad",
    )(
        lengths, *around(state, from_z), emb, rinv, everyone, target, product, stats, gain, normed, rstd, turned,
    )
    keep = call(
        keep_kernel,
        f32(half, width),
        [VMEM, VMEM],
        VMEM,
        flops=docs * tb * width * width,
        moved=2**20,
        name="keep",
    )(turned, d_summed)
    keep, *sends = sum_and_split([keep, swap(send, "ctx", 1)], jnp.bfloat16)
    got = dealt(sends, lambda piece, k: from_plane(piece, k, False))
    keep, *sends = sum_and_split([keep] + got, jnp.float32)
    got = dealt(sends, lambda piece, k: from_plane(piece, k, True))
    keep, *sends = sum_and_split([keep] + got, jnp.float32)
    got = dealt(sends, from_z)
    return (hidden, loss[0, 0], add([keep] + got))


def solution(mesh):
    placed = (P("dp", "ctx", None), P(), P(), P(), P(("dp", "ctx"), None), P(), P("dp"))
    return jax.shard_map(
        shards,
        mesh=mesh,
        in_specs=placed,
        out_specs=(P("dp", "ctx", None), P(), P(("dp", "ctx"), None)),
        check_vma=False,
    )
```

```python
import functools
import math

import jax
import jax.numpy as jnp
from jax import lax
from jax.experimental import pallas as pl
from jax.experimental.pallas import tpu as pltpu
from jax.sharding import PartitionSpec as P

H = 12
WIN = 256
TAU = 0.02
FAR = 1e32
NT = (((1,), (1,)), ((), ()))
TN = (((0,), (0,)), ((), ()))
HIGHEST = lax.Precision.HIGHEST
VMEM = pl.BlockSpec(memory_space=pltpu.VMEM)
SMEM = pl.BlockSpec(memory_space=pltpu.SMEM)
ANY = pl.BlockSpec(memory_space=pl.ANY)

ORDER = (0, 1, 3, 2)


def swap(value, axis, bits):
    return lax.ppermute(value, axis, [(i, i ^ bits) for i in range(lax.axis_size(axis))])


def from_x(value, k):
    size = lax.axis_size("ctx")
    return lax.ppermute(value, "ctx", [((c + 4 * k) % size, c) for c in range(size)])


def from_y(value, k):
    return lax.ppermute(value, "dp", [((d & 4) | ((d + k) & 3), d) for d in range(lax.axis_size("dp"))])


def from_z(value, k):
    n_dp, n_ctx = lax.axis_size("dp"), lax.axis_size("ctx")
    pairs = []
    for d in range(n_dp):
        for c in range(n_ctx):
            z = ((c & 2) + (d >> 2) + k) & 3
            pairs.append((((z & 1) * 4 + (d & 3)) * n_ctx + (c & ~2) + (z & 2), d * n_ctx + c))
    return lax.ppermute(value, ("dp", "ctx"), pairs)


def from_plane(value, k, last):
    n_dp, n_ctx = lax.axis_size("dp"), lax.axis_size("ctx")
    pairs = []
    for d in range(n_dp):
        for c in range(n_ctx):
            along_y = (c & 1 == 1) == last
            source = ((d & 4) | ((d + k) & 3), c) if along_y else (d, (c + 4 * k) % n_ctx)
            pairs.append((source[0] * n_ctx + source[1], d * n_ctx + c))
    return lax.ppermute(value, ("dp", "ctx"), pairs)


def around(value, fetch):
    return [value] + [fetch(value, k) for k in ORDER[1:]]


def here():
    return lax.axis_index("dp"), lax.axis_index("ctx")


def in_hbm(value):
    return pltpu.with_memory_space_constraint(value, pltpu.HBM)


def dealt(pieces, fetch):
    return [fetch(pieces[k - 1], -k) for k in (2, 1, 3)]


def call(kernel, out_shape, in_specs, out_specs, limit=16, flops=0, moved=0, **keywords):
    return pl.pallas_call(
        kernel,
        out_shape=out_shape,
        in_specs=in_specs,
        out_specs=out_specs,
        compiler_params=pltpu.CompilerParams(vmem_limit_bytes=limit * 2**20),
        cost_estimate=pl.CostEstimate(flops=flops, bytes_accessed=moved, transcendentals=0),
        **keywords,
    )


def f32(*shape):
    return jax.ShapeDtypeStruct(shape, jnp.float32)


def bf16(*shape):
    return jax.ShapeDtypeStruct(shape, jnp.bfloat16)


def slopes_of(heads):
    largest = 2 ** int(math.floor(math.log2(heads)))
    listed = [2.0 ** (-8.0 * (h + 1) / largest) for h in range(largest)]
    return listed + [2.0 ** (-4.0 * (2 * m + 1) / largest) for m in range(heads - largest)]


def thirds(value):
    high = value.astype(jnp.bfloat16)
    rest = value - high.astype(jnp.float32)
    middle = rest.astype(jnp.bfloat16)
    low = (rest - middle.astype(jnp.float32)).astype(jnp.bfloat16)
    parts = [p.astype(jnp.float32) for p in (high, middle, low)]
    return jnp.concatenate(parts, axis=0).astype(jnp.bfloat16)


def folded(products):
    rows = products.shape[0] // 3
    return products[0:rows] + products[rows : 2 * rows] + products[2 * rows :]


def attend_kernel(first, *refs):
    far = refs[3]
    lax.fori_loop(0, far.shape[0], lambda index, _: attend_doc(first + index, index, *refs), None)


def attend_doc(
    doc, index, lengths, tok, near_k, far, near_v, qk, v_turned, w, w_v_turned, w_out, gain, *refs
):
    hidden, mixed_all, normed, rstd_out, pool, keys, values, dist, hidden_here, sem = refs[-10:]
    docs, tb, width = tok.shape
    ext = tb + 2 * WIN
    own = pl.ds(pl.multiple_of(doc * tb, tb), tb)
    mixed = mixed_all.at[:, own]
    ctx = lax.axis_index("ctx")
    start, length = ctx * tb, lengths[doc]
    odd = lax.rem(ctx, 2)
    near_at = pl.ds(pl.multiple_of((1 - odd) * (WIN + tb), 128), WIN)
    far_at = pl.ds(pl.multiple_of(odd * (WIN + tb), 128), WIN)
    rows = far[index]
    keys[far_at, :] = jnp.dot(
        rows, w[:, width : 2 * width], preferred_element_type=jnp.float32
    ).astype(jnp.bfloat16)
    keys[near_at, :] = near_k[doc]
    keys[WIN : WIN + tb] = qk[doc, :, width:]
    values[:, far_at] = lax.dot_general(
        w_v_turned[...], rows, NT, preferred_element_type=jnp.float32
    ).astype(jnp.bfloat16)
    values[:, near_at] = near_v[:, own]
    values[:, WIN : WIN + tb] = v_turned[:, own]
    j = lax.broadcasted_iota(jnp.int32, (ext, tb), 0) - WIN
    away = jnp.abs(lax.broadcasted_iota(jnp.int32, (ext, tb), 1) - j)
    kpos = start + j
    seen = (away <= WIN) & (((kpos >= 0) & (kpos < length)) | (away == 0))
    dist[...] = jnp.where(seen, away.astype(jnp.float32), FAR)
    half = lax.broadcasted_iota(jnp.int32, (tb, 128), 1) < 64
    slopes = slopes_of(H)
    lanes = 128
    span = lanes + 2 * WIN

    def scores_of(pair):
        cols = pl.ds(pair * 128, 128)
        query, zero = qk[doc, :, cols] * jnp.bfloat16(0.125), jnp.bfloat16(0)
        both = jnp.concatenate([jnp.where(half, query, zero), jnp.where(half, zero, query)], axis=0)
        return lax.dot_general(keys[:, cols], both, NT, preferred_element_type=jnp.float32)

    upcoming = scores_of(0)
    for pair in range(H // 2):
        scores = upcoming
        if pair + 1 < H // 2:
            upcoming = scores_of(pair + 1)
        for part in range(2):
            columns = []
            for low in range(0, tb, lanes):
                score = scores[low : low + span, part * tb + low : part * tb + low + lanes]
                score = score - slopes[2 * pair + part] * dist[pl.ds(low, span), pl.ds(low, lanes)]
                expo = jnp.exp(score - jnp.max(score, axis=0, keepdims=True))
                weights = (expo * (1.0 / jnp.sum(expo, axis=0, keepdims=True))).astype(jnp.bfloat16)
                above, below = low, ext - span - low
                pieces = [weights]
                if above:
                    pieces = [jnp.zeros((above, lanes), jnp.bfloat16)] + pieces
                if below:
                    pieces = pieces + [jnp.zeros((below, lanes), jnp.bfloat16)]
                columns.append(jnp.concatenate(pieces, axis=0))
            weights = jnp.concatenate(columns, axis=1)
            head = pl.ds(pair * 128 + part * 64, 64)
            mixed[head, :] = jnp.dot(values[head, :], weights, preferred_element_type=jnp.float32).astype(jnp.bfloat16)
    summed = tok[doc].astype(jnp.float32) + lax.dot_general(
        mixed[...], w_out[...], TN, preferred_element_type=jnp.float32
    )
    centred = summed - jnp.mean(summed, axis=1, keepdims=True)
    rstd = lax.rsqrt(jnp.mean(centred * centred, axis=1, keepdims=True) + 1e-05)
    unit = centred * rstd
    hidden_f = unit * gain[...].reshape(1, width)
    hidden_here[...] = hidden_f.astype(jnp.bfloat16)
    leaving = pltpu.make_async_copy(hidden_here, hidden.at[doc], sem)
    leaving.start()
    normed[doc] = unit.astype(jnp.bfloat16)
    rstd_out[doc] = jnp.broadcast_to(rstd, rstd_out.shape[1:])
    keep = start + lax.broadcasted_iota(jnp.int32, (tb, 1), 0) < length
    pool[doc] = jnp.sum(jnp.where(keep, hidden_f, 0.0), axis=0, keepdims=True) / length.astype(jnp.float32)
    leaving.wait()


def attend(first, before, lengths, tokens, near_k, far, near_v, qk, v_turned, w_qkv, w_v_turned, w_out, gain):
    docs, tb, width = tokens.shape
    ext = tb + 2 * WIN
    out_shape = (bf16(docs, tb, width), bf16(width, docs * tb), bf16(docs, tb, width), f32(docs, tb, 128), f32(docs, 1, width))
    out_specs = (ANY,) + (VMEM,) * 4
    operands = [lengths, tokens, near_k, far, near_v, qk, v_turned, w_qkv, w_v_turned, w_out, gain]
    in_specs = [SMEM] + [VMEM] * 10
    aliases = {}
    if before is not None:
        aliases = {len(operands) + k: k for k in range(len(out_shape))}
        operands = operands + list(before)
        in_specs = in_specs + list(out_specs)
    return call(
        functools.partial(attend_kernel, first),
        out_shape,
        in_specs,
        out_specs,
        limit=24,
        flops=5 * 2 * far.shape[0] * tb * ext * width,
        moved=4 * 2**20,
        scratch_shapes=[
            pltpu.VMEM((ext, width), jnp.bfloat16),
            pltpu.VMEM((width, ext), jnp.bfloat16),
            pltpu.VMEM((ext, tb), jnp.float32),
            pltpu.VMEM((tb, width), jnp.bfloat16),
            pltpu.SemaphoreType.DMA,
        ],
        input_output_aliases=aliases,
        name="attend",
    )(*operands)


def near_kernel(near, w, w_v_turned, near_k, near_v):
    docs, tb, width = near.shape

    def some(doc, _):
        rows = near[doc]
        own = pl.ds(pl.multiple_of(doc * tb, tb), tb)
        near_k[doc] = jnp.dot(rows, w[:, width : 2 * width], preferred_element_type=jnp.float32).astype(jnp.bfloat16)
        near_v[:, own] = lax.dot_general(
            w_v_turned[...], rows, NT, preferred_element_type=jnp.float32
        ).astype(jnp.bfloat16)

    lax.fori_loop(0, docs, some, None)


def prepare_kernel(tok, w, qk, v_turned, w_v_turned):
    width = tok.shape[2]

    @pl.when(pl.program_id(0) == 0)
    def _():
        w_v_turned[...] = w[:, 2 * width :].T

    rows = tok[0]
    qk[0] = jnp.dot(rows, w[:, 0 : 2 * width], preferred_element_type=jnp.float32).astype(jnp.bfloat16)
    v_turned[...] = lax.dot_general(w_v_turned[...], rows, NT, preferred_element_type=jnp.float32).astype(jnp.bfloat16)


def prepare(tokens, w_qkv):
    docs, tb, width = tokens.shape
    return call(
        prepare_kernel,
        (bf16(docs, tb, 2 * width), bf16(width, docs * tb), bf16(width, width)),
        [
            pl.BlockSpec((1, tb, width), lambda i: (i, 0, 0)),
            pl.BlockSpec(w_qkv.shape, lambda i: (0, 0), pipeline_mode=pl.Buffered(1)),
        ],
        (
            pl.BlockSpec((1, tb, 2 * width), lambda i: (i, 0, 0)),
            pl.BlockSpec((width, tb), lambda i: (0, i)),
            pl.BlockSpec((width, width), lambda i: (0, 0)),
        ),
        flops=2 * docs * tb * width * 3 * width,
        moved=11 * 2**20,
        grid=(docs,),
        name="prepare",
    )(tokens, w_qkv)


def row_ids(k, shape, dim):
    dp, ctx = here()
    place = lax.broadcasted_iota(jnp.int32, shape, dim)
    return (((dp & 4) | ((dp + k) & 3)) * 16 + (ctx ^ (k // 4))) * shape[dim] + place


def stack_kernel(pool, target, out):
    docs = pool.shape[0]
    for doc in range(docs):
        out[doc : doc + 1, :] = pool[doc]
    out[docs:, :] = target[...]


def add_kernel(*refs):
    terms = [ref[...] for ref in refs[:-1]]
    if len(terms) == 4:
        terms = [terms[0] + terms[3], terms[1] + terms[2]]
    refs[-1][...] = terms[0] + terms[1]


def add(terms):
    return call(add_kernel, f32(*terms[0].shape), [VMEM] * len(terms), VMEM, limit=4, name="add")(*terms)


def merge_kernel(docs, width, *refs):
    refs[-1][...] = merge(docs, width, [ref[...] for ref in refs[:-1]])


def merged(docs, width, states):
    kernel = functools.partial(merge_kernel, docs, width)
    return call(kernel, f32(*states[0].shape), [VMEM] * len(states), VMEM, limit=4, name="merge")(*states)


def target_kernel(docs, positive, *refs):
    pieces, out = refs[:4], refs[4]
    dp, _ = here()
    total = jnp.zeros(out.shape, jnp.float32)
    for k, piece in zip(ORDER, pieces):
        shape = (out.shape[0], piece.shape[0])
        doc = lax.broadcasted_iota(jnp.int32, shape, 0)
        wanted = jnp.zeros(shape, jnp.int32)
        for d in range(2 * docs):
            wanted = jnp.where(doc == d, positive[(d // docs * 4 + (dp & 3)) * docs + d % docs], wanted)
        hit = (row_ids(k, shape, 1) == wanted).astype(jnp.float32).astype(jnp.bfloat16)
        total = total + jnp.dot(hit, piece[...], preferred_element_type=jnp.float32)
    out[...] = total


def turn_kernel(mixed, out):
    width = out.shape[0]
    rows = 384
    lax.fori_loop(0, width // rows, lambda index, _: turn_rows(index * rows, rows, mixed, out), None)


def turn_rows(low, rows, mixed, out):
    width = out.shape[0]
    place = low + lax.broadcasted_iota(jnp.int32, (rows, 1), 0)
    dp, ctx = here()
    each = width // 128
    core = (ctx & 1) ^ (place // (64 * each))
    first, second = place // (16 * each) % 4, place // (4 * each) % 4
    y = ((dp & 3) + jnp.where(core == 0, first, second)) & 3
    x = ((ctx >> 2) + jnp.where(core == 0, second, first)) & 3
    z = ((ctx & 2) + (dp >> 2) + place // each % 4) & 3
    block = ((z & 1) * 4 + y) * 16 + x * 4 + (z >> 1) * 2 + core
    chosen = block * each + place % each == lax.broadcasted_iota(jnp.int32, (rows, width), 1)
    chosen = jnp.where(chosen, 1.0, 0.0).astype(jnp.bfloat16)
    here_rows = pl.ds(pl.multiple_of(low, 64), rows)
    out[here_rows, :] = jnp.dot(chosen, mixed[...], preferred_element_type=jnp.float32).astype(jnp.bfloat16)


def norm_kernel(s0, s1, s3, s2, emb_out, rinv_out, target_out):
    docs = s0.shape[0] // 3
    dp, _ = here()
    own, other = s0[0:docs] + s2[0:docs], s1[0:docs] + s3[0:docs]
    second = dp >= 4
    pooled = jnp.concatenate([jnp.where(second, other, own), jnp.where(second, own, other)], axis=0)
    rinv = lax.rsqrt(jnp.sum(pooled * pooled, axis=1, keepdims=True) + 1e-06)
    emb_out[...] = pooled * rinv
    rinv_out[...] = jnp.broadcast_to(rinv, rinv_out.shape)
    target_out[...] = (s0[docs:] + s2[docs:]) + (s1[docs:] + s3[docs:])


def as_row(column):
    size = column.shape[0]
    same = lax.broadcasted_iota(jnp.int32, (size, size), 0) == lax.broadcasted_iota(jnp.int32, (size, size), 1)
    return jnp.sum(jnp.where(same, column, 0.0), axis=0, keepdims=True)


def score_kernel(docs, positive, *refs):
    embs, tables, (everyone, state, expos) = refs[:4], refs[4:12], refs[12:]
    all_docs, width = everyone.shape
    dp, _ = here()
    y = dp & 3
    group = embs[0].shape[0]
    for k, piece in zip(ORDER, embs):
        everyone[pl.ds(pl.multiple_of(((y + k) & 3) * group, group), group), :] = piece[...]
    rows = tables[0].shape[0]
    emb = thirds(everyone[...])
    scores = [folded(lax.dot_general(emb, t[...], NT, preferred_element_type=jnp.float32)) / TAU for t in tables]
    top = functools.reduce(jnp.maximum, [jnp.max(s, axis=1, keepdims=True) for s in scores])
    row = lax.broadcasted_iota(jnp.int32, (all_docs, rows), 0)
    wanted = jnp.zeros((all_docs, rows), jnp.int32)
    for doc in range(all_docs):
        z, rest = divmod(doc, all_docs // 2)
        wanted = jnp.where(row == rest // docs * group + z * docs + rest % docs, positive[doc], wanted)
    totals, found = [], jnp.zeros((all_docs, 1), jnp.float32)
    for k, s in enumerate(scores):
        expo = jnp.exp(s - top)
        expos[:, k * rows : (k + 1) * rows] = expo
        totals.append(jnp.sum(expo, axis=1, keepdims=True))
        hit = row_ids(ORDER[k % 4] + k // 4 * 4, (all_docs, rows), 1) == wanted
        found = found + jnp.sum(jnp.where(hit, s, 0.0), axis=1, keepdims=True)
    totals = [totals[k] + totals[k + 4] for k in range(4)]
    total = (totals[0] + totals[3]) + (totals[1] + totals[2])
    mine = thirds(expos[pl.ds(pl.multiple_of(y * group, group), group), :])
    mix = jnp.zeros((group, width), jnp.float32)
    for k, t in enumerate(tables):
        mix = mix + folded(jnp.dot(mine[:, k * rows : (k + 1) * rows], t[...], preferred_element_type=jnp.float32))
    column = lax.broadcasted_iota(jnp.int32, (group, all_docs), 1)
    own = column == lax.broadcasted_iota(jnp.int32, (group, all_docs), 0) + y * group
    total_row, top_row, found_row = as_row(total), as_row(top), as_row(found)
    state[...] = jnp.zeros_like(state)
    state[0:group, 0:width] = mix
    for place, values in ((width, total_row), (width + 128, top_row)):
        value = jnp.sum(jnp.where(own, values, 0.0), axis=1, keepdims=True)
        state[0:group, place : place + 128] = jnp.broadcast_to(value, (group, 128))
    for index, values in enumerate((total_row, top_row, found_row)):
        state[group + index : group + index + 1, 0:all_docs] = values


def merge(docs, width, states):
    row = lax.broadcasted_iota(jnp.int32, states[0].shape, 0)
    column = lax.broadcasted_iota(jnp.int32, states[0].shape, 1)
    place = width + 128
    by_row = [s[:, place : place + 1] for s in states]
    by_lane = [s[docs + 1 : docs + 2, :] for s in states]
    top_row = functools.reduce(jnp.maximum, by_row)
    top_lane = functools.reduce(jnp.maximum, by_lane)
    terms = [
        s * jnp.exp(jnp.where(row == docs, b - top_lane, a - top_row)) for s, a, b in zip(states, by_row, by_lane)
    ]
    if len(terms) == 4:
        terms = [terms[0] + terms[3], terms[1] + terms[2]]
    joined = jnp.where((row < docs) & (column >= place), top_row, terms[0] + terms[1])
    return jnp.where(row == docs + 1, top_lane, joined)


def batch_kernel(emb, everyone, product_out, stats):
    everything = everyone[...]
    all_docs = everything.shape[0]
    own = lax.dot_general(emb[...], everything, NT, precision=HIGHEST, preferred_element_type=jnp.float32) / TAU
    product = lax.dot_general(everything, everything, NT, precision=HIGHEST, preferred_element_type=jnp.float32) / TAU
    wide = (all_docs, all_docs)
    same = lax.broadcasted_iota(jnp.int32, wide, 0) == lax.broadcasted_iota(jnp.int32, wide, 1)
    product = jnp.where(same, -1e30, product)
    top = jnp.max(product, axis=0, keepdims=True)
    total = jnp.sum(jnp.exp(product - top), axis=0, keepdims=True)
    product_out[...] = own
    stats[...] = jnp.concatenate([top, total] * 4, axis=0)


def grad_kernel(
    lengths, s0, s1, s2, s3, emb, rinv, everyone, target, product, stats, gain, normed, rstd, turned,
    send_out, d_summed, loss_out,
):
    docs, tb, width = normed.shape
    all_docs, group = everyone.shape[0], emb.shape[0]
    dp, _ = here()
    mine = lambda a: jnp.where(dp >= 4, a[docs:group], a[0:docs])
    own, others = mine(emb), everyone[...]
    now = merge(group, width, [s[...] for s in (s0, s1, s2, s3)])
    total, top, found = (now[group + k : group + k + 1, 0:all_docs] for k in range(3))
    batch_top, batch_total = stats[0:1], stats[1:2]
    peak = jnp.maximum(top, batch_top)
    lse_row = peak + jnp.log(total * jnp.exp(top - peak) + batch_total * jnp.exp(batch_top - peak))
    loss_out[...] = jnp.broadcast_to(jnp.sum(lse_row - found, axis=1, keepdims=True) / all_docs, loss_out.shape)
    column = lax.broadcasted_iota(jnp.int32, (docs, all_docs), 1)
    first = (dp & 3) * group + (dp >> 2) * docs
    same = column == lax.broadcasted_iota(jnp.int32, (docs, all_docs), 0) + first
    lse = jnp.sum(jnp.where(same, lse_row, 0.0), axis=1, keepdims=True)
    scores = mine(product)
    g_batch = jnp.where(same, 0.0, jnp.exp(scores - lse) + jnp.exp(scores - lse_row)) / all_docs
    shares = mine(now)
    mix = shares[:, 0:width] * jnp.exp(shares[:, width + 128 : width + 129] - lse)
    from_batch = jnp.dot(g_batch, others, precision=HIGHEST, preferred_element_type=jnp.float32)
    d_emb = ((mix - mine(target)) / all_docs + from_batch) / TAU
    d_pooled = (d_emb - own * jnp.sum(own * d_emb, axis=1, keepdims=True)) * mine(rinv)[:, 0:1]
    for doc in range(docs):
        dy = d_pooled[doc : doc + 1] / lengths[doc].astype(jnp.float32) * gain[...].reshape(1, width)
        level = dy - jnp.mean(dy, axis=1, keepdims=True)
        unit = normed[doc].astype(jnp.float32)
        along = jnp.mean(unit * dy, axis=1, keepdims=True)
        keep = lax.axis_index("ctx") * tb + lax.broadcasted_iota(jnp.int32, (tb, 1), 0) < lengths[doc]
        scale = jnp.where(keep, rstd[doc, :, 0:1], 0.0)
        d_summed[doc * tb : (doc + 1) * tb, :] = (scale * (level - unit * along)).astype(jnp.bfloat16)
    product_rows(turned, width // 2, d_summed, send_out)


def product_rows(turned, low, d_summed, out):
    rows = 192

    def some(index, _):
        source = pl.ds(pl.multiple_of(low + index * rows, 64), rows)
        here_rows = pl.ds(pl.multiple_of(index * rows, 64), rows)
        product = jnp.dot(turned[source, :], d_summed[...], preferred_element_type=jnp.float32)
        out[here_rows, :] = product.astype(out.dtype)

    lax.fori_loop(0, out.shape[0] // rows, some, None)


def keep_kernel(turned, d_summed, out):
    product_rows(turned, 0, d_summed, out)


def sum_kernel(count, *refs):
    terms, outs = refs[:count], refs[count:]
    total = terms[0][...].astype(jnp.float32)
    for term in terms[1:]:
        total = total + term[...].astype(jnp.float32)
    rows = outs[0].shape[0]
    for index, out in enumerate(outs):
        out[...] = total[index * rows : (index + 1) * rows].astype(out.dtype)


def sum_and_split(terms, kind):
    rows, width = terms[0].shape
    piece = (rows // 4, width)
    shapes = (f32(*piece),) + (jax.ShapeDtypeStruct(piece, kind),) * 3
    return call(
        functools.partial(sum_kernel, len(terms)), shapes, [VMEM] * len(terms), (VMEM,) * 4, limit=8, name="sum_split"
    )(*terms)


def shards(tokens, w_qkv, w_out, ln_gain, cache, positive, lengths):
    docs, tb, width = tokens.shape
    n_ctx, n_dp = lax.axis_size("ctx"), lax.axis_size("dp")
    all_docs = n_dp * docs
    ring = [(i, (i + 2 * (i % 2) - 1) % n_ctx) for i in range(n_ctx)]
    fetch = lambda part: lax.ppermute(part, "ctx", ring)
    early, middle, late = fetch(tokens[0:1]), fetch(tokens[1:3]), tokens[3:]
    near = swap(tokens, "ctx", 1)
    tables = around(cache, from_y)
    qk, v_turned, w_v_turned = prepare(in_hbm(tokens), in_hbm(w_qkv))
    near_k, near_v = call(
        near_kernel,
        (bf16(docs, tb, width), bf16(width, docs * tb)),
        [VMEM] * 3,
        (VMEM,) * 2,
        flops=4 * docs * tb * width * width,
        moved=4 * 2**20,
        name="near",
    )(near, w_qkv, w_v_turned)
    gain = ln_gain
    fixed = (lengths, tokens, near_k), (near_v, qk, v_turned, w_qkv, w_v_turned, w_out, gain)
    *done, pool = attend(0, None, *fixed[0], early, *fixed[1])
    pool, after, *tables = lax.optimization_barrier((pool, positive, *tables))
    others = [swap(table, "ctx", 1) for table in tables]
    target = call(
        functools.partial(target_kernel, docs), f32(2 * docs, width), [SMEM] + [VMEM] * 4, VMEM, name="target"
    )(after, *tables)
    middle, late, target, *others = lax.optimization_barrier((middle, late, target, *others))
    late = fetch(late)
    done = attend(1, [*done, pool], *fixed[0], middle, *fixed[1])
    done = attend(3, done, *fixed[0], late, *fixed[1])
    hidden, mixed, normed, rstd, pool = done

    turned = call(
        turn_kernel,
        bf16(width, docs * tb),
        [VMEM],
        VMEM,
        flops=2 * docs * tb * width * width,
        moved=4 * 2**20,
        name="turn",
    )(mixed)

    group = 2 * docs
    sums = call(stack_kernel, f32(docs + group, width), [VMEM, VMEM], VMEM, limit=4, name="stack")(
        pool, target
    )
    sums = add([sums, swap(sums, "ctx", 1)])
    sums = add(around(sums, from_x))
    emb, rinv, target = call(
        norm_kernel,
        (f32(group, width), f32(group, 128), f32(group, width)),
        [VMEM] * 4,
        (VMEM,) * 3,
        limit=4,
        name="norm",
    )(*around(sums, from_z))
    embs = around(emb, from_y)
    everyone, state = call(
        functools.partial(score_kernel, docs),
        (f32(all_docs, width), f32(2 * group, width + 256)),
        [SMEM] + [VMEM] * 12,
        (VMEM, VMEM),
        moved=2 * 2**20,
        scratch_shapes=[pltpu.VMEM((all_docs, 8 * cache.shape[0]), jnp.float32)],
        name="score",
    )(positive, *embs, *tables, *others)
    product, stats = call(
        batch_kernel,
        (f32(group, all_docs), f32(8, all_docs)),
        [VMEM, VMEM],
        (VMEM, VMEM),
        limit=4,
        name="batch",
    )(emb, everyone)
    state = merged(group, width, around(state, from_x))
    half = width // 2
    send, d_summed, loss = call(
        grad_kernel,
        (bf16(half, width), bf16(docs * tb, width), f32(8, 128)),
        [SMEM] + [VMEM] * 14,
        (VMEM,) * 3,
        flops=docs * tb * width * width,
        moved=8 * 2**20,
        name="grad",
    )(
        lengths, *around(state, from_z), emb, rinv, everyone, target, product, stats, gain, normed, rstd, turned,
    )
    keep = call(
        keep_kernel,
        f32(half, width),
        [VMEM, VMEM],
        VMEM,
        flops=docs * tb * width * width,
        moved=2**20,
        name="keep",
    )(turned, d_summed)
    keep, *sends = sum_and_split([keep, swap(send, "ctx", 1)], jnp.bfloat16)
    got = dealt(sends, lambda piece, k: from_plane(piece, k, False))
    keep, *sends = sum_and_split([keep] + got, jnp.float32)
    got = dealt(sends, lambda piece, k: from_plane(piece, k, True))
    keep, *sends = sum_and_split([keep] + got, jnp.float32)
    got = dealt(sends, from_z)
    return (hidden, loss[0, 0], add([keep] + got))


def solution(mesh):
    placed = (P("dp", "ctx", None), P(), P(), P(), P(("dp", "ctx"), None), P(), P("dp"))
    return jax.shard_map(
        shards,
        mesh=mesh,
        in_specs=placed,
        out_specs=(P("dp", "ctx", None), P(), P(("dp", "ctx"), None)),
        check_vma=False,
    )
```
